32 devices in a mesh: group: 2 (over y), tensor: 4 (over z), example: 4 (over x, core).
Axes of the slice: x: 2, y: 2, z: 4, core: 2. Of those that a mesh axis runs over, the one named last changes fastest.
Arguments:
- layer_input: bfloat16 [32, 128, 8192], P(('group', 'example'), None, 'tensor'), parts along dimension 0, may hold values from -6 to 6
- gate_pre: bfloat16 [32, 128, 28672], P(('group', 'example'), None, 'tensor'), parts along dimension 0, may hold values from -7 to 7
- up_pre: bfloat16 [32, 128, 28672], P(('group', 'example'), None, 'tensor'), parts along dimension 0, may hold values from -6 to 6
- output_grad: bfloat16 [32, 128, 8192], P(('group', 'example'), None, 'tensor'), parts along dimension 0, may hold values from -6 to 6
- down_weight: bfloat16 [28672, 8192], P('tensor', 'example'), may hold values from -0.03125 to 0.03125
- proj_input: bfloat16 [64, 8192], P(None, 'tensor'), may hold values from -0.0625 to 0.0625
- proj_hidden: bfloat16 [64, 28672], P(None, 'tensor'), may hold values from -0.03125 to 0.03125
- proj_output: bfloat16 [64, 8192], P(None, 'tensor'), may hold values from -0.0625 to 0.0625
- proj_gate: bfloat16 [64, 28672], P(None, 'tensor'), may hold values from -0.03125 to 0.03125
- proj_up: bfloat16 [64, 28672], P(None, 'tensor'), may hold values from -0.03125 to 0.03125
- query_sketches: bfloat16 [2048, 12288], P(('group', 'example'), 'tensor'), parts along dimension 0, may hold values from -6 to 6
- rev_lengths: int32 [32], P(('group', 'example')), parts along dimension 0, may hold values from 1 to 128, 1280 in all
- rev_slot: int32 [32], P('group'), parts along dimension 0, may hold values from 0 to 15, each once
- query_slot: int32 [2048], P(('group', 'example')), parts along dimension 0, may hold values from 0 to 1023, each once
Outputs:
- scores: float32 [16, 512], P('group', 'example'), parts along dimension 0
The draws below stay inside these ranges and needn't reach their ends.
There are 2 independent parts, one for each index of `group`. The reference program is written for one: setup_inputs(seed, part) draws one part's arguments, and reference() takes and returns one part's arrays. A program takes and returns all parts, laid end to end along the dimension named above; an argument that names none is the same for every part. Nothing has to cross between parts.
Inputs may be any that keep to these rules, and one draw needn't show every extreme that they name: `rev_lengths`: some revision example has length exactly 128. `rev_slot`: A permutation of the revision examples' slots. `query_slot`: A permutation of the query examples' slots.
All inputs are finite; a program needn't handle non-finite values. No bound on the sum of `rev_lengths` on one device may be relied on, other than what follows from the above.
Results may differ from the reference program's by a relative error of at most 0.0035.
Values may be sent and summed in bfloat16 or wider, within the bound.
No kernel may reach another device: no remote copies, remote signals or barrier semaphores. Data moves between devices by JAX's collectives and lax.ppermute only.
A program may use at most 384 MiB of HBM per device.

```python
import math
import jax
import jax.numpy as jnp
import numpy as np
from jax import lax

D = 8192
FF = 28672
RANK = 64
SLOT = 128
REX = 16
RPAIRS = 8
QEX = 1024
QPAIRS = 512
FEAT = 12288


def block_levels(own_key, extent, split, low, top_value):
    gain = 1.0
    for axis_at, parts in split:
        heights = jax.random.uniform(jax.random.fold_in(jax.random.fold_in(own_key, 6), axis_at), (parts,), jnp.float32, low / len(split), top_value / len(split))
        gain = gain * jnp.repeat(jnp.exp(heights), extent[axis_at] // parts).reshape((-1,) + (1,) * (len(extent) - 1 - axis_at))
    return gain


def length_profile(number_of, total, reach, skew):
    portions = [(1 << 20) // math.isqrt(standing ** skew) + 1 for standing in range(2, number_of + 1)]
    spare, given = total - reach - (number_of - 1), [1] * (number_of - 1)
    while spare > 0:
        free = [i for i in range(number_of - 1) if given[i] < reach]
        pool, budget = sum([portions[i] for i in free]), spare
        for i in free:
            addition = min(reach - given[i], max(1, budget * portions[i] // pool), spare)
            given[i] = given[i] + addition
            spare = spare - addition
    return np.array([reach] + given)


def uneven_parts(rng, amount, total, most, lean):
    if amount == 2:
        one = jax.random.randint(rng, (), max(1, total - most), min(most, total - 1) + 1)
        return jnp.stack([one, total - one])
    tallies = jnp.asarray(length_profile(amount, total, most, lean), jnp.int32)
    twos = (amount - 1) // 2
    source_of, sink = tallies[1:1 + 2 * twos:2], tallies[2:2 + 2 * twos:2]
    margin = jnp.minimum(source_of - 1, most - sink)
    shifted = jax.random.randint(jax.random.fold_in(rng, 1), (twos,), 0, 1 << 20) % (margin + 1)
    tallies = tallies.at[1:1 + 2 * twos:2].set(source_of - shifted).at[2:2 + 2 * twos:2].set(sink + shifted)
    return tallies[jax.random.permutation(jax.random.fold_in(rng, 2), amount)]


def bell_draw(stream_key, shape, scale, limit, cuts=(), kind=jnp.bfloat16):
    drawn = jax.random.normal(stream_key, shape, jnp.float32) * scale
    if len(cuts) > 0:
        drawn = block_levels(stream_key, shape, cuts, -0.22, 0.18) * drawn
    return jnp.clip(drawn, min=-limit, max=limit).astype(kind)


def setup_inputs(seed: int = 0, part: int = 0) -> dict:
    streams_of = jax.random.split(jax.random.key(seed), 15)
    part_splits = jax.random.split(jax.random.fold_in(streams_of[14], part), 15)
    return {
        "layer_input": bell_draw(part_splits[0], (REX, SLOT, D), 1.0, 6.0, ((0, 4), (2, 4))),
        "gate_pre": bell_draw(part_splits[1], (REX, SLOT, FF), 1.5, 7.0, ((0, 4), (2, 4))),
        "up_pre": bell_draw(part_splits[2], (REX, SLOT, FF), 1.0, 6.0, ((0, 4), (2, 4))),
        "output_grad": bell_draw(part_splits[3], (REX, SLOT, D), 1.0, 6.0, ((0, 4), (2, 4))),
        "down_weight": bell_draw(streams_of[4], (FF, D), FF ** -0.5, 0.03125, ((0, 4), (1, 4))),
        "proj_input": bell_draw(streams_of[5], (RANK, D), D ** -0.5, 0.0625, ((1, 4),)),
        "proj_hidden": bell_draw(streams_of[6], (RANK, FF), FF ** -0.5, 0.03125, ((1, 4),)),
        "proj_output": bell_draw(streams_of[7], (RANK, D), D ** -0.5, 0.0625, ((1, 4),)),
        "proj_gate": bell_draw(streams_of[8], (RANK, FF), FF ** -0.5, 0.03125, ((1, 4),)),
        "proj_up": bell_draw(streams_of[9], (RANK, FF), FF ** -0.5, 0.03125, ((1, 4),)),
        "query_sketches": bell_draw(part_splits[10], (QEX, FEAT), 1.0, 6.0, ((0, 4), (1, 4))),
        "rev_lengths": uneven_parts(part_splits[11], REX, REX * SLOT * 5 // 8, SLOT, 1).astype(jnp.int32),
        "rev_slot": jax.random.permutation(part_splits[12], REX).astype(jnp.int32),
        "query_slot": jax.random.permutation(part_splits[13], QEX).astype(jnp.int32),
    }


def pairing_table(slots, pairs):
    pair_index = slots // 2
    signs = (1 - 2 * (slots % 2)).astype(jnp.float32)
    targets = jnp.arange(pairs, dtype=jnp.int32)
    return jnp.where(targets[:, None] == pair_index[None, :], signs[None, :], jnp.float32(0.0))


def reference(layer_input, gate_pre, up_pre, output_grad, down_weight, proj_input, proj_hidden, proj_output, proj_gate, proj_up, query_sketches, rev_lengths, rev_slot, query_slot):
    row_total = REX * SLOT
    inputs_rows = layer_input.reshape(row_total, D)
    grad_rows = output_grad.reshape(row_total, D)
    gate_values = gate_pre.reshape(row_total, FF).astype(jnp.float32)
    up_values = up_pre.reshape(row_total, FF).astype(jnp.float32)
    sigma = jax.nn.sigmoid(gate_values)
    active = gate_values * sigma
    hidden = (active * up_values).astype(jnp.bfloat16)
    hidden_grad = lax.dot_general(grad_rows, down_weight, (((1,), (1,)), ((), ())), preferred_element_type=jnp.float32).astype(jnp.bfloat16)
    hidden_grad = lax.optimization_barrier(hidden_grad).astype(jnp.float32)
    grad_up = (hidden_grad * active).astype(jnp.bfloat16)
    grad_gate = (hidden_grad * up_values * sigma * (1.0 + gate_values * (1.0 - sigma))).astype(jnp.bfloat16)

    def project(rows_data, projection):
        return lax.dot_general(rows_data, projection, (((1,), (1,)), ((), ())), preferred_element_type=jnp.float32)

    in_gate = project(inputs_rows, proj_input)
    in_down = project(hidden, proj_hidden)
    out_gate = project(grad_gate, proj_gate)
    out_up = project(grad_up, proj_up)
    out_down = project(grad_rows, proj_output)
    positions = jnp.arange(SLOT, dtype=jnp.int32)
    mask = (positions[None, :] < rev_lengths[:, None]).astype(jnp.float32).reshape(row_total)
    left = jnp.stack([in_gate, in_gate, in_down]) * mask[None, :, None]
    right = jnp.stack([out_gate, out_up, out_down])
    left = left.reshape(3, REX, SLOT, RANK)
    right = right.reshape(3, REX, SLOT, RANK)
    sketch = jnp.einsum('meti,metj->eimj', left, right, precision=lax.Precision.HIGHEST).reshape(REX, FEAT)
    revision_pairs = jnp.dot(pairing_table(rev_slot, RPAIRS), sketch, precision=lax.Precision.HIGHEST)
    example_scores = lax.dot_general(revision_pairs, query_sketches.astype(jnp.float32), (((1,), (1,)), ((), ())), precision=lax.Precision.HIGHEST)
    query_pairing = pairing_table(query_slot, QPAIRS)
    summed = lax.dot_general(example_scores, query_pairing, (((1,), (1,)), ((), ())), precision=lax.Precision.HIGHEST)
    return summed / jnp.float32(RANK * RANK)
```

```python
import functools

import jax
import jax.numpy as jnp
from jax import lax
from jax.sharding import PartitionSpec as P

CHUNKS = 2
LEVELS = (704, 768, 896)


def contract(left_side, right_side):
    return lax.dot_general(
        left_side, right_side, (((1,), (1,)), ((), ())), preferred_element_type=jnp.float32
    )


def contract_exact(left_side, right_side):
    return lax.dot_general(
        left_side,
        right_side,
        (((1,), (1,)), ((), ())),
        precision=lax.Precision.HIGHEST,
        preferred_element_type=jnp.float32,
    )


def pairing_table(slots, pairs):
    pair_index = slots // 2
    signs = (1 - 2 * (slots % 2)).astype(jnp.float32)
    targets = jnp.arange(pairs, dtype=jnp.int32)
    return jnp.where(targets[:, None] == pair_index[None, :], signs[None, :], jnp.float32(0.0))


def take(array, start, size, axis):
    return lax.dynamic_slice_in_dim(array, start, size, axis)


def swap_near(array):
    count = lax.axis_size("example")
    return lax.ppermute(array, "example", [(i, i ^ 1) for i in range(count)])


def swap_far(array):
    count = lax.axis_size("example")
    return lax.ppermute(array, "example", [(i, i ^ 2) for i in range(count)])


def packed_scores(capacity, args):
    (
        layer_input,
        gate_pre,
        up_pre,
        grad_rows,
        grad_near,
        down_weight,
        proj_input,
        proj_hidden,
        proj_output,
        proj_gate,
        proj_up,
        rev_slot,
        lengths,
    ) = args
    ex_count, slot_len, width_local = layer_input.shape
    hidden_local = gate_pre.shape[2]
    row_total = ex_count * slot_len
    rank_size = proj_input.shape[0]
    tensor_size = lax.axis_size("tensor")
    per_rank = rank_size // tensor_size
    rev_pairs = rev_slot.shape[0] // 2
    example_at = lax.axis_index("example")
    near = example_at % 2
    far_half = example_at // 2
    half_hidden = hidden_local // 2
    half_rows = capacity // 2
    step_rows = half_rows // CHUNKS
    width_block = down_weight.shape[1]

    chip_lengths = take(lengths, far_half * 2 * ex_count, 2 * ex_count, 0)
    offsets = jnp.cumsum(chip_lengths) - chip_lengths
    positions = jnp.arange(slot_len, dtype=jnp.int32)
    place = (offsets[:, None] + positions[None, :] + (capacity - near * half_rows)) % capacity
    which, at = place // half_rows, place % half_rows
    place = (at // step_rows) * (2 * step_rows) + which * step_rows + at % step_rows
    place = jnp.where(positions[None, :] < chip_lengths[:, None], place, -1)

    def own_first(array):
        return jnp.concatenate(
            [take(array, near * ex_count, ex_count, 0), take(array, (1 - near) * ex_count, ex_count, 0)]
        )

    place = own_first(place).reshape(2 * row_total)
    slots_here = own_first(take(rev_slot, far_half * 2 * ex_count, 2 * ex_count, 0))
    select = jnp.arange(capacity, dtype=jnp.int32)[:, None] == place[None, :]
    select = select.astype(jnp.bfloat16)

    def pack(rows):
        return jnp.dot(select, rows, preferred_element_type=jnp.float32).astype(jnp.bfloat16)

    grad_both = jnp.concatenate([grad_rows, grad_near])
    columns = [
        (2 * far_half + near) * width_block,
        (2 * far_half + 1 - near) * width_block,
        (2 * (1 - far_half) + near) * width_block,
        (2 * (1 - far_half) + 1 - near) * width_block,
    ]
    gathered = []
    for step in range(CHUNKS):
        own_select = select[step * 2 * step_rows : step * 2 * step_rows + step_rows]
        block = jnp.dot(own_select, grad_both, preferred_element_type=jnp.float32).astype(jnp.bfloat16)
        gathered.append(lax.all_gather(block, "tensor", axis=1, tiled=True))

    weight_keep = take(down_weight, near * half_hidden, half_hidden, 0)
    weight_near = swap_near(take(down_weight, (1 - near) * half_hidden, half_hidden, 0))

    def split_hidden(array):
        rows = array.reshape(row_total, hidden_local)
        keep = take(rows, near * half_hidden, half_hidden, 1)
        return pack(jnp.concatenate([keep, swap_near(take(rows, (1 - near) * half_hidden, half_hidden, 1))]))

    gate_packed = split_hidden(gate_pre)
    up_packed = split_hidden(up_pre)
    proj_gate_here = take(proj_gate, near * half_hidden, half_hidden, 1)
    proj_up_here = take(proj_up, near * half_hidden, half_hidden, 1)

    inputs_rows = layer_input.reshape(row_total, width_local)
    gate_values = gate_pre.reshape(row_total, hidden_local).astype(jnp.float32)
    up_values = up_pre.reshape(row_total, hidden_local).astype(jnp.float32)
    hidden = (gate_values * jax.nn.sigmoid(gate_values) * up_values).astype(jnp.bfloat16)
    early = jnp.stack(
        [
            contract(inputs_rows, proj_input),
            contract(hidden, proj_hidden),
            contract(grad_rows, proj_output),
        ]
    )
    in_gate, in_down, out_down = lax.psum(early, "tensor")
    table = pairing_table(slots_here, rev_pairs)
    own_lengths = take(lengths, example_at * ex_count, ex_count, 0)
    mask = (positions[None, :] < own_lengths[:, None]).astype(jnp.float32).reshape(row_total)
    left_down = take(in_down, lax.axis_index("tensor") * per_rank, per_rank, 1) * mask[:, None]
    sketch_down = jnp.einsum(
        "pe,eti,etj->pij",
        table[:, :ex_count],
        left_down.reshape(ex_count, slot_len, per_rank),
        out_down.reshape(ex_count, slot_len, rank_size),
        precision=lax.Precision.HIGHEST,
    )
    in_gate = jnp.concatenate([in_gate, swap_near(in_gate)])
    select_exact = select.astype(jnp.float32)
    in_gate = jnp.dot(select_exact, in_gate, precision=lax.Precision.HIGHEST)
    table_rows = jnp.dot(select, jnp.repeat(table, slot_len, axis=1).T.astype(jnp.bfloat16))
    left = table_rows.astype(jnp.float32)[:, :, None] * in_gate[:, None, :]
    left = left.reshape(capacity, rev_pairs * rank_size)

    own_blocks, far_blocks, sent = [], [], []
    for step in range(CHUNKS):
        mine, mine_near, away, away_near = [take(gathered[step], c, width_block, 1) for c in columns]
        came = swap_far(jnp.stack([away, away_near]))
        there = swap_near(jnp.stack([came[1], came[0]]))
        far_blocks.append((jnp.concatenate([came[0], there[0]]), jnp.concatenate([came[1], there[1]])))
        here = swap_near(jnp.stack([mine_near, mine]))
        own_blocks.append((jnp.concatenate([mine, here[0]]), jnp.concatenate([mine_near, here[1]])))
    for step in range(CHUNKS):
        first, second = far_blocks[step]
        partial = contract(first, weight_keep) + contract(second, weight_near)
        sent.append(swap_far(partial.astype(jnp.bfloat16)))
    right = []
    for step in range(CHUNKS):
        rows = slice(step * 2 * step_rows, (step + 1) * 2 * step_rows)
        first, second = own_blocks[step]
        partial = contract(first, weight_keep) + contract(second, weight_near)
        hidden_grad = (partial + sent[step].astype(jnp.float32)).astype(jnp.bfloat16)
        hidden_grad = lax.optimization_barrier(hidden_grad).astype(jnp.float32)
        gate_values = gate_packed[rows].astype(jnp.float32)
        up_values = up_packed[rows].astype(jnp.float32)
        sigma = jax.nn.sigmoid(gate_values)
        grad_up = (hidden_grad * (gate_values * sigma)).astype(jnp.bfloat16)
        grad_gate = (hidden_grad * up_values * sigma * (1.0 + gate_values * (1.0 - sigma))).astype(
            jnp.bfloat16
        )
        right.append(
            jnp.concatenate([contract(grad_gate, proj_gate_here), contract(grad_up, proj_up_here)], axis=1)
        )
    right = jnp.concatenate(right)
    sketch_late = lax.dot_general(
        left, right, (((0,), (0,)), ((), ())), precision=lax.Precision.HIGHEST
    ).reshape(rev_pairs, tensor_size, per_rank, 2 * rank_size)
    sketch_late = lax.all_to_all(sketch_late, "tensor", 1, 0, tiled=False).sum(0)
    sketch_late = sketch_late.reshape(rev_pairs, per_rank, 2, rank_size)
    return jnp.concatenate([sketch_late, sketch_down[:, :, None, :]], axis=2)


def local(
    layer_input,
    gate_pre,
    up_pre,
    output_grad,
    down_weight,
    proj_input,
    proj_hidden,
    proj_output,
    proj_gate,
    proj_up,
    query_sketches,
    rev_lengths,
    rev_slot,
    query_slot,
):
    ex_count, slot_len, width_local = layer_input.shape
    row_total = ex_count * slot_len
    rank_size = proj_input.shape[0]
    example_size = lax.axis_size("example")
    grad_rows = output_grad.reshape(row_total, width_local)
    grad_near = swap_near(grad_rows)
    every_length = lax.all_gather(rev_lengths, ("group", "example"), axis=0, tiled=True)
    halves = every_length.reshape(-1, 2 * ex_count).sum(1)
    lengths = take(every_length, lax.axis_index("group") * rev_slot.shape[0], rev_slot.shape[0], 0)
    full = 2 * row_total
    levels = [level for level in LEVELS if level < full] + [full]
    branch = jnp.sum((jnp.max(halves) > jnp.array(levels[:-1], jnp.int32)).astype(jnp.int32))
    sketches = lax.switch(
        branch,
        [functools.partial(packed_scores, level) for level in levels],
        (
            layer_input,
            gate_pre,
            up_pre,
            grad_rows,
            grad_near,
            down_weight,
            proj_input,
            proj_hidden,
            proj_output,
            proj_gate,
            proj_up,
            rev_slot,
            lengths,
        ),
    )
    rev_pairs = rev_slot.shape[0] // 2
    revision_pairs = lax.all_gather(sketches.reshape(rev_pairs, -1), "example", axis=0).sum(0)
    example_scores = contract_exact(revision_pairs, query_sketches.astype(jnp.float32))
    query_pairs = query_slot.shape[0] * example_size // 2
    pair_terms = contract_exact(example_scores, pairing_table(query_slot, query_pairs))
    every_term = lax.all_gather(pair_terms, ("tensor", "example"), axis=0)
    owned = query_pairs // example_size
    total = take(every_term, lax.axis_index("example") * owned, owned, 2).sum(0)
    return total / jnp.float32(rank_size * rank_size)


def solution(mesh):
    return jax.shard_map(
        local,
        mesh=mesh,
        in_specs=(
            P(("group", "example"), None, "tensor"),
            P(("group", "example"), None, "tensor"),
            P(("group", "example"), None, "tensor"),
            P(("group", "example"), None, "tensor"),
            P("tensor", "example"),
            P(None, "tensor"),
            P(None, "tensor"),
            P(None, "tensor"),
            P(None, "tensor"),
            P(None, "tensor"),
            P(("group", "example"), "tensor"),
            P(("group", "example")),
            P("group"),
            P(("group", "example")),
        ),
        out_specs=P("group", "example"),
        check_vma=False,
    )
```

```python
import functools

import jax
import jax.numpy as jnp
from jax import lax
from jax.experimental import pallas as pl
from jax.experimental.pallas import tpu as pltpu
from jax.sharding import PartitionSpec as P

CHUNKS = 4
LEVELS = (672, 704, 736, 768, 832)
TILE = 512
VMEM_LIMIT = 48 * 1024 * 1024


def contract(left_side, right_side):
    return lax.dot_general(
        left_side, right_side, (((1,), (1,)), ((), ())), preferred_element_type=jnp.float32
    )


def contract_exact(left_side, right_side):
    return lax.dot_general(
        left_side,
        right_side,
        (((1,), (1,)), ((), ())),
        precision=lax.Precision.HIGHEST,
        preferred_element_type=jnp.float32,
    )


def pairing_table(slots, pairs):
    pair_index = slots // 2
    signs = (1 - 2 * (slots % 2)).astype(jnp.float32)
    targets = jnp.arange(pairs, dtype=jnp.int32)
    return jnp.where(targets[:, None] == pair_index[None, :], signs[None, :], jnp.float32(0.0))


def take(array, start, size, axis):
    return lax.dynamic_slice_in_dim(array, start, size, axis)


def swap(array, axis, bits):
    count = lax.axis_size(axis)
    return lax.ppermute(array, axis, [(i, i ^ bits) for i in range(count)])


def chain_pairs(rule):
    pairs = []
    for t in range(4):
        for e in range(4):
            far, near = e // 2, e % 2
            goal = rule(3 - t if far else t, far, near)
            if goal is not None:
                order, far, near = goal
                pairs.append((t * 4 + e, (3 - order if far else order) * 4 + 2 * far + near))
    return pairs


CROSS = chain_pairs(lambda u, f, n: (3 - u, 1 - f, n) if u >= 2 else None)
UP_FIRST = chain_pairs(lambda u, f, n: (u + 1, f, n) if u in (0, 1) else None)
UP_SECOND = chain_pairs(lambda u, f, n: (u + 1, f, n) if u in (1, 2) else None)
UP_THIRD = chain_pairs(lambda u, f, n: (u + 1, f, n) if u == 2 else None)
DOWN = chain_pairs(lambda u, f, n: (0, f, n) if u == 1 else None)


def move(array, pairs):
    return lax.ppermute(array, ("tensor", "example"), pairs)


def kernel_params():
    return pltpu.CompilerParams(vmem_limit_bytes=VMEM_LIMIT)


def pack_kernel(starts, sizes, near_ref, place_ref, own_ref, other_ref, *refs):
    outs, select = refs[:-1], refs[-1]
    rows_own = own_ref.shape[0]

    @pl.when(pl.program_id(0) == 0)
    def _():
        base = 0
        for start, size in zip(starts, sizes):
            at = lax.broadcasted_iota(jnp.int32, (size, select.shape[1]), 0) + start
            select[base : base + size, :] = jnp.where(at == place_ref[...], 1.0, 0.0).astype(jnp.bfloat16)
            base += size

    base = 0
    for out, size in zip(outs, sizes):
        rows = slice(base, base + size)
        total = jnp.dot(select[rows, :rows_own], own_ref[...], preferred_element_type=jnp.float32)
        total += jnp.dot(select[rows, rows_own:], other_ref[...], preferred_element_type=jnp.float32)
        out[...] = total.astype(jnp.bfloat16)
        base += size


def pack(starts, sizes, near_offset, place, own, other):
    rows, columns = other.shape
    total = sum(sizes)
    return pl.pallas_call(
        functools.partial(pack_kernel, starts, sizes),
        grid_spec=pltpu.PrefetchScalarGridSpec(
            num_scalar_prefetch=1,
            grid=(columns // TILE,),
            in_specs=[
                pl.BlockSpec((1, 2 * rows), lambda i, near: (0, 0)),
                pl.BlockSpec((rows, TILE), lambda i, near: (0, near[0] + i)),
                pl.BlockSpec((rows, TILE), lambda i, near: (0, i)),
            ],
            out_specs=[pl.BlockSpec((size, TILE), lambda i, near: (0, i)) for size in sizes],
            scratch_shapes=[pltpu.VMEM((total, 2 * rows), jnp.bfloat16)],
        ),
        out_shape=[jax.ShapeDtypeStruct((size, columns), jnp.bfloat16) for size in sizes],
        compiler_params=kernel_params(),
        cost_estimate=pl.CostEstimate(
            flops=4 * total * rows * columns,
            bytes_accessed=(4 * rows + 2 * total) * columns,
            transcendentals=0,
        ),
        name="pack_rows",
    )(near_offset, place, own, other)


def partial_kernel(near_ref, a0, a1, b0, b1, keep_ref, other_ref, out_ref, left):
    size, width = a0.shape

    @pl.when(pl.program_id(0) == 0)
    def _():
        left[:size, :width] = a0[...]
        left[size:, :width] = a1[...]
        left[:size, width:] = b0[...]
        left[size:, width:] = b1[...]

    total = contract(left[:, :width], keep_ref[...])
    total += contract(left[:, width:], other_ref[...])
    out_ref[...] = total.astype(out_ref.dtype)


def partial_product(part, near_offset, own_k, own_k_near, near_k, near_k_near, weight, weight_near, dtype):
    size, width = own_k.shape[0] // 2, own_k.shape[1]
    hidden = weight_near.shape[0]
    rows = pl.BlockSpec((size, width), lambda i, near: (part, 0))
    return pl.pallas_call(
        partial_kernel,
        grid_spec=pltpu.PrefetchScalarGridSpec(
            num_scalar_prefetch=1,
            grid=(hidden // TILE,),
            in_specs=[rows] * 4
            + [
                pl.BlockSpec((TILE, width), lambda i, near: (near[0] + i, 0)),
                pl.BlockSpec((TILE, width), lambda i, near: (i, 0)),
            ],
            out_specs=pl.BlockSpec((2 * size, TILE), lambda i, near: (0, i)),
            scratch_shapes=[pltpu.VMEM((2 * size, 2 * width), jnp.bfloat16)],
        ),
        out_shape=jax.ShapeDtypeStruct((2 * size, hidden), dtype),
        compiler_params=kernel_params(),
        cost_estimate=pl.CostEstimate(
            flops=8 * size * width * hidden,
            bytes_accessed=4 * width * hidden + 8 * size * hidden,
            transcendentals=0,
        ),
        name="partial_product",
    )(near_offset, own_k, own_k_near, near_k, near_k_near, weight, weight_near)


def finish_kernel(near_ref, own_ref, came_ref, gate_ref, up_ref, proj_gate_ref, proj_up_ref, gate_out, up_out):
    @pl.when(pl.program_id(0) == 0)
    def _():
        gate_out[...] = jnp.zeros_like(gate_out)
        up_out[...] = jnp.zeros_like(up_out)

    hidden_grad = (own_ref[...] + came_ref[...].astype(jnp.float32)).astype(jnp.bfloat16)
    hidden_grad = hidden_grad.astype(jnp.float32)
    gate = gate_ref[...].astype(jnp.float32)
    up = up_ref[...].astype(jnp.float32)
    sigma = jax.nn.sigmoid(gate)
    grad_up = (hidden_grad * (gate * sigma)).astype(jnp.bfloat16)
    grad_gate = (hidden_grad * up * sigma * (1.0 + gate * (1.0 - sigma))).astype(jnp.bfloat16)
    gate_out[...] += contract(grad_gate, proj_gate_ref[...])
    up_out[...] += contract(grad_up, proj_up_ref[...])


def finish(near_offset, own, came, gate, up, proj_gate, proj_up):
    rows, hidden = own.shape
    rank_size = proj_gate.shape[0]
    tile = pl.BlockSpec((rows, TILE), lambda i, near: (0, i))
    proj = pl.BlockSpec((rank_size, TILE), lambda i, near: (0, near[0] + i))
    out = pl.BlockSpec((rows, rank_size), lambda i, near: (0, 0))
    return pl.pallas_call(
        finish_kernel,
        grid_spec=pltpu.PrefetchScalarGridSpec(
            num_scalar_prefetch=1,
            grid=(hidden // TILE,),
            in_specs=[tile, tile, tile, tile, proj, proj],
            out_specs=[out, out],
        ),
        out_shape=[jax.ShapeDtypeStruct((rows, rank_size), jnp.float32)] * 2,
        compiler_params=kernel_params(),
        cost_estimate=pl.CostEstimate(
            flops=4 * rows * hidden * rank_size,
            bytes_accessed=10 * rows * hidden,
            transcendentals=rows * hidden,
        ),
        name="finish_chunk",
    )(near_offset, own, came, gate, up, proj_gate, proj_up)


def sum_over(array, axis):
    parts = [swap(array, axis, bits) for bits in (1, 2, 3)]
    return (array + parts[0]) + (parts[1] + parts[2])


def scatter_over(array, axis, dim):
    at = lax.axis_index(axis)
    size = array.shape[dim] // 4
    parts = [swap(take(array, (at ^ bits) * size, size, dim), axis, bits) for bits in (1, 2, 3)]
    return (take(array, at * size, size, dim) + parts[0]) + (parts[1] + parts[2])


def packed_scores(capacity, args):
    (
        layer_input,
        gate_pre,
        up_pre,
        grad_rows,
        grad_near,
        down_weight,
        proj_input,
        proj_hidden,
        proj_output,
        proj_gate,
        proj_up,
        query_sketches,
        query_slot,
        rev_slot,
        own_lengths,
        near_lengths,
    ) = args
    ex_count, slot_len, width_local = layer_input.shape
    hidden_local = gate_pre.shape[2]
    row_total = ex_count * slot_len
    rank_size = proj_input.shape[0]
    per_rank = rank_size // 4
    rev_pairs = rev_slot.shape[0] // 2
    example_at = lax.axis_index("example")
    tensor_at = lax.axis_index("tensor")
    near, far = example_at % 2, example_at // 2
    order = jnp.where(far == 1, 3 - tensor_at, tensor_at)
    half_hidden = hidden_local // 2
    half_rows = capacity // 2
    units = half_rows // 16
    sizes = [16 * (units // CHUNKS + (k < units % CHUNKS)) for k in range(CHUNKS)]
    begins = [sum(sizes[:k]) for k in range(CHUNKS)]
    offset = (near * (half_hidden // TILE)).astype(jnp.int32).reshape(1)
    no_offset = jnp.zeros((1,), jnp.int32)

    both_lengths = jnp.concatenate([own_lengths, near_lengths])
    own_begin = near * jnp.sum(near_lengths)
    near_begin = (1 - near) * jnp.sum(own_lengths)
    offsets = jnp.concatenate(
        [
            own_begin + jnp.cumsum(own_lengths) - own_lengths,
            near_begin + jnp.cumsum(near_lengths) - near_lengths,
        ]
    )
    positions = jnp.arange(slot_len, dtype=jnp.int32)
    place = offsets[:, None] + positions[None, :] - near * half_rows
    place = jnp.where(place < 0, place + capacity, place)
    other_half = place >= half_rows
    at = jnp.where(other_half, place - half_rows, place)
    place = at + jnp.where(other_half, sizes[0], 0)
    for k in range(1, CHUNKS):
        place += jnp.where(
            at >= begins[k], sizes[k - 1] + jnp.where(other_half, sizes[k] - sizes[k - 1], 0), 0
        )
    place = jnp.where(positions[None, :] < both_lengths[:, None], place, -1).reshape(1, 2 * row_total)

    starts = [2 * b for b in begins]
    doubles = [2 * s for s in sizes]
    blocks = pack(starts, sizes, no_offset, place, grad_rows, grad_near)

    weight_near = swap(take(down_weight, (1 - near) * half_hidden, half_hidden, 0), "example", 1)

    def split_hidden(array):
        rows = array.reshape(row_total, hidden_local)
        other = swap(take(rows, (1 - near) * half_hidden, half_hidden, 1), "example", 1)
        return pack(starts, doubles, offset, place, rows, other)

    gate_packed = split_hidden(gate_pre)
    up_packed = split_hidden(up_pre)

    columns_match = near == far
    lefts = []
    for k in range(CHUNKS):
        source = jnp.concatenate([blocks[k], move(blocks[k], CROSS)])
        first = move(source, UP_FIRST)
        down = move(source, DOWN)
        second = move(first, UP_SECOND)
        third = move(second, UP_THIRD)
        outer = lax.select_n(order, source, first, second, third)
        inner = lax.select_n(order, down, source, first, second)
        own_k = jnp.where(columns_match, outer, inner)
        near_k = jnp.where(columns_match, inner, outer)
        lefts.append((own_k, swap(near_k, "example", 1), near_k, swap(own_k, "example", 1)))
    came = [
        swap(partial_product(1, offset, *lefts[k], down_weight, weight_near, jnp.bfloat16), "example", 2)
        for k in range(CHUNKS)
    ]
    own = [
        partial_product(0, offset, *lefts[k], down_weight, weight_near, jnp.float32)
        for k in range(CHUNKS)
    ]

    inputs_rows = layer_input.reshape(row_total, width_local)
    gate_values = gate_pre.reshape(row_total, hidden_local).astype(jnp.float32)
    up_values = up_pre.reshape(row_total, hidden_local).astype(jnp.float32)
    hidden = (gate_values * jax.nn.sigmoid(gate_values) * up_values).astype(jnp.bfloat16)
    early = jnp.concatenate(
        [
            contract(inputs_rows, proj_input),
            contract(hidden, proj_hidden),
            contract(grad_rows, proj_output),
        ]
    )
    early, _ = lax.optimization_barrier((early, lefts[-1][0]))
    early = sum_over(early, "tensor")
    in_gate, in_down, out_down = (early[k * row_total : (k + 1) * row_total] for k in range(3))
    slots_here = jnp.concatenate(
        [
            take(rev_slot, example_at * ex_count, ex_count, 0),
            take(rev_slot, (example_at ^ 1) * ex_count, ex_count, 0),
        ]
    )
    table = pairing_table(slots_here, rev_pairs)
    mask = (positions[None, :] < own_lengths[:, None]).astype(jnp.float32).reshape(row_total)
    left_down = take(in_down, tensor_at * per_rank, per_rank, 1) * mask[:, None]
    sketch_down = jnp.einsum(
        "pe,eti,etj->pij",
        table[:, :ex_count],
        left_down.reshape(ex_count, slot_len, per_rank),
        out_down.reshape(ex_count, slot_len, rank_size),
        precision=lax.Precision.HIGHEST,
    )
    in_gate = jnp.concatenate([in_gate, swap(in_gate, "example", 1)])
    select = jnp.arange(capacity, dtype=jnp.int32)[:, None] == place
    in_gate = jnp.dot(select.astype(jnp.float32), in_gate, precision=lax.Precision.HIGHEST)
    table_rows = jnp.dot(
        select.astype(jnp.bfloat16), jnp.repeat(table, slot_len, axis=1).T.astype(jnp.bfloat16)
    )
    left = table_rows.astype(jnp.float32)[:, :, None] * in_gate[:, None, :]
    left = left.reshape(capacity, rev_pairs * rank_size)

    right = [
        jnp.concatenate(finish(offset, own[k], came[k], gate_packed[k], up_packed[k], proj_gate, proj_up), axis=1)
        for k in range(CHUNKS)
    ]
    sketch_late = lax.dot_general(
        left, jnp.concatenate(right), (((0,), (0,)), ((), ())), precision=lax.Precision.HIGHEST
    ).reshape(rev_pairs, rank_size, 2 * rank_size)
    sketch_late = scatter_over(sketch_late, "tensor", 1)
    revision_pairs = sum_over(jnp.concatenate([sketch_late, sketch_down], axis=2), "example")
    example_scores = contract_exact(
        revision_pairs.reshape(rev_pairs, -1), query_sketches.astype(jnp.float32)
    )
    query_pairs = query_slot.shape[0] * 4 // 2
    pair_terms = contract_exact(example_scores, pairing_table(query_slot, query_pairs))
    total = sum_over(scatter_over(pair_terms, "example", 1), "tensor")
    return total / jnp.float32(rank_size * rank_size)


def local_four(
    layer_input,
    gate_pre,
    up_pre,
    output_grad,
    down_weight,
    proj_input,
    proj_hidden,
    proj_output,
    proj_gate,
    proj_up,
    query_sketches,
    rev_lengths,
    rev_slot,
    query_slot,
):
    ex_count, slot_len, width_local = layer_input.shape
    row_total = ex_count * slot_len
    grad_rows = output_grad.reshape(row_total, width_local)
    grad_near = swap(grad_rows, "example", 1)
    others = [swap(rev_lengths, "example", bits) for bits in (1, 2, 3)]
    sums = jnp.stack([jnp.sum(rev_lengths) + jnp.sum(others[0]), jnp.sum(others[1]) + jnp.sum(others[2])])
    most = jnp.max(sums).reshape(1)
    count = lax.axis_size("group")
    for step in range(1, count):
        shifted = lax.ppermute(most, "group", [(i, (i + step) % count) for i in range(count)])
        most = jnp.maximum(most, shifted)
    full = 2 * row_total
    levels = [level for level in LEVELS if level < full] + [full]
    branch = jnp.sum((most[0] > jnp.array(levels[:-1], jnp.int32)).astype(jnp.int32))
    return lax.switch(
        branch,
        [functools.partial(packed_scores, level) for level in levels],
        (
            layer_input,
            gate_pre,
            up_pre,
            grad_rows,
            grad_near,
            down_weight,
            proj_input,
            proj_hidden,
            proj_output,
            proj_gate,
            proj_up,
            query_sketches,
            query_slot,
            rev_slot,
            rev_lengths,
            others[0],
        ),
    )


def local_any(
    layer_input,
    gate_pre,
    up_pre,
    output_grad,
    down_weight,
    proj_input,
    proj_hidden,
    proj_output,
    proj_gate,
    proj_up,
    query_sketches,
    rev_lengths,
    rev_slot,
    query_slot,
):
    ex_count, slot_len, width_local = layer_input.shape
    hidden_local = gate_pre.shape[2]
    row_total = ex_count * slot_len
    rank_size = proj_input.shape[0]
    per_rank = rank_size // lax.axis_size("tensor")
    inputs_rows = layer_input.reshape(row_total, width_local)
    grad_rows = output_grad.reshape(row_total, width_local)
    gate_values = gate_pre.reshape(row_total, hidden_local).astype(jnp.float32)
    up_values = up_pre.reshape(row_total, hidden_local).astype(jnp.float32)
    grad_full = lax.all_gather(grad_rows, "tensor", axis=1, tiled=True)
    hidden_grad = contract(grad_full, lax.all_gather(down_weight, "example", axis=1, tiled=True))
    hidden_grad = lax.optimization_barrier(hidden_grad.astype(jnp.bfloat16)).astype(jnp.float32)
    sigma = jax.nn.sigmoid(gate_values)
    active = gate_values * sigma
    hidden = (active * up_values).astype(jnp.bfloat16)
    grad_up = (hidden_grad * active).astype(jnp.bfloat16)
    grad_gate = (hidden_grad * up_values * sigma * (1.0 + gate_values * (1.0 - sigma))).astype(
        jnp.bfloat16
    )
    partials = jnp.stack(
        [
            contract(inputs_rows, proj_input),
            contract(hidden, proj_hidden),
            contract(grad_gate, proj_gate),
            contract(grad_up, proj_up),
            contract(grad_rows, proj_output),
        ]
    )
    summed = lax.psum(partials, "tensor")
    begin = lax.axis_index("tensor") * per_rank
    left = lax.dynamic_slice_in_dim(summed[:2], begin, per_rank, 2)
    right = summed[2:]
    positions = jnp.arange(slot_len, dtype=jnp.int32)
    mask = (positions[None, :] < rev_lengths[:, None]).astype(jnp.float32).reshape(row_total)
    left = left * mask[None, :, None]
    left = jnp.stack([left[0], left[0], left[1]]).reshape(3, ex_count, slot_len, per_rank)
    right = right.reshape(3, ex_count, slot_len, rank_size)
    sketches = jnp.einsum("meti,metj->eimj", left, right, precision=lax.Precision.HIGHEST).reshape(
        ex_count, per_rank * 3 * rank_size
    )
    every_sketch = lax.all_gather(sketches, "example", axis=0, tiled=True)
    rev_pairs = rev_slot.shape[0] // 2
    revision_pairs = jnp.dot(
        pairing_table(rev_slot, rev_pairs), every_sketch, precision=lax.Precision.HIGHEST
    )
    example_scores = contract_exact(revision_pairs, query_sketches.astype(jnp.float32))
    query_pairs = query_slot.shape[0] * lax.axis_size("example") // 2
    pair_terms = contract_exact(example_scores, pairing_table(query_slot, query_pairs))
    owned = lax.psum_scatter(pair_terms, "example", scatter_dimension=1, tiled=True)
    total = lax.psum(owned, "tensor")
    return total / jnp.float32(rank_size * rank_size)


def solution(mesh):
    four = mesh.shape["tensor"] == 4 and mesh.shape["example"] == 4
    return jax.shard_map(
        local_four if four else local_any,
        mesh=mesh,
        in_specs=(
            P(("group", "example"), None, "tensor"),
            P(("group", "example"), None, "tensor"),
            P(("group", "example"), None, "tensor"),
            P(("group", "example"), None, "tensor"),
            P("tensor", "example"),
            P(None, "tensor"),
            P(None, "tensor"),
            P(None, "tensor"),
            P(None, "tensor"),
            P(None, "tensor"),
            P(("group", "example"), "tensor"),
            P(("group", "example")),
            P("group"),
            P(("group", "example")),
        ),
        out_specs=P("group", "example"),
        check_vma=False,
    )
```

```python
import functools

import jax
import jax.numpy as jnp
from jax import lax
from jax.experimental import pallas as pl
from jax.experimental.pallas import tpu as pltpu
from jax.sharding import PartitionSpec as P

CHUNKS = 4
LEVELS = (672, 704, 736, 768, 832)
TILE = 512
WIDE = 896
VMEM_LIMIT = 48 * 1024 * 1024


def contract(left_side, right_side):
    return lax.dot_general(
        left_side, right_side, (((1,), (1,)), ((), ())), preferred_element_type=jnp.float32
    )


def contract_exact(left_side, right_side):
    return lax.dot_general(
        left_side,
        right_side,
        (((1,), (1,)), ((), ())),
        precision=lax.Precision.HIGHEST,
        preferred_element_type=jnp.float32,
    )


def pairing_table(slots, pairs):
    pair_index = slots // 2
    signs = (1 - 2 * (slots % 2)).astype(jnp.float32)
    targets = jnp.arange(pairs, dtype=jnp.int32)
    return jnp.where(targets[:, None] == pair_index[None, :], signs[None, :], jnp.float32(0.0))


def take(array, start, size, axis):
    return lax.dynamic_slice_in_dim(array, start, size, axis)


def swap(array, axis, bits):
    count = lax.axis_size(axis)
    return lax.ppermute(array, axis, [(i, i ^ bits) for i in range(count)])


def kernel_params():
    return pltpu.CompilerParams(vmem_limit_bytes=VMEM_LIMIT)


def pack_kernel(starts, sizes, near_ref, place_ref, own_ref, other_ref, *refs):
    outs, select = refs[-1 - len(sizes) : -1], refs[-1]
    rows_own = own_ref.shape[0]

    @pl.when(pl.program_id(0) == 0)
    def _():
        base = 0
        for start, size in zip(starts, sizes):
            at = lax.broadcasted_iota(jnp.int32, (size, select.shape[1]), 0) + start
            select[base : base + size, :] = jnp.where(at == place_ref[...], 1.0, 0.0).astype(jnp.bfloat16)
            base += size

    base = 0
    for out, size in zip(outs, sizes):
        rows = slice(base, base + size)
        total = jnp.dot(select[rows, :rows_own], own_ref[...], preferred_element_type=jnp.float32)
        total += jnp.dot(select[rows, rows_own:], other_ref[...], preferred_element_type=jnp.float32)
        out[...] = total.astype(jnp.bfloat16)
        base += size


def pack(starts, sizes, near_offset, place, own, other, after=()):
    rows, columns = other.shape
    total = sum(sizes)
    return pl.pallas_call(
        functools.partial(pack_kernel, starts, sizes),
        grid_spec=pltpu.PrefetchScalarGridSpec(
            num_scalar_prefetch=1,
            grid=(columns // TILE,),
            in_specs=[
                pl.BlockSpec((1, 2 * rows), lambda i, near: (0, 0)),
                pl.BlockSpec((rows, TILE), lambda i, near: (0, near[0] + i)),
                pl.BlockSpec((rows, TILE), lambda i, near: (0, i)),
            ]
            + [pl.BlockSpec(memory_space=pl.ANY)] * len(after),
            out_specs=[pl.BlockSpec((size, TILE), lambda i, near: (0, i)) for size in sizes],
            scratch_shapes=[pltpu.VMEM((total, 2 * rows), jnp.bfloat16)],
        ),
        out_shape=[jax.ShapeDtypeStruct((size, columns), jnp.bfloat16) for size in sizes],
        compiler_params=kernel_params(),
        cost_estimate=pl.CostEstimate(
            flops=4 * total * rows * columns,
            bytes_accessed=(4 * rows + 2 * total) * columns,
            transcendentals=0,
        ),
        name="pack_rows",
    )(near_offset, place, own, other, *after)


def cut_kernel(far_ref, mine_in, away_in, *refs):
    mine_out, away_out = refs[-2:]
    mine_out[...] = mine_in[...]
    away_out[...] = away_in[...]


def cut(far, gathered, width, after):
    rows = gathered.shape[0]
    block = width // 2
    return pl.pallas_call(
        cut_kernel,
        grid_spec=pltpu.PrefetchScalarGridSpec(
            num_scalar_prefetch=1,
            grid=(4,),
            in_specs=[
                pl.BlockSpec((rows, block), lambda i, far: (0, 4 * far[0] + i)),
                pl.BlockSpec((rows, block), lambda i, far: (0, 4 * (1 - far[0]) + i)),
            ]
            + [pl.BlockSpec(memory_space=pl.ANY)] * len(after),
            out_specs=[pl.BlockSpec((rows, block), lambda i, far: (0, i))] * 2,
        ),
        out_shape=[jax.ShapeDtypeStruct((rows, 2 * width), gathered.dtype)] * 2,
        compiler_params=kernel_params(),
        cost_estimate=pl.CostEstimate(flops=0, bytes_accessed=16 * rows * width, transcendentals=0),
        name="cut_columns",
    )(far, gathered, gathered, *after)


def gate_kernel(value, *refs):
    refs[-1][...] = value[...]


def ordered(value, after):
    return pl.pallas_call(
        gate_kernel,
        in_specs=[pl.BlockSpec(memory_space=pltpu.VMEM)]
        + [pl.BlockSpec(memory_space=pl.ANY)] * len(after),
        out_specs=pl.BlockSpec(memory_space=pltpu.VMEM),
        out_shape=jax.ShapeDtypeStruct(value.shape, value.dtype),
        compiler_params=kernel_params(),
        name="ordered_copy",
    )(value, *after)


def partial_kernel(near_ref, a0, a1, b0, b1, keep_ref, other_ref, *refs):
    out_ref, left, right = refs[-3:]
    size, width = a0.shape

    @pl.when(pl.program_id(0) == 0)
    def _():
        left[...] = jnp.zeros_like(left)
        left[:size, :] = a0[...]
        left[size : 2 * size, :] = a1[...]
        right[:width, :] = left[...].T
        left[:size, :] = b0[...]
        left[size : 2 * size, :] = b1[...]
        right[width:, :] = left[...].T

    total = jnp.dot(keep_ref[...], right[:width, :], preferred_element_type=jnp.float32)
    total += jnp.dot(other_ref[...], right[width:, :], preferred_element_type=jnp.float32)
    out_ref[...] = total.T[: 2 * size, :].astype(out_ref.dtype)


def partial_product(near_offset, near, rows_here, rows_near, weight, weight_near, dtype, after):
    size, width = rows_here.shape[0], rows_here.shape[1] // 2
    hidden = weight_near.shape[0]
    padded = -(-2 * size // 128) * 128
    first = pl.BlockSpec((size, width), lambda i, offset, near: (0, near[0]))
    second = pl.BlockSpec((size, width), lambda i, offset, near: (0, 1 - near[0]))

    def body(offset_ref, near_ref, *refs):
        partial_kernel(near_ref, *refs)

    return pl.pallas_call(
        body,
        grid_spec=pltpu.PrefetchScalarGridSpec(
            num_scalar_prefetch=2,
            grid=(hidden // TILE,),
            in_specs=[first, first, second, second]
            + [
                pl.BlockSpec((TILE, width), lambda i, offset, near: (offset[0] + i, 0)),
                pl.BlockSpec((TILE, width), lambda i, offset, near: (i, 0)),
            ]
            + [pl.BlockSpec(memory_space=pl.ANY)] * len(after),
            out_specs=pl.BlockSpec((2 * size, TILE), lambda i, offset, near: (0, i)),
            scratch_shapes=[
                pltpu.VMEM((padded, width), jnp.bfloat16),
                pltpu.VMEM((2 * width, padded), jnp.bfloat16),
            ],
        ),
        out_shape=jax.ShapeDtypeStruct((2 * size, hidden), dtype),
        compiler_params=kernel_params(),
        cost_estimate=pl.CostEstimate(
            flops=8 * size * width * hidden,
            bytes_accessed=4 * width * hidden + 8 * size * hidden,
            transcendentals=0,
        ),
        name="partial_product",
    )(near_offset, near, rows_here, rows_near, rows_here, rows_near, weight, weight_near, *after)


def finish_kernel(near_ref, own_ref, came_ref, gate_ref, up_ref, proj_gate_ref, proj_up_ref, *refs):
    gate_out, up_out = refs[-2:]

    @pl.when(pl.program_id(0) == 0)
    def _():
        gate_out[...] = jnp.zeros_like(gate_out)
        up_out[...] = jnp.zeros_like(up_out)

    hidden_grad = (own_ref[...] + came_ref[...].astype(jnp.float32)).astype(jnp.bfloat16)
    hidden_grad = hidden_grad.astype(jnp.float32)
    gate = gate_ref[...].astype(jnp.float32)
    up = up_ref[...].astype(jnp.float32)
    sigma = jax.nn.sigmoid(gate)
    grad_up = (hidden_grad * (gate * sigma)).astype(jnp.bfloat16)
    grad_gate = (hidden_grad * up * sigma * (1.0 + gate * (1.0 - sigma))).astype(jnp.bfloat16)
    gate_out[...] += contract(grad_gate, proj_gate_ref[...])
    up_out[...] += contract(grad_up, proj_up_ref[...])


def finish(near_offset, own, came, gate, up, proj_gate, proj_up, after):
    rows, hidden = own.shape
    rank_size = proj_gate.shape[0]
    tile = pl.BlockSpec((rows, WIDE), lambda i, near: (0, i))
    proj = pl.BlockSpec((rank_size, WIDE), lambda i, near: (0, near[0] + i))
    out = pl.BlockSpec((rows, rank_size), lambda i, near: (0, 0))
    return pl.pallas_call(
        finish_kernel,
        grid_spec=pltpu.PrefetchScalarGridSpec(
            num_scalar_prefetch=1,
            grid=(hidden // WIDE,),
            in_specs=[tile, tile, tile, tile, proj, proj]
            + [pl.BlockSpec(memory_space=pl.ANY)] * len(after),
            out_specs=[out, out],
        ),
        out_shape=[jax.ShapeDtypeStruct((rows, rank_size), jnp.float32)] * 2,
        compiler_params=kernel_params(),
        cost_estimate=pl.CostEstimate(
            flops=4 * rows * hidden * rank_size,
            bytes_accessed=10 * rows * hidden,
            transcendentals=rows * hidden,
        ),
        name="finish_chunk",
    )(near_offset, own, came, gate, up, proj_gate, proj_up, *after)


def sum_over(array, axis):
    parts = [swap(array, axis, bits) for bits in (1, 2, 3)]
    return (array + parts[0]) + (parts[1] + parts[2])


def scatter_over(array, axis, dim):
    at = lax.axis_index(axis)
    size = array.shape[dim] // 4
    parts = [swap(take(array, (at ^ bits) * size, size, dim), axis, bits) for bits in (1, 2, 3)]
    return (take(array, at * size, size, dim) + parts[0]) + (parts[1] + parts[2])


def packed_scores(capacity, args):
    (
        layer_input,
        gate_pre,
        up_pre,
        grad_rows,
        grad_near,
        down_weight,
        proj_input,
        proj_hidden,
        proj_output,
        proj_gate,
        proj_up,
        query_sketches,
        query_slot,
        rev_slot,
        own_lengths,
        near_lengths,
    ) = args
    ex_count, slot_len, width_local = layer_input.shape
    hidden_local = gate_pre.shape[2]
    row_total = ex_count * slot_len
    rank_size = proj_input.shape[0]
    per_rank = rank_size // 4
    rev_pairs = rev_slot.shape[0] // 2
    example_at = lax.axis_index("example")
    tensor_at = lax.axis_index("tensor")
    near, far = example_at % 2, example_at // 2
    half_hidden = hidden_local // 2
    half_rows = capacity // 2
    units = half_rows // 16
    sizes = [16 * (units // CHUNKS + (k < units % CHUNKS)) for k in range(CHUNKS)]
    begins = [sum(sizes[:k]) for k in range(CHUNKS)]
    offset = (near * (half_hidden // TILE)).astype(jnp.int32).reshape(1)
    wide_offset = (near * (half_hidden // WIDE)).astype(jnp.int32).reshape(1)
    no_offset = jnp.zeros((1,), jnp.int32)

    both_lengths = jnp.concatenate([own_lengths, near_lengths])
    own_begin = near * jnp.sum(near_lengths)
    near_begin = (1 - near) * jnp.sum(own_lengths)
    offsets = jnp.concatenate(
        [
            own_begin + jnp.cumsum(own_lengths) - own_lengths,
            near_begin + jnp.cumsum(near_lengths) - near_lengths,
        ]
    )
    positions = jnp.arange(slot_len, dtype=jnp.int32)
    place = offsets[:, None] + positions[None, :] - near * half_rows
    place = jnp.where(place < 0, place + capacity, place)
    other_half = place >= half_rows
    at = jnp.where(other_half, place - half_rows, place)
    place = at + jnp.where(other_half, sizes[0], 0)
    for k in range(1, CHUNKS):
        place += jnp.where(
            at >= begins[k], sizes[k - 1] + jnp.where(other_half, sizes[k] - sizes[k - 1], 0), 0
        )
    place = jnp.where(positions[None, :] < both_lengths[:, None], place, -1).reshape(1, 2 * row_total)

    starts = [2 * b for b in begins]
    doubles = [2 * s for s in sizes]
    blocks = pack(starts, sizes, no_offset, place, grad_rows, grad_near)
    gathered = [lax.all_gather(block, "tensor", axis=1, tiled=True) for block in blocks]
    weight_near = swap(take(down_weight, (1 - near) * half_hidden, half_hidden, 0), "example", 1)

    def send_hidden(array):
        rows = array.reshape(row_total, hidden_local)
        return rows, swap(take(rows, (1 - near) * half_hidden, half_hidden, 1), "example", 1)

    gate_both, up_both = send_hidden(gate_pre), send_hidden(up_pre)

    near_at, far_at = near.astype(jnp.int32).reshape(1), far.astype(jnp.int32).reshape(1)
    width = down_weight.shape[1]
    came, own, right = [], [], []
    packed = {}

    def product(rows_here, rows_near, dtype, after):
        return partial_product(offset, near_at, rows_here, rows_near, down_weight, weight_near, dtype, after)

    def finish_step(k, after):
        right.append(
            jnp.concatenate(
                finish(wide_offset, own[k], came[k], packed["gate"][k], packed["up"][k], proj_gate, proj_up, after),
                axis=1,
            )
        )

    last, waiting = (), []
    for k in range(CHUNKS):
        mine, away = cut(far_at, gathered[k], width, last)
        far_rows = swap(away, "example", 2)
        mine_near = swap(mine, "example", 1)
        done = []
        if k == 1:
            packed["gate"] = pack(starts, doubles, offset, place, *gate_both, after=(away,))
            packed["up"] = pack(starts, doubles, offset, place, *up_both, after=(away,))
        if k > 0:
            own.append(product(*waiting, jnp.float32, (away,)))
            done.append(own[-1])
        if k > 1:
            finish_step(k - 2, (away,))
            done.append(right[-1])
        waiting = [mine, mine_near]
        partial = product(far_rows, swap(far_rows, "example", 1), jnp.bfloat16, tuple(done))
        came.append(swap(partial, "example", 2))
        last = (partial,)
    own.append(product(*waiting, jnp.float32, last))
    finish_step(CHUNKS - 2, (own[-1],))
    finish_step(CHUNKS - 1, (right[-1],))

    inputs_rows = layer_input.reshape(row_total, width_local)
    gate_values = gate_pre.reshape(row_total, hidden_local).astype(jnp.float32)
    up_values = up_pre.reshape(row_total, hidden_local).astype(jnp.float32)
    hidden = (gate_values * jax.nn.sigmoid(gate_values) * up_values).astype(jnp.bfloat16)
    early = jnp.concatenate(
        [
            contract(inputs_rows, proj_input),
            contract(hidden, proj_hidden),
            contract(grad_rows, proj_output),
        ]
    )
    early = sum_over(ordered(early, last), "tensor")
    in_gate, in_down, out_down = (early[k * row_total : (k + 1) * row_total] for k in range(3))
    slots_here = jnp.concatenate(
        [
            take(rev_slot, example_at * ex_count, ex_count, 0),
            take(rev_slot, (example_at ^ 1) * ex_count, ex_count, 0),
        ]
    )
    table = pairing_table(slots_here, rev_pairs)
    mask = (positions[None, :] < own_lengths[:, None]).astype(jnp.float32).reshape(row_total)
    left_down = take(in_down, tensor_at * per_rank, per_rank, 1) * mask[:, None]
    sketch_down = jnp.einsum(
        "pe,eti,etj->pij",
        table[:, :ex_count],
        left_down.reshape(ex_count, slot_len, per_rank),
        out_down.reshape(ex_count, slot_len, rank_size),
        precision=lax.Precision.HIGHEST,
    )
    in_gate = jnp.concatenate([in_gate, swap(in_gate, "example", 1)])
    select = jnp.arange(capacity, dtype=jnp.int32)[:, None] == place
    in_gate = jnp.dot(select.astype(jnp.float32), in_gate, precision=lax.Precision.HIGHEST)
    table_rows = jnp.dot(
        select.astype(jnp.bfloat16), jnp.repeat(table, slot_len, axis=1).T.astype(jnp.bfloat16)
    )
    left = table_rows.astype(jnp.float32)[:, :, None] * in_gate[:, None, :]
    left = left.reshape(capacity, rev_pairs * rank_size)

    sketch_late = lax.dot_general(
        left, jnp.concatenate(right), (((0,), (0,)), ((), ())), precision=lax.Precision.HIGHEST
    ).reshape(rev_pairs, rank_size, 2 * rank_size)
    sketch_late = scatter_over(sketch_late, "tensor", 1)
    revision_pairs = sum_over(jnp.concatenate([sketch_late, sketch_down], axis=2), "example")
    example_scores = contract_exact(
        revision_pairs.reshape(rev_pairs, -1), query_sketches.astype(jnp.float32)
    )
    query_pairs = query_slot.shape[0] * 4 // 2
    pair_terms = contract_exact(example_scores, pairing_table(query_slot, query_pairs))
    total = sum_over(scatter_over(pair_terms, "example", 1), "tensor")
    return total / jnp.float32(rank_size * rank_size)


def local_four(
    layer_input,
    gate_pre,
    up_pre,
    output_grad,
    down_weight,
    proj_input,
    proj_hidden,
    proj_output,
    proj_gate,
    proj_up,
    query_sketches,
    rev_lengths,
    rev_slot,
    query_slot,
):
    ex_count, slot_len, width_local = layer_input.shape
    row_total = ex_count * slot_len
    grad_rows = output_grad.reshape(row_total, width_local)
    grad_near = swap(grad_rows, "example", 1)
    others = [swap(rev_lengths, "example", bits) for bits in (1, 2, 3)]
    sums = jnp.stack([jnp.sum(rev_lengths) + jnp.sum(others[0]), jnp.sum(others[1]) + jnp.sum(others[2])])
    most = jnp.max(sums).reshape(1)
    count = lax.axis_size("group")
    for step in range(1, count):
        shifted = lax.ppermute(most, "group", [(i, (i + step) % count) for i in range(count)])
        most = jnp.maximum(most, shifted)
    full = 2 * row_total
    levels = [level for level in LEVELS if level < full] + [full]
    branch = jnp.sum((most[0] > jnp.array(levels[:-1], jnp.int32)).astype(jnp.int32))
    return lax.switch(
        branch,
        [functools.partial(packed_scores, level) for level in levels],
        (
            layer_input,
            gate_pre,
            up_pre,
            grad_rows,
            grad_near,
            down_weight,
            proj_input,
            proj_hidden,
            proj_output,
            proj_gate,
            proj_up,
            query_sketches,
            query_slot,
            rev_slot,
            rev_lengths,
            others[0],
        ),
    )


def local_any(
    layer_input,
    gate_pre,
    up_pre,
    output_grad,
    down_weight,
    proj_input,
    proj_hidden,
    proj_output,
    proj_gate,
    proj_up,
    query_sketches,
    rev_lengths,
    rev_slot,
    query_slot,
):
    ex_count, slot_len, width_local = layer_input.shape
    hidden_local = gate_pre.shape[2]
    row_total = ex_count * slot_len
    rank_size = proj_input.shape[0]
    per_rank = rank_size // lax.axis_size("tensor")
    inputs_rows = layer_input.reshape(row_total, width_local)
    grad_rows = output_grad.reshape(row_total, width_local)
    gate_values = gate_pre.reshape(row_total, hidden_local).astype(jnp.float32)
    up_values = up_pre.reshape(row_total, hidden_local).astype(jnp.float32)
    grad_full = lax.all_gather(grad_rows, "tensor", axis=1, tiled=True)
    hidden_grad = contract(grad_full, lax.all_gather(down_weight, "example", axis=1, tiled=True))
    hidden_grad = lax.optimization_barrier(hidden_grad.astype(jnp.bfloat16)).astype(jnp.float32)
    sigma = jax.nn.sigmoid(gate_values)
    active = gate_values * sigma
    hidden = (active * up_values).astype(jnp.bfloat16)
    grad_up = (hidden_grad * active).astype(jnp.bfloat16)
    grad_gate = (hidden_grad * up_values * sigma * (1.0 + gate_values * (1.0 - sigma))).astype(
        jnp.bfloat16
    )
    partials = jnp.stack(
        [
            contract(inputs_rows, proj_input),
            contract(hidden, proj_hidden),
            contract(grad_gate, proj_gate),
            contract(grad_up, proj_up),
            contract(grad_rows, proj_output),
        ]
    )
    summed = lax.psum(partials, "tensor")
    begin = lax.axis_index("tensor") * per_rank
    left = lax.dynamic_slice_in_dim(summed[:2], begin, per_rank, 2)
    right = summed[2:]
    positions = jnp.arange(slot_len, dtype=jnp.int32)
    mask = (positions[None, :] < rev_lengths[:, None]).astype(jnp.float32).reshape(row_total)
    left = left * mask[None, :, None]
    left = jnp.stack([left[0], left[0], left[1]]).reshape(3, ex_count, slot_len, per_rank)
    right = right.reshape(3, ex_count, slot_len, rank_size)
    sketches = jnp.einsum("meti,metj->eimj", left, right, precision=lax.Precision.HIGHEST).reshape(
        ex_count, per_rank * 3 * rank_size
    )
    every_sketch = lax.all_gather(sketches, "example", axis=0, tiled=True)
    rev_pairs = rev_slot.shape[0] // 2
    revision_pairs = jnp.dot(
        pairing_table(rev_slot, rev_pairs), every_sketch, precision=lax.Precision.HIGHEST
    )
    example_scores = contract_exact(revision_pairs, query_sketches.astype(jnp.float32))
    query_pairs = query_slot.shape[0] * lax.axis_size("example") // 2
    pair_terms = contract_exact(example_scores, pairing_table(query_slot, query_pairs))
    owned = lax.psum_scatter(pair_terms, "example", scatter_dimension=1, tiled=True)
    total = lax.psum(owned, "tensor")
    return total / jnp.float32(rank_size * rank_size)


def solution(mesh):
    four = mesh.shape["tensor"] == 4 and mesh.shape["example"] == 4
    return jax.shard_map(
        local_four if four else local_any,
        mesh=mesh,
        in_specs=(
            P(("group", "example"), None, "tensor"),
            P(("group", "example"), None, "tensor"),
            P(("group", "example"), None, "tensor"),
            P(("group", "example"), None, "tensor"),
            P("tensor", "example"),
            P(None, "tensor"),
            P(None, "tensor"),
            P(None, "tensor"),
            P(None, "tensor"),
            P(None, "tensor"),
            P(("group", "example"), "tensor"),
            P(("group", "example")),
            P("group"),
            P(("group", "example")),
        ),
        out_specs=P("group", "example"),
        check_vma=False,
    )
```

```python
import functools

import jax
import jax.numpy as jnp
from jax import lax
from jax.experimental import pallas as pl
from jax.experimental.pallas import tpu as pltpu
from jax.sharding import PartitionSpec as P

CHUNKS = 4
LEVELS = (736, 832)
TILE = 512
STEP = 256
WIDE = 896
VMEM_LIMIT = 58 * 1024 * 1024


def contract(left_side, right_side):
    return lax.dot_general(
        left_side, right_side, (((1,), (1,)), ((), ())), preferred_element_type=jnp.float32
    )


def contract_exact(left_side, right_side):
    return lax.dot_general(
        left_side,
        right_side,
        (((1,), (1,)), ((), ())),
        precision=lax.Precision.HIGHEST,
        preferred_element_type=jnp.float32,
    )


def pairing_table(slots, pairs):
    pair_index = slots // 2
    signs = (1 - 2 * (slots % 2)).astype(jnp.float32)
    targets = jnp.arange(pairs, dtype=jnp.int32)
    return jnp.where(targets[:, None] == pair_index[None, :], signs[None, :], jnp.float32(0.0))


def take(array, start, size, axis):
    return lax.dynamic_slice_in_dim(array, start, size, axis)


def swap(array, axis, bits):
    count = lax.axis_size(axis)
    return lax.ppermute(array, axis, [(i, i ^ bits) for i in range(count)])


def kernel_params():
    return pltpu.CompilerParams(vmem_limit_bytes=VMEM_LIMIT)


def pack_kernel(starts, sizes, near_ref, place_ref, own_ref, other_ref, *refs):
    outs, select = refs[-1 - len(sizes) : -1], refs[-1]
    rows_own = own_ref.shape[0]

    @pl.when(pl.program_id(0) == 0)
    def _():
        base = 0
        for start, size in zip(starts, sizes):
            at = lax.broadcasted_iota(jnp.int32, (size, select.shape[1]), 0) + start
            select[base : base + size, :] = jnp.where(at == place_ref[...], 1.0, 0.0).astype(jnp.bfloat16)
            base += size

    base = 0
    for out, size in zip(outs, sizes):
        rows = slice(base, base + size)
        total = jnp.dot(select[rows, :rows_own], own_ref[...], preferred_element_type=jnp.float32)
        total += jnp.dot(select[rows, rows_own:], other_ref[...], preferred_element_type=jnp.float32)
        out[...] = total.astype(jnp.bfloat16)
        base += size


def pack(starts, sizes, near_offset, place, own, other, after=()):
    rows, columns = other.shape
    total = sum(sizes)
    return pl.pallas_call(
        functools.partial(pack_kernel, starts, sizes),
        grid_spec=pltpu.PrefetchScalarGridSpec(
            num_scalar_prefetch=1,
            grid=(columns // TILE,),
            in_specs=[
                pl.BlockSpec((1, 2 * rows), lambda i, near: (0, 0)),
                pl.BlockSpec((rows, TILE), lambda i, near: (0, near[0] + i)),
                pl.BlockSpec((rows, TILE), lambda i, near: (0, i)),
            ]
            + [pl.BlockSpec(memory_space=pl.ANY)] * len(after),
            out_specs=[pl.BlockSpec((size, TILE), lambda i, near: (0, i)) for size in sizes],
            scratch_shapes=[pltpu.VMEM((total, 2 * rows), jnp.bfloat16)],
        ),
        out_shape=[jax.ShapeDtypeStruct((size, columns), jnp.bfloat16) for size in sizes],
        compiler_params=kernel_params(),
        cost_estimate=pl.CostEstimate(
            flops=4 * total * rows * columns,
            bytes_accessed=(4 * rows + 2 * total) * columns,
            transcendentals=0,
        ),
        name="pack_rows",
    )(near_offset, place, own, other, *after)


def cut_kernel(far_ref, mine_in, away_in, *refs):
    mine_out, away_out = refs[-2:]
    mine_out[...] = mine_in[...]
    away_out[...] = away_in[...]


def cut(far, gathered, width, after):
    rows = gathered.shape[0]
    block = width // 2
    return pl.pallas_call(
        cut_kernel,
        grid_spec=pltpu.PrefetchScalarGridSpec(
            num_scalar_prefetch=1,
            grid=(4,),
            in_specs=[
                pl.BlockSpec((rows, block), lambda i, far: (0, 4 * far[0] + i)),
                pl.BlockSpec((rows, block), lambda i, far: (0, 4 * (1 - far[0]) + i)),
            ]
            + [pl.BlockSpec(memory_space=pl.ANY)] * len(after),
            out_specs=[pl.BlockSpec((rows, block), lambda i, far: (0, i))] * 2,
        ),
        out_shape=[jax.ShapeDtypeStruct((rows, 2 * width), gathered.dtype)] * 2,
        compiler_params=kernel_params(),
        cost_estimate=pl.CostEstimate(flops=0, bytes_accessed=16 * rows * width, transcendentals=0),
        name="cut_columns",
    )(far, gathered, gathered, *after)


def gate_kernel(value, *refs):
    refs[-1][...] = value[...]


def ordered(value, after):
    return pl.pallas_call(
        gate_kernel,
        in_specs=[pl.BlockSpec(memory_space=pltpu.VMEM)]
        + [pl.BlockSpec(memory_space=pl.ANY)] * len(after),
        out_specs=pl.BlockSpec(memory_space=pltpu.VMEM),
        out_shape=jax.ShapeDtypeStruct(value.shape, value.dtype),
        compiler_params=kernel_params(),
        name="ordered_copy",
    )(value, *after)


def partial_kernel(parts, offset_ref, near_ref, keep_ref, other_ref, *refs):
    ins, outs = refs[: 4 * parts], refs[-1 - 2 * parts : -1 - parts]
    rights, left = refs[-1 - parts : -1], refs[-1]
    width = keep_ref.shape[1]

    @pl.when(pl.program_id(0) == 0)
    def _():
        left[...] = jnp.zeros_like(left)
        for part in range(parts):
            size = ins[4 * part].shape[0]
            padded = rights[part].shape[1]
            for side in range(2):
                left[:size, :] = ins[4 * part + 2 * side][...]
                left[size : 2 * size, :] = ins[4 * part + 2 * side + 1][...]

                @pl.loop(0, width // STEP)
                def _(c):
                    at = pl.multiple_of(c * STEP, STEP)
                    to = pl.multiple_of(side * width + c * STEP, STEP)
                    rights[part][pl.ds(to, STEP), :] = left[:padded, pl.ds(at, STEP)].T

    @pl.loop(0, TILE // STEP)
    def _(r):
        at = pl.multiple_of(r * STEP, STEP)
        rows = pl.ds(at, STEP)
        for part in range(parts):
            total = jnp.dot(keep_ref[rows, :], rights[part][:width, :], preferred_element_type=jnp.float32)
            total += jnp.dot(other_ref[rows, :], rights[part][width:, :], preferred_element_type=jnp.float32)
            out = outs[part]
            out[:, rows] = total.T[: out.shape[0], :].astype(out.dtype)


def partial_products(near_offset, near, parts, weight, weight_near, after):
    hidden, width = weight_near.shape
    ins, in_specs, out_specs, out_shape, rights = [], [], [], [], []
    most = 0
    for here, near_rows, dtype in parts:
        size = here.shape[0]
        padded = -(-2 * size // 128) * 128
        most = max(most, padded)
        ins += [here, near_rows, here, near_rows]
        in_specs += [pl.BlockSpec((size, width), lambda i, offset, near: (0, near[0]))] * 2
        in_specs += [pl.BlockSpec((size, width), lambda i, offset, near: (0, 1 - near[0]))] * 2
        out_specs.append(pl.BlockSpec((2 * size, TILE), lambda i, offset, near: (0, i)))
        out_shape.append(jax.ShapeDtypeStruct((2 * size, hidden), dtype))
        rights.append(pltpu.VMEM((2 * width, padded), jnp.bfloat16))
    total = sum(shape.shape[0] for shape in out_shape)
    return pl.pallas_call(
        functools.partial(partial_kernel, len(parts)),
        grid_spec=pltpu.PrefetchScalarGridSpec(
            num_scalar_prefetch=2,
            grid=(hidden // TILE,),
            in_specs=[
                pl.BlockSpec((TILE, width), lambda i, offset, near: (offset[0] + i, 0)),
                pl.BlockSpec((TILE, width), lambda i, offset, near: (i, 0)),
            ]
            + in_specs
            + [pl.BlockSpec(memory_space=pl.ANY)] * len(after),
            out_specs=out_specs,
            scratch_shapes=rights + [pltpu.VMEM((most, width), jnp.bfloat16)],
        ),
        out_shape=out_shape,
        compiler_params=kernel_params(),
        cost_estimate=pl.CostEstimate(
            flops=4 * total * width * hidden,
            bytes_accessed=4 * width * hidden + 4 * total * hidden,
            transcendentals=0,
        ),
        name="partial_products",
    )(near_offset, near, weight, weight_near, *ins, *after)


def copy_kernel(at_ref, value, *refs):
    refs[-1][...] = value[...]


def copy_half(array, at, axis, after):
    rows, columns = array.shape
    steps = 7
    if axis == 0:
        rows //= 2
        block = (rows // steps, columns)
        source, goal = (lambda i, at: (at[0] * steps + i, 0)), (lambda i, at: (i, 0))
    else:
        columns //= 2
        block = (rows, columns // steps)
        source, goal = (lambda i, at: (0, at[0] * steps + i)), (lambda i, at: (0, i))
    return pl.pallas_call(
        copy_kernel,
        grid_spec=pltpu.PrefetchScalarGridSpec(
            num_scalar_prefetch=1,
            grid=(steps,),
            in_specs=[pl.BlockSpec(block, source)] + [pl.BlockSpec(memory_space=pl.ANY)] * len(after),
            out_specs=pl.BlockSpec(block, goal),
        ),
        out_shape=jax.ShapeDtypeStruct((rows, columns), array.dtype),
        compiler_params=kernel_params(),
        cost_estimate=pl.CostEstimate(flops=0, bytes_accessed=4 * rows * columns, transcendentals=0),
        name="copy_half",
    )(at, array, *after)


def finish_kernel(near_ref, own_ref, came_ref, gate_ref, up_ref, proj_gate_ref, proj_up_ref, *refs):
    gate_out, up_out = refs[-2:]

    @pl.when(pl.program_id(0) == 0)
    def _():
        gate_out[...] = jnp.zeros_like(gate_out)
        up_out[...] = jnp.zeros_like(up_out)

    hidden_grad = (own_ref[...] + came_ref[...].astype(jnp.float32)).astype(jnp.bfloat16)
    hidden_grad = hidden_grad.astype(jnp.float32)
    gate = gate_ref[...].astype(jnp.float32)
    up = up_ref[...].astype(jnp.float32)
    sigma = jax.nn.sigmoid(gate)
    grad_up = (hidden_grad * (gate * sigma)).astype(jnp.bfloat16)
    grad_gate = (hidden_grad * up * sigma * (1.0 + gate * (1.0 - sigma))).astype(jnp.bfloat16)
    gate_out[...] += contract(grad_gate, proj_gate_ref[...])
    up_out[...] += contract(grad_up, proj_up_ref[...])


def finish(near_offset, own, came, gate, up, proj_gate, proj_up, after):
    rows, hidden = own.shape
    rank_size = proj_gate.shape[0]
    tile = pl.BlockSpec((rows, WIDE), lambda i, near: (0, i))
    proj = pl.BlockSpec((rank_size, WIDE), lambda i, near: (0, near[0] + i))
    out = pl.BlockSpec((rows, rank_size), lambda i, near: (0, 0))
    return pl.pallas_call(
        finish_kernel,
        grid_spec=pltpu.PrefetchScalarGridSpec(
            num_scalar_prefetch=1,
            grid=(hidden // WIDE,),
            in_specs=[tile, tile, tile, tile, proj, proj]
            + [pl.BlockSpec(memory_space=pl.ANY)] * len(after),
            out_specs=[out, out],
        ),
        out_shape=[jax.ShapeDtypeStruct((rows, rank_size), jnp.float32)] * 2,
        compiler_params=kernel_params(),
        cost_estimate=pl.CostEstimate(
            flops=4 * rows * hidden * rank_size,
            bytes_accessed=10 * rows * hidden,
            transcendentals=rows * hidden,
        ),
        name="finish_chunk",
    )(near_offset, own, came, gate, up, proj_gate, proj_up, *after)


def sum_over(array, axis):
    parts = [swap(array, axis, bits) for bits in (1, 2, 3)]
    return (array + parts[0]) + (parts[1] + parts[2])


def scatter_over(array, axis, dim):
    at = lax.axis_index(axis)
    size = array.shape[dim] // 4
    parts = [swap(take(array, (at ^ bits) * size, size, dim), axis, bits) for bits in (1, 2, 3)]
    return (take(array, at * size, size, dim) + parts[0]) + (parts[1] + parts[2])


def packed_scores(capacity, args):
    (
        layer_input,
        gate_pre,
        up_pre,
        grad_rows,
        grad_near,
        down_weight,
        proj_input,
        proj_hidden,
        proj_output,
        proj_gate,
        proj_up,
        rev_slot,
        own_lengths,
        near_lengths,
    ) = args
    ex_count, slot_len, width_local = layer_input.shape
    hidden_local = gate_pre.shape[2]
    row_total = ex_count * slot_len
    rank_size = proj_input.shape[0]
    per_rank = rank_size // 4
    rev_pairs = rev_slot.shape[0] // 2
    example_at = lax.axis_index("example")
    tensor_at = lax.axis_index("tensor")
    near, far = example_at % 2, example_at // 2
    half_hidden = hidden_local // 2
    half_rows = capacity // 2
    units = half_rows // 16
    sizes = [16 * (units // CHUNKS + (k < units % CHUNKS)) for k in range(CHUNKS)]
    begins = [sum(sizes[:k]) for k in range(CHUNKS)]
    offset = (near * (half_hidden // TILE)).astype(jnp.int32).reshape(1)
    wide_offset = (near * (half_hidden // WIDE)).astype(jnp.int32).reshape(1)
    no_offset = jnp.zeros((1,), jnp.int32)

    both_lengths = jnp.concatenate([own_lengths, near_lengths])
    own_begin = near * jnp.sum(near_lengths)
    near_begin = (1 - near) * jnp.sum(own_lengths)
    offsets = jnp.concatenate(
        [
            own_begin + jnp.cumsum(own_lengths) - own_lengths,
            near_begin + jnp.cumsum(near_lengths) - near_lengths,
        ]
    )
    positions = jnp.arange(slot_len, dtype=jnp.int32)
    place = offsets[:, None] + positions[None, :] - near * half_rows
    place = jnp.where(place < 0, place + capacity, place)
    other_half = place >= half_rows
    at = jnp.where(other_half, place - half_rows, place)
    place = at + jnp.where(other_half, sizes[0], 0)
    for k in range(1, CHUNKS):
        place += jnp.where(
            at >= begins[k], sizes[k - 1] + jnp.where(other_half, sizes[k] - sizes[k - 1], 0), 0
        )
    place = jnp.where(positions[None, :] < both_lengths[:, None], place, -1).reshape(1, 2 * row_total)

    starts = [2 * b for b in begins]
    doubles = [2 * s for s in sizes]
    blocks = pack(starts, sizes, no_offset, place, grad_rows, grad_near)
    gathered = [lax.all_gather(block, "tensor", axis=1, tiled=True) for block in blocks]
    near_at, far_at = near.astype(jnp.int32).reshape(1), far.astype(jnp.int32).reshape(1)
    gate_rows = gate_pre.reshape(row_total, hidden_local)
    up_rows = up_pre.reshape(row_total, hidden_local)
    weight_sent = copy_half(down_weight, 1 - near_at, 0, (blocks[0],))
    gate_sent = copy_half(gate_rows, 1 - near_at, 1, (weight_sent,))
    up_sent = copy_half(up_rows, 1 - near_at, 1, (gate_sent,))
    weight_near = swap(weight_sent, "example", 1)
    gate_near = swap(gate_sent, "example", 1)
    up_near = swap(up_sent, "example", 1)

    width = down_weight.shape[1]
    came, own, right = [], [], []
    packed = {}

    def products(parts, after):
        return partial_products(offset, near_at, parts, down_weight, weight_near, after)

    def finish_step(k, after):
        right.append(
            jnp.concatenate(
                finish(wide_offset, own[k], came[k], packed["gate"][k], packed["up"][k], proj_gate, proj_up, after),
                axis=1,
            )
        )

    last, waiting = (up_sent,), []
    for k in range(CHUNKS):
        mine, away = cut(far_at, gathered[k], width, last)
        far_rows = swap(away, "example", 2)
        mine_near = swap(mine, "example", 1)
        done = []
        if k == 1:
            packed["gate"] = pack(starts, doubles, offset, place, gate_rows, gate_near, after=(away,))
            packed["up"] = pack(starts, doubles, offset, place, up_rows, up_near, after=(away,))
            done += [packed["gate"][0], packed["up"][0]]
        if k > 1:
            finish_step(k - 2, (away,))
            done.append(right[-1])
        parts = [(far_rows, swap(far_rows, "example", 1), jnp.bfloat16)]
        if k > 0:
            parts.append((*waiting, jnp.float32))
        results = products(parts, tuple(done))
        own += results[1:]
        waiting = [mine, mine_near]
        came.append(swap(results[0], "example", 2))
        last = (results[0],)
    own += products([(*waiting, jnp.float32)], last)
    finish_step(CHUNKS - 2, (own[-1],))
    finish_step(CHUNKS - 1, (right[-1],))

    inputs_rows = layer_input.reshape(row_total, width_local)
    gate_values = gate_pre.reshape(row_total, hidden_local).astype(jnp.float32)
    up_values = up_pre.reshape(row_total, hidden_local).astype(jnp.float32)
    hidden = (gate_values * jax.nn.sigmoid(gate_values) * up_values).astype(jnp.bfloat16)
    early = jnp.concatenate(
        [
            contract(inputs_rows, proj_input),
            contract(hidden, proj_hidden),
            contract(grad_rows, proj_output),
        ]
    )
    early = sum_over(ordered(early, last), "tensor")
    in_gate, in_down, out_down = (early[k * row_total : (k + 1) * row_total] for k in range(3))
    slots_here = jnp.concatenate(
        [
            take(rev_slot, example_at * ex_count, ex_count, 0),
            take(rev_slot, (example_at ^ 1) * ex_count, ex_count, 0),
        ]
    )
    table = pairing_table(slots_here, rev_pairs)
    mask = (positions[None, :] < own_lengths[:, None]).astype(jnp.float32).reshape(row_total)
    left_down = take(in_down, tensor_at * per_rank, per_rank, 1) * mask[:, None]
    sketch_down = jnp.einsum(
        "pe,eti,etj->pij",
        table[:, :ex_count],
        left_down.reshape(ex_count, slot_len, per_rank),
        out_down.reshape(ex_count, slot_len, rank_size),
        precision=lax.Precision.HIGHEST,
    )
    in_gate = jnp.concatenate([in_gate, swap(in_gate, "example", 1)])
    select = jnp.arange(capacity, dtype=jnp.int32)[:, None] == place
    in_gate = jnp.dot(select.astype(jnp.float32), in_gate, precision=lax.Precision.HIGHEST)
    table_rows = jnp.dot(
        select.astype(jnp.bfloat16), jnp.repeat(table, slot_len, axis=1).T.astype(jnp.bfloat16)
    )
    left = table_rows.astype(jnp.float32)[:, :, None] * in_gate[:, None, :]
    left = left.reshape(capacity, rev_pairs * rank_size)

    sketch_late = lax.dot_general(
        left, jnp.concatenate(right), (((0,), (0,)), ((), ())), precision=lax.Precision.HIGHEST
    ).reshape(rev_pairs, rank_size, 2 * rank_size)
    return sketch_late, sketch_down


def local_four(
    layer_input,
    gate_pre,
    up_pre,
    output_grad,
    down_weight,
    proj_input,
    proj_hidden,
    proj_output,
    proj_gate,
    proj_up,
    query_sketches,
    rev_lengths,
    rev_slot,
    query_slot,
):
    ex_count, slot_len, width_local = layer_input.shape
    row_total = ex_count * slot_len
    grad_rows = output_grad.reshape(row_total, width_local)
    grad_near = swap(grad_rows, "example", 1)
    others = [swap(rev_lengths, "example", bits) for bits in (1, 2, 3)]
    sums = jnp.stack([jnp.sum(rev_lengths) + jnp.sum(others[0]), jnp.sum(others[1]) + jnp.sum(others[2])])
    most = jnp.max(sums).reshape(1)
    count = lax.axis_size("group")
    for step in range(1, count):
        shifted = lax.ppermute(most, "group", [(i, (i + step) % count) for i in range(count)])
        most = jnp.maximum(most, shifted)
    full = 2 * row_total
    levels = [level for level in LEVELS if level < full] + [full]
    branch = jnp.sum((most[0] > jnp.array(levels[:-1], jnp.int32)).astype(jnp.int32))
    sketch_late, sketch_down = lax.switch(
        branch,
        [functools.partial(packed_scores, level) for level in levels],
        (
            layer_input,
            gate_pre,
            up_pre,
            grad_rows,
            grad_near,
            down_weight,
            proj_input,
            proj_hidden,
            proj_output,
            proj_gate,
            proj_up,
            rev_slot,
            rev_lengths,
            others[0],
        ),
    )
    rank_size = proj_input.shape[0]
    rev_pairs = rev_slot.shape[0] // 2
    sketch_late = scatter_over(sketch_late, "tensor", 1)
    revision_pairs = sum_over(jnp.concatenate([sketch_late, sketch_down], axis=2), "example")
    example_scores = contract_exact(
        revision_pairs.reshape(rev_pairs, -1), query_sketches.astype(jnp.float32)
    )
    query_pairs = query_slot.shape[0] * 4 // 2
    pair_terms = contract_exact(example_scores, pairing_table(query_slot, query_pairs))
    total = sum_over(scatter_over(pair_terms, "example", 1), "tensor")
    return total / jnp.float32(rank_size * rank_size)


def local_any(
    layer_input,
    gate_pre,
    up_pre,
    output_grad,
    down_weight,
    proj_input,
    proj_hidden,
    proj_output,
    proj_gate,
    proj_up,
    query_sketches,
    rev_lengths,
    rev_slot,
    query_slot,
):
    ex_count, slot_len, width_local = layer_input.shape
    hidden_local = gate_pre.shape[2]
    row_total = ex_count * slot_len
    rank_size = proj_input.shape[0]
    per_rank = rank_size // lax.axis_size("tensor")
    inputs_rows = layer_input.reshape(row_total, width_local)
    grad_rows = output_grad.reshape(row_total, width_local)
    gate_values = gate_pre.reshape(row_total, hidden_local).astype(jnp.float32)
    up_values = up_pre.reshape(row_total, hidden_local).astype(jnp.float32)
    grad_full = lax.all_gather(grad_rows, "tensor", axis=1, tiled=True)
    hidden_grad = contract(grad_full, lax.all_gather(down_weight, "example", axis=1, tiled=True))
    hidden_grad = lax.optimization_barrier(hidden_grad.astype(jnp.bfloat16)).astype(jnp.float32)
    sigma = jax.nn.sigmoid(gate_values)
    active = gate_values * sigma
    hidden = (active * up_values).astype(jnp.bfloat16)
    grad_up = (hidden_grad * active).astype(jnp.bfloat16)
    grad_gate = (hidden_grad * up_values * sigma * (1.0 + gate_values * (1.0 - sigma))).astype(
        jnp.bfloat16
    )
    partials = jnp.stack(
        [
            contract(inputs_rows, proj_input),
            contract(hidden, proj_hidden),
            contract(grad_gate, proj_gate),
            contract(grad_up, proj_up),
            contract(grad_rows, proj_output),
        ]
    )
    summed = lax.psum(partials, "tensor")
    begin = lax.axis_index("tensor") * per_rank
    left = lax.dynamic_slice_in_dim(summed[:2], begin, per_rank, 2)
    right = summed[2:]
    positions = jnp.arange(slot_len, dtype=jnp.int32)
    mask = (positions[None, :] < rev_lengths[:, None]).astype(jnp.float32).reshape(row_total)
    left = left * mask[None, :, None]
    left = jnp.stack([left[0], left[0], left[1]]).reshape(3, ex_count, slot_len, per_rank)
    right = right.reshape(3, ex_count, slot_len, rank_size)
    sketches = jnp.einsum("meti,metj->eimj", left, right, precision=lax.Precision.HIGHEST).reshape(
        ex_count, per_rank * 3 * rank_size
    )
    every_sketch = lax.all_gather(sketches, "example", axis=0, tiled=True)
    rev_pairs = rev_slot.shape[0] // 2
    revision_pairs = jnp.dot(
        pairing_table(rev_slot, rev_pairs), every_sketch, precision=lax.Precision.HIGHEST
    )
    example_scores = contract_exact(revision_pairs, query_sketches.astype(jnp.float32))
    query_pairs = query_slot.shape[0] * lax.axis_size("example") // 2
    pair_terms = contract_exact(example_scores, pairing_table(query_slot, query_pairs))
    owned = lax.psum_scatter(pair_terms, "example", scatter_dimension=1, tiled=True)
    total = lax.psum(owned, "tensor")
    return total / jnp.float32(rank_size * rank_size)


def solution(mesh):
    four = mesh.shape["tensor"] == 4 and mesh.shape["example"] == 4
    return jax.shard_map(
        local_four if four else local_any,
        mesh=mesh,
        in_specs=(
            P(("group", "example"), None, "tensor"),
            P(("group", "example"), None, "tensor"),
            P(("group", "example"), None, "tensor"),
            P(("group", "example"), None, "tensor"),
            P("tensor", "example"),
            P(None, "tensor"),
            P(None, "tensor"),
            P(None, "tensor"),
            P(None, "tensor"),
            P(None, "tensor"),
            P(("group", "example"), "tensor"),
            P(("group", "example")),
            P("group"),
            P(("group", "example")),
        ),
        out_specs=P("group", "example"),
        check_vma=False,
    )
```

```python
import functools

import jax
import jax.numpy as jnp
from jax import lax
from jax.experimental import pallas as pl
from jax.experimental.pallas import tpu as pltpu
from jax.sharding import PartitionSpec as P

LEVELS = (736, 832)
TILE = 512
STEP = 256
LANES = 128
VMEM_LIMIT = 58 * 1024 * 1024


def contract(left_side, right_side):
    return lax.dot_general(
        left_side, right_side, (((1,), (1,)), ((), ())), preferred_element_type=jnp.float32
    )


def contract_exact(left_side, right_side):
    return lax.dot_general(
        left_side,
        right_side,
        (((1,), (1,)), ((), ())),
        precision=lax.Precision.HIGHEST,
        preferred_element_type=jnp.float32,
    )


def pairing_table(slots, pairs):
    pair_index = slots // 2
    signs = (1 - 2 * (slots % 2)).astype(jnp.float32)
    targets = jnp.arange(pairs, dtype=jnp.int32)
    return jnp.where(targets[:, None] == pair_index[None, :], signs[None, :], jnp.float32(0.0))


def take(array, start, size, axis):
    return lax.dynamic_slice_in_dim(array, start, size, axis)


def swap(array, axis, bits):
    count = lax.axis_size(axis)
    return lax.ppermute(array, axis, [(i, i ^ bits) for i in range(count)])


def kernel_params():
    return pltpu.CompilerParams(vmem_limit_bytes=VMEM_LIMIT)


def pack_kernel(starts, sizes, near_ref, place_ref, own_ref, other_ref, *refs):
    outs, select = refs[-1 - len(sizes) : -1], refs[-1]
    rows_own = own_ref.shape[0]

    @pl.when(pl.program_id(0) == 0)
    def _():
        base = 0
        for start, size in zip(starts, sizes):
            at = lax.broadcasted_iota(jnp.int32, (size, select.shape[1]), 0) + start
            select[base : base + size, :] = jnp.where(at == place_ref[...], 1.0, 0.0).astype(jnp.bfloat16)
            base += size

    base = 0
    for out, size in zip(outs, sizes):
        rows = slice(base, base + size)
        total = jnp.dot(select[rows, :rows_own], own_ref[...], preferred_element_type=jnp.float32)
        total += jnp.dot(select[rows, rows_own:], other_ref[...], preferred_element_type=jnp.float32)
        out[...] = total.astype(jnp.bfloat16)
        base += size


def pack(starts, sizes, near_offset, place, own, other, after=()):
    rows, columns = other.shape
    total = sum(sizes)
    return pl.pallas_call(
        functools.partial(pack_kernel, starts, sizes),
        grid_spec=pltpu.PrefetchScalarGridSpec(
            num_scalar_prefetch=1,
            grid=(columns // TILE,),
            in_specs=[
                pl.BlockSpec((1, 2 * rows), lambda i, near: (0, 0)),
                pl.BlockSpec((rows, TILE), lambda i, near: (0, near[0] + i)),
                pl.BlockSpec((rows, TILE), lambda i, near: (0, i)),
            ]
            + [pl.BlockSpec(memory_space=pl.ANY)] * len(after),
            out_specs=[pl.BlockSpec((size, TILE), lambda i, near: (0, i)) for size in sizes],
            scratch_shapes=[pltpu.VMEM((total, 2 * rows), jnp.bfloat16)],
        ),
        out_shape=[jax.ShapeDtypeStruct((size, columns), jnp.bfloat16) for size in sizes],
        compiler_params=kernel_params(),
        cost_estimate=pl.CostEstimate(
            flops=4 * total * rows * columns,
            bytes_accessed=(4 * rows + 2 * total) * columns,
            transcendentals=0,
        ),
        name="pack_rows",
    )(near_offset, place, own, other, *after)


def cut_kernel(far_ref, mine_in, away_in, *refs):
    mine_out, away_out = refs[-2:]
    mine_out[...] = mine_in[...]
    away_out[...] = away_in[...]


def cut(far, gathered, width, after):
    rows = gathered.shape[0]
    block = width // 2
    return pl.pallas_call(
        cut_kernel,
        grid_spec=pltpu.PrefetchScalarGridSpec(
            num_scalar_prefetch=1,
            grid=(4,),
            in_specs=[
                pl.BlockSpec((rows, block), lambda i, far: (0, 4 * far[0] + i)),
                pl.BlockSpec((rows, block), lambda i, far: (0, 4 * (1 - far[0]) + i)),
            ]
            + [pl.BlockSpec(memory_space=pl.ANY)] * len(after),
            out_specs=[pl.BlockSpec((rows, block), lambda i, far: (0, i))] * 2,
        ),
        out_shape=[jax.ShapeDtypeStruct((rows, 2 * width), gathered.dtype)] * 2,
        compiler_params=kernel_params(),
        cost_estimate=pl.CostEstimate(flops=0, bytes_accessed=16 * rows * width, transcendentals=0),
        name="cut_columns",
    )(far, gathered, gathered, *after)


def gate_kernel(value, *refs):
    refs[-1][...] = value[...]


def ordered(value, after):
    return pl.pallas_call(
        gate_kernel,
        in_specs=[pl.BlockSpec(memory_space=pltpu.VMEM)]
        + [pl.BlockSpec(memory_space=pl.ANY)] * len(after),
        out_specs=pl.BlockSpec(memory_space=pltpu.VMEM),
        out_shape=jax.ShapeDtypeStruct(value.shape, value.dtype),
        compiler_params=kernel_params(),
        name="ordered_copy",
    )(value, *after)


def stage_kernel(far, own, offset_ref, near_ref, *refs):
    refs = list(refs)
    weights = [refs.pop(0) for _ in range(4)]
    far_ins = [refs.pop(0) for _ in range(4 * far)]
    own_ins = [refs.pop(0) for _ in range(4 * own)]
    extra = [refs.pop(0) for _ in range(5 * own)]
    left = refs.pop()
    own_right = refs.pop() if own else None
    far_right = refs.pop() if far else None
    out = refs.pop() if own else None
    far_out = refs.pop() if far else None
    depth = weights[0].shape[1]
    width = 2 * depth

    def turn(ins, right):
        size, padded = ins[0].shape[0], right.shape[1]
        if 2 * size < padded:
            left[2 * size : padded, :] = jnp.zeros((padded - 2 * size, width), jnp.bfloat16)
        for side in range(2):
            left[:size, :] = ins[2 * side][...]
            left[size : 2 * size, :] = ins[2 * side + 1][...]

            @pl.loop(0, width // STEP)
            def _(c):
                at = pl.multiple_of(c * STEP, STEP)
                to = pl.multiple_of(side * width + c * STEP, STEP)
                right[pl.ds(to, STEP), :] = left[:padded, pl.ds(at, STEP)].T

    def half_sum(rows, right):
        total = 0.0
        for k in range(4):
            block = right[k * depth : (k + 1) * depth, :]
            total += jnp.dot(weights[k][rows, :], block, preferred_element_type=jnp.float32)
        return total

    @pl.when(pl.program_id(0) == 0)
    def _():
        if far:
            turn(far_ins, far_right)
        if own:
            turn(own_ins, own_right)
            out[...] = jnp.zeros_like(out)

    @pl.loop(0, TILE // STEP)
    def _(r):
        rows = pl.ds(pl.multiple_of(r * STEP, STEP), STEP)
        if far:
            far_out[:, rows] = half_sum(rows, far_right).astype(jnp.bfloat16).T[: far_out.shape[0], :]
        if own:
            came, gate_ref, up_ref, proj_gate, proj_up = extra
            rank_size = proj_gate.shape[0]
            total = half_sum(rows, own_right).T[: came.shape[0], :]
            hidden_grad = (total + came[:, rows].astype(jnp.float32)).astype(jnp.bfloat16)
            hidden_grad = hidden_grad.astype(jnp.float32)
            gate = gate_ref[:, rows].astype(jnp.float32)
            up = up_ref[:, rows].astype(jnp.float32)
            sigma = jax.nn.sigmoid(gate)
            grad_up = (hidden_grad * (gate * sigma)).astype(jnp.bfloat16)
            grad_gate = (hidden_grad * up * sigma * (1.0 + gate * (1.0 - sigma))).astype(jnp.bfloat16)
            out[:, :rank_size] += contract(grad_gate, proj_gate[:, rows])
            out[:, rank_size:] += contract(grad_up, proj_up[:, rows])


def stage(near_offset, near, tiles, far, own, weight, weight_near, after):
    hidden, width = weight_near.shape
    begin, count = tiles
    depth = width // 2
    arrays, specs, outs, shapes, rights = [], [], [], [], []
    most = 0

    def add(array, block, index):
        arrays.append(array)
        specs.append(pl.BlockSpec(block, index))

    for k in range(2):
        add(weight, (TILE, depth), lambda i, offset, near, k=k: (offset[0] + begin + i, k))
    for k in range(2):
        add(weight_near, (TILE, depth), lambda i, offset, near, k=k: (begin + i, k))
    for rows in (far, own):
        if rows is not None:
            size = rows[0].shape[0]
            padded = -(-2 * size // LANES) * LANES
            most = max(most, padded)
            rights.append(pltpu.VMEM((2 * width, padded), jnp.bfloat16))
            for k in range(4):
                side = k // 2
                add(
                    rows[k % 2],
                    (size, width),
                    lambda i, offset, near, side=side: (0, near[0] + side * (1 - 2 * near[0])),
                )
    if far is not None:
        double = 2 * far[0].shape[0]
        outs.append(pl.BlockSpec((double, TILE), lambda i, offset, near: (0, i)))
        shapes.append(jax.ShapeDtypeStruct((double, count * TILE), jnp.bfloat16))
    if own is not None:
        came, gate, up, proj_gate, proj_up = own[2:]
        double, rank_size = came.shape[0], proj_gate.shape[0]
        add(came, (double, TILE), lambda i, offset, near: (0, i))
        for array in (gate, up):
            add(array, (double, TILE), lambda i, offset, near: (0, begin + i))
        for array in (proj_gate, proj_up):
            add(array, (rank_size, TILE), lambda i, offset, near: (0, offset[0] + begin + i))
        outs.append(pl.BlockSpec((double, 2 * rank_size), lambda i, offset, near: (0, 0)))
        shapes.append(jax.ShapeDtypeStruct((double, 2 * rank_size), jnp.float32))
    parts = len(rights)
    return pl.pallas_call(
        functools.partial(stage_kernel, far is not None, own is not None),
        grid_spec=pltpu.PrefetchScalarGridSpec(
            num_scalar_prefetch=2,
            grid=(count,),
            in_specs=specs + [pl.BlockSpec(memory_space=pl.ANY)] * len(after),
            out_specs=outs,
            scratch_shapes=rights + [pltpu.VMEM((most, width), jnp.bfloat16)],
        ),
        out_shape=shapes,
        compiler_params=kernel_params(),
        cost_estimate=pl.CostEstimate(
            flops=4 * parts * most * width * count * TILE,
            bytes_accessed=4 * width * count * TILE + 4 * parts * most * count * TILE,
            transcendentals=0,
        ),
        name="stage",
    )(near_offset, near, *arrays, *after)


def copy_kernel(at_ref, value, *refs):
    refs[-1][...] = value[...]


def copy_half(array, at, axis, after):
    rows, columns = array.shape
    steps = 7
    if axis == 0:
        rows //= 2
        block = (rows // steps, columns)
        source, goal = (lambda i, at: (at[0] * steps + i, 0)), (lambda i, at: (i, 0))
    else:
        columns //= 2
        block = (rows, columns // steps)
        source, goal = (lambda i, at: (0, at[0] * steps + i)), (lambda i, at: (0, i))
    return pl.pallas_call(
        copy_kernel,
        grid_spec=pltpu.PrefetchScalarGridSpec(
            num_scalar_prefetch=1,
            grid=(steps,),
            in_specs=[pl.BlockSpec(block, source)] + [pl.BlockSpec(memory_space=pl.ANY)] * len(after),
            out_specs=pl.BlockSpec(block, goal),
        ),
        out_shape=jax.ShapeDtypeStruct((rows, columns), array.dtype),
        compiler_params=kernel_params(),
        cost_estimate=pl.CostEstimate(flops=0, bytes_accessed=4 * rows * columns, transcendentals=0),
        name="copy_half",
    )(at, array, *after)


def sum_over(array, axis):
    parts = [swap(array, axis, bits) for bits in (1, 2, 3)]
    return (array + parts[0]) + (parts[1] + parts[2])


def scatter_over(array, axis, dim):
    at = lax.axis_index(axis)
    size = array.shape[dim] // 4
    parts = [swap(take(array, (at ^ bits) * size, size, dim), axis, bits) for bits in (1, 2, 3)]
    return (take(array, at * size, size, dim) + parts[0]) + (parts[1] + parts[2])


def packed_scores(capacity, args):
    (
        layer_input,
        gate_pre,
        up_pre,
        grad_rows,
        grad_near,
        down_weight,
        proj_input,
        proj_hidden,
        proj_output,
        proj_gate,
        proj_up,
        rev_slot,
        own_lengths,
        near_lengths,
    ) = args
    ex_count, slot_len, width_local = layer_input.shape
    hidden_local = gate_pre.shape[2]
    row_total = ex_count * slot_len
    rank_size = proj_input.shape[0]
    per_rank = rank_size // 4
    rev_pairs = rev_slot.shape[0] // 2
    example_at = lax.axis_index("example")
    tensor_at = lax.axis_index("tensor")
    near, far = example_at % 2, example_at // 2
    half_hidden = hidden_local // 2
    half_rows = capacity // 2
    chunks = -(-half_rows // LANES)
    units = half_rows // 16
    sizes = [16 * (units // chunks + (k < units % chunks)) for k in range(chunks)]
    begins = [sum(sizes[:k]) for k in range(chunks)]
    offset = (near * (half_hidden // TILE)).astype(jnp.int32).reshape(1)
    no_offset = jnp.zeros((1,), jnp.int32)

    both_lengths = jnp.concatenate([own_lengths, near_lengths])
    own_begin = near * jnp.sum(near_lengths)
    near_begin = (1 - near) * jnp.sum(own_lengths)
    offsets = jnp.concatenate(
        [
            own_begin + jnp.cumsum(own_lengths) - own_lengths,
            near_begin + jnp.cumsum(near_lengths) - near_lengths,
        ]
    )
    positions = jnp.arange(slot_len, dtype=jnp.int32)
    place = offsets[:, None] + positions[None, :] - near * half_rows
    place = jnp.where(place < 0, place + capacity, place)
    other_half = place >= half_rows
    at = jnp.where(other_half, place - half_rows, place)
    place = at + jnp.where(other_half, sizes[0], 0)
    for k in range(1, chunks):
        place += jnp.where(
            at >= begins[k], sizes[k - 1] + jnp.where(other_half, sizes[k] - sizes[k - 1], 0), 0
        )
    place = jnp.where(positions[None, :] < both_lengths[:, None], place, -1).reshape(1, 2 * row_total)

    starts = [2 * b for b in begins]
    doubles = [2 * s for s in sizes]
    blocks = pack(starts, sizes, no_offset, place, grad_rows, grad_near)
    gathered = [lax.all_gather(block, "tensor", axis=1, tiled=True) for block in blocks]
    near_at, far_at = near.astype(jnp.int32).reshape(1), far.astype(jnp.int32).reshape(1)
    gate_rows = gate_pre.reshape(row_total, hidden_local)
    up_rows = up_pre.reshape(row_total, hidden_local)
    weight_sent = copy_half(down_weight, 1 - near_at, 0, (blocks[0],))
    gate_sent = copy_half(gate_rows, 1 - near_at, 1, (weight_sent,))
    up_sent = copy_half(up_rows, 1 - near_at, 1, (gate_sent,))
    weight_near = swap(weight_sent, "example", 1)
    gate_near = swap(gate_sent, "example", 1)
    up_near = swap(up_sent, "example", 1)

    width = down_weight.shape[1]
    tile_count = half_hidden // TILE
    split = tile_count - tile_count // 2
    tile_parts = [(0, split), (split, tile_count - split)]

    def near_pair(rows):
        return rows, swap(rows, "example", 1)

    def run(tiles, far, own, after):
        return stage(offset, near_at, tiles, far, own, down_weight, weight_near, after)

    cuts = [cut(far_at, gathered[0], width, (up_sent,))]
    came, right = [], []
    gate_packed, up_packed, before = [], [], None
    after = ()
    for k in range(chunks):
        mine, away = cuts[k]
        far_pair = near_pair(swap(away, "example", 2))
        if k == 1:
            gate_packed = pack(starts, doubles, offset, place, gate_rows, gate_near, after=(away,))
            up_packed = pack(starts, doubles, offset, place, up_rows, up_near, after=(away,))
        if 0 < k < chunks - 1:
            order = (away, gate_packed[0], up_packed[0])
            cuts.append(cut(far_at, gathered[k + 1], width, order))
            after += (cuts[-1][0],)
        arrived, came = came, []
        for h, tiles in enumerate(tile_parts):
            own = None
            if k > 0:
                own = (*before, arrived[h], gate_packed[k - 1], up_packed[k - 1], proj_gate, proj_up)
            results = run(tiles, far_pair, own, after)
            after = (results[0],)
            came.append(swap(results[0], "example", 2))
            if k > 0:
                right.append(results[1])
        before = near_pair(mine)
        if k == 0:
            cuts.append(cut(far_at, gathered[1], width, after))
    last = after
    for h, tiles in enumerate(tile_parts):
        own = (*before, came[h], gate_packed[-1], up_packed[-1], proj_gate, proj_up)
        right += run(tiles, None, own, after)
        after = (right[-1],)
    right = jnp.concatenate([right[k] + right[k + 1] for k in range(0, 2 * chunks, 2)])

    inputs_rows = layer_input.reshape(row_total, width_local)
    gate_values = gate_pre.reshape(row_total, hidden_local).astype(jnp.float32)
    up_values = up_pre.reshape(row_total, hidden_local).astype(jnp.float32)
    hidden = (gate_values * jax.nn.sigmoid(gate_values) * up_values).astype(jnp.bfloat16)
    early = jnp.concatenate(
        [
            contract(inputs_rows, proj_input),
            contract(hidden, proj_hidden),
            contract(grad_rows, proj_output),
        ]
    )
    early = sum_over(ordered(early, last), "tensor")
    in_gate, in_down, out_down = (early[k * row_total : (k + 1) * row_total] for k in range(3))
    slots_here = jnp.concatenate(
        [
            take(rev_slot, example_at * ex_count, ex_count, 0),
            take(rev_slot, (example_at ^ 1) * ex_count, ex_count, 0),
        ]
    )
    table = pairing_table(slots_here, rev_pairs)
    mask = (positions[None, :] < own_lengths[:, None]).astype(jnp.float32).reshape(row_total)
    left_down = take(in_down, tensor_at * per_rank, per_rank, 1) * mask[:, None]
    sketch_down = jnp.einsum(
        "pe,eti,etj->pij",
        table[:, :ex_count],
        left_down.reshape(ex_count, slot_len, per_rank),
        out_down.reshape(ex_count, slot_len, rank_size),
        precision=lax.Precision.HIGHEST,
    )
    in_gate = jnp.concatenate([in_gate, swap(in_gate, "example", 1)])
    select = jnp.arange(capacity, dtype=jnp.int32)[:, None] == place
    in_gate = jnp.dot(select.astype(jnp.float32), in_gate, precision=lax.Precision.HIGHEST)
    table_rows = jnp.dot(
        select.astype(jnp.bfloat16), jnp.repeat(table, slot_len, axis=1).T.astype(jnp.bfloat16)
    )
    left = table_rows.astype(jnp.float32)[:, :, None] * in_gate[:, None, :]
    left = left.reshape(capacity, rev_pairs * rank_size)

    sketch_late = lax.dot_general(
        left, right, (((0,), (0,)), ((), ())), precision=lax.Precision.HIGHEST
    ).reshape(rev_pairs, rank_size, 2 * rank_size)
    return sketch_late, sketch_down


def local_four(
    layer_input,
    gate_pre,
    up_pre,
    output_grad,
    down_weight,
    proj_input,
    proj_hidden,
    proj_output,
    proj_gate,
    proj_up,
    query_sketches,
    rev_lengths,
    rev_slot,
    query_slot,
):
    ex_count, slot_len, width_local = layer_input.shape
    row_total = ex_count * slot_len
    grad_rows = output_grad.reshape(row_total, width_local)
    grad_near = swap(grad_rows, "example", 1)
    others = [swap(rev_lengths, "example", bits) for bits in (1, 2, 3)]
    sums = jnp.stack([jnp.sum(rev_lengths) + jnp.sum(others[0]), jnp.sum(others[1]) + jnp.sum(others[2])])
    most = jnp.max(sums).reshape(1)
    count = lax.axis_size("group")
    for step in range(1, count):
        shifted = lax.ppermute(most, "group", [(i, (i + step) % count) for i in range(count)])
        most = jnp.maximum(most, shifted)
    full = 2 * row_total
    levels = [level for level in LEVELS if level < full] + [full]
    branch = jnp.sum((most[0] > jnp.array(levels[:-1], jnp.int32)).astype(jnp.int32))
    sketch_late, sketch_down = lax.switch(
        branch,
        [functools.partial(packed_scores, level) for level in levels],
        (
            layer_input,
            gate_pre,
            up_pre,
            grad_rows,
            grad_near,
            down_weight,
            proj_input,
            proj_hidden,
            proj_output,
            proj_gate,
            proj_up,
            rev_slot,
            rev_lengths,
            others[0],
        ),
    )
    rank_size = proj_input.shape[0]
    rev_pairs = rev_slot.shape[0] // 2
    sketch_late = scatter_over(sketch_late, "tensor", 1)
    revision_pairs = sum_over(jnp.concatenate([sketch_late, sketch_down], axis=2), "example")
    example_scores = contract_exact(
        revision_pairs.reshape(rev_pairs, -1), query_sketches.astype(jnp.float32)
    )
    query_pairs = query_slot.shape[0] * 4 // 2
    pair_terms = contract_exact(example_scores, pairing_table(query_slot, query_pairs))
    total = sum_over(scatter_over(pair_terms, "example", 1), "tensor")
    return total / jnp.float32(rank_size * rank_size)


def local_any(
    layer_input,
    gate_pre,
    up_pre,
    output_grad,
    down_weight,
    proj_input,
    proj_hidden,
    proj_output,
    proj_gate,
    proj_up,
    query_sketches,
    rev_lengths,
    rev_slot,
    query_slot,
):
    ex_count, slot_len, width_local = layer_input.shape
    hidden_local = gate_pre.shape[2]
    row_total = ex_count * slot_len
    rank_size = proj_input.shape[0]
    per_rank = rank_size // lax.axis_size("tensor")
    inputs_rows = layer_input.reshape(row_total, width_local)
    grad_rows = output_grad.reshape(row_total, width_local)
    gate_values = gate_pre.reshape(row_total, hidden_local).astype(jnp.float32)
    up_values = up_pre.reshape(row_total, hidden_local).astype(jnp.float32)
    grad_full = lax.all_gather(grad_rows, "tensor", axis=1, tiled=True)
    hidden_grad = contract(grad_full, lax.all_gather(down_weight, "example", axis=1, tiled=True))
    hidden_grad = lax.optimization_barrier(hidden_grad.astype(jnp.bfloat16)).astype(jnp.float32)
    sigma = jax.nn.sigmoid(gate_values)
    active = gate_values * sigma
    hidden = (active * up_values).astype(jnp.bfloat16)
    grad_up = (hidden_grad * active).astype(jnp.bfloat16)
    grad_gate = (hidden_grad * up_values * sigma * (1.0 + gate_values * (1.0 - sigma))).astype(
        jnp.bfloat16
    )
    partials = jnp.stack(
        [
            contract(inputs_rows, proj_input),
            contract(hidden, proj_hidden),
            contract(grad_gate, proj_gate),
            contract(grad_up, proj_up),
            contract(grad_rows, proj_output),
        ]
    )
    summed = lax.psum(partials, "tensor")
    begin = lax.axis_index("tensor") * per_rank
    left = lax.dynamic_slice_in_dim(summed[:2], begin, per_rank, 2)
    right = summed[2:]
    positions = jnp.arange(slot_len, dtype=jnp.int32)
    mask = (positions[None, :] < rev_lengths[:, None]).astype(jnp.float32).reshape(row_total)
    left = left * mask[None, :, None]
    left = jnp.stack([left[0], left[0], left[1]]).reshape(3, ex_count, slot_len, per_rank)
    right = right.reshape(3, ex_count, slot_len, rank_size)
    sketches = jnp.einsum("meti,metj->eimj", left, right, precision=lax.Precision.HIGHEST).reshape(
        ex_count, per_rank * 3 * rank_size
    )
    every_sketch = lax.all_gather(sketches, "example", axis=0, tiled=True)
    rev_pairs = rev_slot.shape[0] // 2
    revision_pairs = jnp.dot(
        pairing_table(rev_slot, rev_pairs), every_sketch, precision=lax.Precision.HIGHEST
    )
    example_scores = contract_exact(revision_pairs, query_sketches.astype(jnp.float32))
    query_pairs = query_slot.shape[0] * lax.axis_size("example") // 2
    pair_terms = contract_exact(example_scores, pairing_table(query_slot, query_pairs))
    owned = lax.psum_scatter(pair_terms, "example", scatter_dimension=1, tiled=True)
    total = lax.psum(owned, "tensor")
    return total / jnp.float32(rank_size * rank_size)


def solution(mesh):
    four = mesh.shape["tensor"] == 4 and mesh.shape["example"] == 4
    return jax.shard_map(
        local_four if four else local_any,
        mesh=mesh,
        in_specs=(
            P(("group", "example"), None, "tensor"),
            P(("group", "example"), None, "tensor"),
            P(("group", "example"), None, "tensor"),
            P(("group", "example"), None, "tensor"),
            P("tensor", "example"),
            P(None, "tensor"),
            P(None, "tensor"),
            P(None, "tensor"),
            P(None, "tensor"),
            P(None, "tensor"),
            P(("group", "example"), "tensor"),
            P(("group", "example")),
            P("group"),
            P(("group", "example")),
        ),
        out_specs=P("group", "example"),
        check_vma=False,
    )
```

```python
import functools

import jax
import jax.numpy as jnp
from jax import lax
from jax.experimental import pallas as pl
from jax.experimental.pallas import tpu as pltpu
from jax.sharding import PartitionSpec as P

LEVELS = (768,)
TILE = 512
STEP = 256
LANES = 128
VMEM_LIMIT = 58 * 1024 * 1024


def contract(left_side, right_side):
    return lax.dot_general(
        left_side, right_side, (((1,), (1,)), ((), ())), preferred_element_type=jnp.float32
    )


def contract_exact(left_side, right_side):
    return lax.dot_general(
        left_side,
        right_side,
        (((1,), (1,)), ((), ())),
        precision=lax.Precision.HIGHEST,
        preferred_element_type=jnp.float32,
    )


def pairing_table(slots, pairs):
    pair_index = slots // 2
    signs = (1 - 2 * (slots % 2)).astype(jnp.float32)
    targets = jnp.arange(pairs, dtype=jnp.int32)
    return jnp.where(targets[:, None] == pair_index[None, :], signs[None, :], jnp.float32(0.0))


def take(array, start, size, axis):
    return lax.dynamic_slice_in_dim(array, start, size, axis)


def swap(array, axis, bits):
    count = lax.axis_size(axis)
    return lax.ppermute(array, axis, [(i, i ^ bits) for i in range(count)])


def kernel_params():
    return pltpu.CompilerParams(vmem_limit_bytes=VMEM_LIMIT)


def pack_kernel(size, count, near_ref, place_ref, own_ref, other_ref, *refs):
    outs, select = refs[-1 - count : -1], refs[-1]
    rows_own = own_ref.shape[0]

    @pl.when(pl.program_id(0) == 0)
    def _():
        @pl.loop(0, count)
        def _(c):
            at = lax.broadcasted_iota(jnp.int32, (size, select.shape[1]), 0) + c * 2 * LANES
            chosen = jnp.where(at == place_ref[...], 1.0, 0.0).astype(jnp.bfloat16)
            select[pl.ds(pl.multiple_of(c * size, size), size), :] = chosen

    for c in range(count):
        rows = slice(c * size, (c + 1) * size)
        total = jnp.dot(select[rows, :rows_own], own_ref[...], preferred_element_type=jnp.float32)
        total += jnp.dot(select[rows, rows_own:], other_ref[...], preferred_element_type=jnp.float32)
        outs[c][...] = total.astype(jnp.bfloat16).T


def pack(count, size, near_offset, place, own, other, after=()):
    rows, columns = other.shape
    total = count * size
    return pl.pallas_call(
        functools.partial(pack_kernel, size, count),
        grid_spec=pltpu.PrefetchScalarGridSpec(
            num_scalar_prefetch=1,
            grid=(columns // TILE,),
            in_specs=[
                pl.BlockSpec((1, 2 * rows), lambda i, near: (0, 0)),
                pl.BlockSpec((rows, TILE), lambda i, near: (0, near[0] + i)),
                pl.BlockSpec((rows, TILE), lambda i, near: (0, i)),
            ]
            + [pl.BlockSpec(memory_space=pl.ANY)] * len(after),
            out_specs=[pl.BlockSpec((TILE, size), lambda i, near: (i, 0))] * count,
            scratch_shapes=[pltpu.VMEM((total, 2 * rows), jnp.bfloat16)],
        ),
        out_shape=[jax.ShapeDtypeStruct((columns, size), jnp.bfloat16)] * count,
        compiler_params=kernel_params(),
        cost_estimate=pl.CostEstimate(
            flops=4 * total * rows * columns,
            bytes_accessed=(4 * rows + 2 * total) * columns,
            transcendentals=0,
        ),
        name="pack_rows",
    )(near_offset, place, own, other, *after)


def cut_kernel(at_ref, source, *refs):
    out, sems = refs[-2:]
    rows = out.shape[0] // 4
    copies = []
    for k in range(4):
        begin = pl.multiple_of(at_ref[0] * out.shape[0] + k * rows, rows)
        copies.append(
            pltpu.make_async_copy(source.at[pl.ds(begin, rows), :], out.at[pl.ds(k * rows, rows), :], sems.at[k])
        )
    for copy in copies:
        copy.start()
    for copy in copies:
        copy.wait()


def cut(at, gathered, after):
    columns, rows = gathered.shape
    return pl.pallas_call(
        cut_kernel,
        in_specs=[pl.BlockSpec(memory_space=pltpu.SMEM)]
        + [pl.BlockSpec(memory_space=pl.ANY)] * (1 + len(after)),
        out_specs=pl.BlockSpec(memory_space=pl.ANY),
        scratch_shapes=[pltpu.SemaphoreType.DMA((4,))],
        out_shape=jax.ShapeDtypeStruct((columns // 2, rows), gathered.dtype),
        compiler_params=kernel_params(),
        cost_estimate=pl.CostEstimate(flops=0, bytes_accessed=2 * columns * rows, transcendentals=0),
        name="cut_columns",
    )(at, gathered, *after)


def gate_kernel(value, *refs):
    refs[-1][...] = value[...]


def ordered(value, after):
    return pl.pallas_call(
        gate_kernel,
        in_specs=[pl.BlockSpec(memory_space=pltpu.VMEM)]
        + [pl.BlockSpec(memory_space=pl.ANY)] * len(after),
        out_specs=pl.BlockSpec(memory_space=pltpu.VMEM),
        out_shape=jax.ShapeDtypeStruct(value.shape, value.dtype),
        compiler_params=kernel_params(),
        name="ordered_copy",
    )(value, *after)


def stage_kernel(far, own, offset_ref, near_ref, *refs):
    refs = list(refs)
    weights = [refs.pop(0) for _ in range(4)]
    far_ins = [refs.pop(0) for _ in range(4 * far)]
    own_ins = [refs.pop(0) for _ in range(4 * own)]
    extra = [refs.pop(0) for _ in range(5 * own)]
    own_right = refs.pop() if own else None
    far_right = refs.pop() if far else None
    out = refs.pop() if own else None
    far_out = refs.pop() if far else None
    depth = weights[0].shape[1]
    width = 2 * depth

    def join(ins, right):
        for side in range(2):
            for k in range(2):
                right[side * width : (side + 1) * width, k * LANES : (k + 1) * LANES] = ins[2 * side + k][...]

    def half_sum(rows, right):
        total = 0.0
        for k in range(4):
            block = right[k * depth : (k + 1) * depth, :]
            total += jnp.dot(weights[k][rows, :], block, preferred_element_type=jnp.float32)
        return total

    @pl.when(pl.program_id(0) == 0)
    def _():
        if far:
            join(far_ins, far_right)
        if own:
            join(own_ins, own_right)
            out[...] = jnp.zeros_like(out)

    @pl.loop(0, TILE // STEP)
    def _(r):
        rows = pl.ds(pl.multiple_of(r * STEP, STEP), STEP)
        if far:
            far_out[rows, :] = half_sum(rows, far_right).astype(jnp.bfloat16)
        if own:
            came, gate_ref, up_ref, proj_gate, proj_up = extra
            rank_size = proj_gate.shape[0]
            total = half_sum(rows, own_right)
            hidden_grad = (total + came[rows, :].astype(jnp.float32)).astype(jnp.bfloat16)
            hidden_grad = hidden_grad.astype(jnp.float32)
            gate = gate_ref[rows, :].astype(jnp.float32)
            up = up_ref[rows, :].astype(jnp.float32)
            sigma = jax.nn.sigmoid(gate)
            grad_up = (hidden_grad * (gate * sigma)).astype(jnp.bfloat16)
            grad_gate = (hidden_grad * up * sigma * (1.0 + gate * (1.0 - sigma))).astype(jnp.bfloat16)
            out[:rank_size, :] += jnp.dot(proj_gate[:, rows], grad_gate, preferred_element_type=jnp.float32)
            out[rank_size:, :] += jnp.dot(proj_up[:, rows], grad_up, preferred_element_type=jnp.float32)


def stage(near_offset, near, tiles, far, own, weight, weight_near, after):
    hidden, width = weight_near.shape
    begin, count = tiles
    depth = width // 2
    both = 2 * LANES
    arrays, specs, outs, shapes, rights = [], [], [], [], []

    def add(array, block, index):
        arrays.append(array)
        specs.append(pl.BlockSpec(block, index))

    for k in range(2):
        add(weight, (TILE, depth), lambda i, offset, near, k=k: (offset[0] + begin + i, k))
    for k in range(2):
        add(weight_near, (TILE, depth), lambda i, offset, near, k=k: (begin + i, k))
    for rows in (far, own):
        if rows is not None:
            rights.append(pltpu.VMEM((2 * width, both), jnp.bfloat16))
            for k in range(4):
                side = k // 2
                add(
                    rows[k % 2],
                    (width, LANES),
                    lambda i, offset, near, side=side: (near[0] + side * (1 - 2 * near[0]), 0),
                )
    if far is not None:
        outs.append(pl.BlockSpec((TILE, both), lambda i, offset, near: (i, 0)))
        shapes.append(jax.ShapeDtypeStruct((count * TILE, both), jnp.bfloat16))
    if own is not None:
        (came, first), gate, up, proj_gate, proj_up = own[2:]
        rank_size = proj_gate.shape[0]
        add(came, (TILE, both), lambda i, offset, near: (begin - first + i, 0))
        for array in (gate, up):
            add(array, (TILE, both), lambda i, offset, near: (begin + i, 0))
        for array in (proj_gate, proj_up):
            add(array, (rank_size, TILE), lambda i, offset, near: (0, offset[0] + begin + i))
        outs.append(pl.BlockSpec((2 * rank_size, both), lambda i, offset, near: (0, 0)))
        shapes.append(jax.ShapeDtypeStruct((2 * rank_size, both), jnp.float32))
    parts = len(rights)
    return pl.pallas_call(
        functools.partial(stage_kernel, far is not None, own is not None),
        grid_spec=pltpu.PrefetchScalarGridSpec(
            num_scalar_prefetch=2,
            grid=(count,),
            in_specs=specs + [pl.BlockSpec(memory_space=pl.ANY)] * len(after),
            out_specs=outs,
            scratch_shapes=rights,
        ),
        out_shape=shapes,
        compiler_params=kernel_params(),
        cost_estimate=pl.CostEstimate(
            flops=4 * parts * both * width * count * TILE,
            bytes_accessed=4 * width * count * TILE + 4 * parts * both * count * TILE,
            transcendentals=0,
        ),
        name="stage",
    )(near_offset, near, *arrays, *after)


def copy_kernel(at_ref, value, *refs):
    refs[-1][...] = value[...]


def copy_half(array, at, axis, after):
    rows, columns = array.shape
    steps = 7
    if axis == 0:
        rows //= 2
        block = (rows // steps, columns)
        source, goal = (lambda i, at: (at[0] * steps + i, 0)), (lambda i, at: (i, 0))
    else:
        columns //= 2
        block = (rows, columns // steps)
        source, goal = (lambda i, at: (0, at[0] * steps + i)), (lambda i, at: (0, i))
    return pl.pallas_call(
        copy_kernel,
        grid_spec=pltpu.PrefetchScalarGridSpec(
            num_scalar_prefetch=1,
            grid=(steps,),
            in_specs=[pl.BlockSpec(block, source)] + [pl.BlockSpec(memory_space=pl.ANY)] * len(after),
            out_specs=pl.BlockSpec(block, goal),
        ),
        out_shape=jax.ShapeDtypeStruct((rows, columns), array.dtype),
        compiler_params=kernel_params(),
        cost_estimate=pl.CostEstimate(flops=0, bytes_accessed=4 * rows * columns, transcendentals=0),
        name="copy_half",
    )(at, array, *after)


def sum_over(array, axis):
    parts = [swap(array, axis, bits) for bits in (1, 2, 3)]
    return (array + parts[0]) + (parts[1] + parts[2])


def scatter_over(array, axis, dim):
    at = lax.axis_index(axis)
    size = array.shape[dim] // 4
    parts = [swap(take(array, (at ^ bits) * size, size, dim), axis, bits) for bits in (1, 2, 3)]
    return (take(array, at * size, size, dim) + parts[0]) + (parts[1] + parts[2])


def packed_scores(capacity, args):
    (
        layer_input,
        gate_pre,
        up_pre,
        grad_rows,
        grad_near,
        down_weight,
        weight_sent,
        proj_input,
        proj_hidden,
        proj_output,
        proj_gate,
        proj_up,
        rev_slot,
        own_lengths,
        near_lengths,
    ) = args
    ex_count, slot_len, width_local = layer_input.shape
    hidden_local = gate_pre.shape[2]
    row_total = ex_count * slot_len
    rank_size = proj_input.shape[0]
    rev_pairs = rev_slot.shape[0] // 2
    example_at = lax.axis_index("example")
    tensor_at = lax.axis_index("tensor")
    near, far = example_at % 2, example_at // 2
    half_hidden = hidden_local // 2
    half_rows = capacity // 2
    chunks = half_rows // LANES
    offset = (near * (half_hidden // TILE)).astype(jnp.int32).reshape(1)
    no_offset = jnp.zeros((1,), jnp.int32)

    both_lengths = jnp.concatenate([own_lengths, near_lengths])
    own_begin = near * jnp.sum(near_lengths)
    near_begin = (1 - near) * jnp.sum(own_lengths)
    offsets = jnp.concatenate(
        [
            own_begin + jnp.cumsum(own_lengths) - own_lengths,
            near_begin + jnp.cumsum(near_lengths) - near_lengths,
        ]
    )
    positions = jnp.arange(slot_len, dtype=jnp.int32)
    place = offsets[:, None] + positions[None, :] - near * half_rows
    place = jnp.where(place < 0, place + capacity, place)
    other_half = place >= half_rows
    at = jnp.where(other_half, place - half_rows, place)
    place = at + (at // LANES) * LANES + jnp.where(other_half, LANES, 0)
    place = jnp.where(positions[None, :] < both_lengths[:, None], place, -1).reshape(1, 2 * row_total)

    blocks = pack(chunks, LANES, no_offset, place, grad_rows, grad_near)
    gathered = [lax.all_gather(blocks[k], "tensor", axis=0, tiled=True) for k in range(chunks)]
    near_at, far_at = near.astype(jnp.int32).reshape(1), far.astype(jnp.int32).reshape(1)
    weight_near = swap(weight_sent, "example", 1)

    tile_count = half_hidden // TILE
    split = tile_count - tile_count // 2
    tile_parts = [(0, split), (split, tile_count - split)]

    def near_pair(rows):
        return rows, swap(rows, "example", 1)

    def run(tiles, far, own, after):
        return stage(offset, near_at, tiles, far, own, down_weight, weight_near, after)

    gate_rows = gate_pre.reshape(row_total, hidden_local)
    up_rows = up_pre.reshape(row_total, hidden_local)
    away = cut(1 - far_at, gathered[0], ())
    gate_sent = copy_half(gate_rows, 1 - near_at, 1, (away,))
    up_sent = copy_half(up_rows, 1 - near_at, 1, (gate_sent,))
    mine = cut(far_at, gathered[0], (up_sent,))
    gate_near = swap(gate_sent, "example", 1)
    up_near = swap(up_sent, "example", 1)
    far_pair = near_pair(swap(away, "example", 2))
    came, right, after = [], [], ()
    for tiles in tile_parts:
        results = run(tiles, far_pair, None, after)
        came.append((swap(results[0], "example", 2), tiles[0]))
        after = (results[0],)
    for k in range(1, chunks):
        before = near_pair(mine)
        if k == 1:
            away = cut(1 - far_at, gathered[1], after)
            mine = cut(far_at, gathered[1], (away,))
            far_pair = near_pair(swap(away, "example", 2))
            gate_packed = pack(chunks, 2 * LANES, offset, place, gate_rows, gate_near, after=(away,))
            up_packed = pack(chunks, 2 * LANES, offset, place, up_rows, up_near, after=(away,))
            after = (gate_packed[0], up_packed[0])
        else:
            away, mine = next_away, next_mine
            far_pair = near_pair(ordered(far_next, after))
        if k + 1 < chunks:
            next_away = cut(1 - far_at, gathered[k + 1], after)
            next_mine = cut(far_at, gathered[k + 1], (next_away,))
            far_next = swap(next_away, "example", 2)
            after += (next_away,)
            if k == 1:
                middle = (next_mine,)
        arrived, came = came, []
        for h, tiles in enumerate(tile_parts):
            own = (*before, arrived[h], gate_packed[k - 1], up_packed[k - 1])
            results = run(tiles, far_pair, (*own, proj_gate, proj_up), after)
            after = (results[0],)
            came.append((swap(results[0], "example", 2), tiles[0]))
            right.append(results[1])
    before = near_pair(mine)
    for h, tiles in enumerate(tile_parts):
        own = (*before, came[h], gate_packed[-1], up_packed[-1], proj_gate, proj_up)
        right += run(tiles, None, own, after)
        after = (right[-1],)
    right = jnp.concatenate([right[k] + right[k + 1] for k in range(0, 2 * chunks, 2)], axis=1)

    inputs_rows = layer_input.reshape(row_total, width_local)
    gate_values = gate_pre.reshape(row_total, hidden_local).astype(jnp.float32)
    up_values = up_pre.reshape(row_total, hidden_local).astype(jnp.float32)
    hidden = (gate_values * jax.nn.sigmoid(gate_values) * up_values).astype(jnp.bfloat16)
    early = jnp.concatenate(
        [
            contract(proj_input, inputs_rows),
            contract(proj_hidden, hidden),
            contract(proj_output, grad_rows),
        ]
    )
    early = scatter_over(ordered(early, middle), "tensor", 1)
    in_gate, in_down, out_down = (early[k * rank_size : (k + 1) * rank_size] for k in range(3))
    in_gate = jnp.stack([in_gate] + [swap(in_gate, "tensor", bits) for bits in (1, 2, 3)])
    in_gate = jnp.concatenate([take(in_gate, tensor_at ^ t, 1, 0)[0] for t in range(4)], axis=1)
    in_gate = jnp.concatenate([in_gate, swap(in_gate, "example", 1)], axis=1)
    slots_here = jnp.concatenate(
        [
            take(rev_slot, example_at * ex_count, ex_count, 0),
            take(rev_slot, (example_at ^ 1) * ex_count, ex_count, 0),
        ]
    )
    table = pairing_table(slots_here, rev_pairs)
    mask = (positions < take(own_lengths, tensor_at, 1, 0)).astype(jnp.float32)
    sketch_down = contract_exact(in_down * mask[None, :], out_down)
    sketch_down = take(table, tensor_at, 1, 1)[:, :, None] * sketch_down[None, :, :]
    select = jnp.arange(capacity, dtype=jnp.int32)[:, None] == place
    in_gate = contract_exact(in_gate, select.astype(jnp.float32))
    table_rows = contract(
        jnp.repeat(table, slot_len, axis=1).astype(jnp.bfloat16), select.astype(jnp.bfloat16)
    )
    left = (table_rows[:, None, :] * in_gate[None, :, :]).reshape(rev_pairs * rank_size, capacity)
    sketch_late = contract_exact(left, right).reshape(rev_pairs, rank_size, 2 * rank_size)
    return jnp.concatenate([sketch_late, sketch_down], axis=2)


def local_four(
    layer_input,
    gate_pre,
    up_pre,
    output_grad,
    down_weight,
    proj_input,
    proj_hidden,
    proj_output,
    proj_gate,
    proj_up,
    query_sketches,
    rev_lengths,
    rev_slot,
    query_slot,
):
    ex_count, slot_len, width_local = layer_input.shape
    row_total = ex_count * slot_len
    grad_rows = output_grad.reshape(row_total, width_local)
    grad_near = swap(grad_rows, "example", 1)
    near_at = (lax.axis_index("example") % 2).astype(jnp.int32).reshape(1)
    weight_sent = copy_half(down_weight, 1 - near_at, 0, ())
    others = [swap(rev_lengths, "example", bits) for bits in (1, 2, 3)]
    sums = jnp.stack([jnp.sum(rev_lengths) + jnp.sum(others[0]), jnp.sum(others[1]) + jnp.sum(others[2])])
    most = jnp.max(sums).reshape(1)
    count = lax.axis_size("group")
    for step in range(1, count):
        shifted = lax.ppermute(most, "group", [(i, (i + step) % count) for i in range(count)])
        most = jnp.maximum(most, shifted)
    full = 2 * row_total
    levels = [level for level in LEVELS if level < full] + [full]
    branch = jnp.sum((most[0] > jnp.array(levels[:-1], jnp.int32)).astype(jnp.int32))
    sketch = lax.switch(
        branch,
        [functools.partial(packed_scores, level) for level in levels],
        (
            layer_input,
            gate_pre,
            up_pre,
            grad_rows,
            grad_near,
            down_weight,
            weight_sent,
            proj_input,
            proj_hidden,
            proj_output,
            proj_gate,
            proj_up,
            rev_slot,
            rev_lengths,
            others[0],
        ),
    )
    rank_size = proj_input.shape[0]
    rev_pairs = rev_slot.shape[0] // 2
    revision_pairs = sum_over(scatter_over(sketch, "tensor", 1), "example")
    example_scores = contract_exact(
        revision_pairs.reshape(rev_pairs, -1), query_sketches.astype(jnp.float32)
    )
    query_pairs = query_slot.shape[0] * 4 // 2
    pair_terms = contract_exact(example_scores, pairing_table(query_slot, query_pairs))
    total = sum_over(scatter_over(pair_terms, "example", 1), "tensor")
    return total / jnp.float32(rank_size * rank_size)


def local_any(
    layer_input,
    gate_pre,
    up_pre,
    output_grad,
    down_weight,
    proj_input,
    proj_hidden,
    proj_output,
    proj_gate,
    proj_up,
    query_sketches,
    rev_lengths,
    rev_slot,
    query_slot,
):
    ex_count, slot_len, width_local = layer_input.shape
    hidden_local = gate_pre.shape[2]
    row_total = ex_count * slot_len
    rank_size = proj_input.shape[0]
    per_rank = rank_size // lax.axis_size("tensor")
    inputs_rows = layer_input.reshape(row_total, width_local)
    grad_rows = output_grad.reshape(row_total, width_local)
    gate_values = gate_pre.reshape(row_total, hidden_local).astype(jnp.float32)
    up_values = up_pre.reshape(row_total, hidden_local).astype(jnp.float32)
    grad_full = lax.all_gather(grad_rows, "tensor", axis=1, tiled=True)
    hidden_grad = contract(grad_full, lax.all_gather(down_weight, "example", axis=1, tiled=True))
    hidden_grad = lax.optimization_barrier(hidden_grad.astype(jnp.bfloat16)).astype(jnp.float32)
    sigma = jax.nn.sigmoid(gate_values)
    active = gate_values * sigma
    hidden = (active * up_values).astype(jnp.bfloat16)
    grad_up = (hidden_grad * active).astype(jnp.bfloat16)
    grad_gate = (hidden_grad * up_values * sigma * (1.0 + gate_values * (1.0 - sigma))).astype(
        jnp.bfloat16
    )
    partials = jnp.stack(
        [
            contract(inputs_rows, proj_input),
            contract(hidden, proj_hidden),
            contract(grad_gate, proj_gate),
            contract(grad_up, proj_up),
            contract(grad_rows, proj_output),
        ]
    )
    summed = lax.psum(partials, "tensor")
    begin = lax.axis_index("tensor") * per_rank
    left = lax.dynamic_slice_in_dim(summed[:2], begin, per_rank, 2)
    right = summed[2:]
    positions = jnp.arange(slot_len, dtype=jnp.int32)
    mask = (positions[None, :] < rev_lengths[:, None]).astype(jnp.float32).reshape(row_total)
    left = left * mask[None, :, None]
    left = jnp.stack([left[0], left[0], left[1]]).reshape(3, ex_count, slot_len, per_rank)
    right = right.reshape(3, ex_count, slot_len, rank_size)
    sketches = jnp.einsum("meti,metj->eimj", left, right, precision=lax.Precision.HIGHEST).reshape(
        ex_count, per_rank * 3 * rank_size
    )
    every_sketch = lax.all_gather(sketches, "example", axis=0, tiled=True)
    rev_pairs = rev_slot.shape[0] // 2
    revision_pairs = jnp.dot(
        pairing_table(rev_slot, rev_pairs), every_sketch, precision=lax.Precision.HIGHEST
    )
    example_scores = contract_exact(revision_pairs, query_sketches.astype(jnp.float32))
    query_pairs = query_slot.shape[0] * lax.axis_size("example") // 2
    pair_terms = contract_exact(example_scores, pairing_table(query_slot, query_pairs))
    owned = lax.psum_scatter(pair_terms, "example", scatter_dimension=1, tiled=True)
    total = lax.psum(owned, "tensor")
    return total / jnp.float32(rank_size * rank_size)


def solution(mesh):
    four = mesh.shape["tensor"] == 4 and mesh.shape["example"] == 4
    return jax.shard_map(
        local_four if four else local_any,
        mesh=mesh,
        in_specs=(
            P(("group", "example"), None, "tensor"),
            P(("group", "example"), None, "tensor"),
            P(("group", "example"), None, "tensor"),
            P(("group", "example"), None, "tensor"),
            P("tensor", "example"),
            P(None, "tensor"),
            P(None, "tensor"),
            P(None, "tensor"),
            P(None, "tensor"),
            P(None, "tensor"),
            P(("group", "example"), "tensor"),
            P(("group", "example")),
            P("group"),
            P(("group", "example")),
        ),
        out_specs=P("group", "example"),
        check_vma=False,
    )
```

```python
import functools

import jax
import jax.numpy as jnp
from jax import lax
from jax.experimental import pallas as pl
from jax.experimental.pallas import tpu as pltpu
from jax.sharding import PartitionSpec as P

LEVELS = (768,)
TILE = 512
STEP = 256
LANES = 128
VMEM_LIMIT = 58 * 1024 * 1024


def contract(left_side, right_side):
    return lax.dot_general(
        left_side, right_side, (((1,), (1,)), ((), ())), preferred_element_type=jnp.float32
    )


def contract_exact(left_side, right_side):
    return lax.dot_general(
        left_side,
        right_side,
        (((1,), (1,)), ((), ())),
        precision=lax.Precision.HIGHEST,
        preferred_element_type=jnp.float32,
    )


def pairing_table(slots, pairs):
    pair_index = slots // 2
    signs = (1 - 2 * (slots % 2)).astype(jnp.float32)
    targets = jnp.arange(pairs, dtype=jnp.int32)
    return jnp.where(targets[:, None] == pair_index[None, :], signs[None, :], jnp.float32(0.0))


def take(array, start, size, axis):
    return lax.dynamic_slice_in_dim(array, start, size, axis)


def swap(array, axis, bits):
    count = lax.axis_size(axis)
    return lax.ppermute(array, axis, [(i, i ^ bits) for i in range(count)])


def kernel_params():
    return pltpu.CompilerParams(vmem_limit_bytes=VMEM_LIMIT)


def pack_kernel(size, count, near_ref, place_ref, own_ref, other_ref, *refs):
    outs, select = refs[-1 - count : -1], refs[-1]
    rows_own = own_ref.shape[0]

    @pl.when(pl.program_id(0) == 0)
    def _():
        @pl.loop(0, count)
        def _(c):
            at = lax.broadcasted_iota(jnp.int32, (size, select.shape[1]), 0) + c * 2 * LANES
            chosen = jnp.where(at == place_ref[...], 1.0, 0.0).astype(jnp.bfloat16)
            select[pl.ds(pl.multiple_of(c * size, size), size), :] = chosen

    for c in range(count):
        rows = slice(c * size, (c + 1) * size)
        total = jnp.dot(select[rows, :rows_own], own_ref[...], preferred_element_type=jnp.float32)
        total += jnp.dot(select[rows, rows_own:], other_ref[...], preferred_element_type=jnp.float32)
        outs[c][...] = total.astype(jnp.bfloat16).T


def pack(count, size, columns, near_offset, place, own, other, after=()):
    rows = own.shape[0]
    total = count * size
    return pl.pallas_call(
        functools.partial(pack_kernel, size, count),
        grid_spec=pltpu.PrefetchScalarGridSpec(
            num_scalar_prefetch=1,
            grid=(columns // TILE,),
            in_specs=[
                pl.BlockSpec((1, 2 * rows), lambda i, near: (0, 0)),
                pl.BlockSpec((rows, TILE), lambda i, near: (0, near[0] + i)),
                pl.BlockSpec((rows, TILE), lambda i, near: (0, near[0] + i)),
            ]
            + [pl.BlockSpec(memory_space=pl.ANY)] * len(after),
            out_specs=[pl.BlockSpec((TILE, size), lambda i, near: (i, 0))] * count,
            scratch_shapes=[pltpu.VMEM((total, 2 * rows), jnp.bfloat16)],
        ),
        out_shape=[jax.ShapeDtypeStruct((columns, size), jnp.bfloat16)] * count,
        compiler_params=kernel_params(),
        cost_estimate=pl.CostEstimate(
            flops=4 * total * rows * columns,
            bytes_accessed=(4 * rows + 2 * total) * columns,
            transcendentals=0,
        ),
        name="pack_rows",
    )(near_offset, place, own, other, *after)


def cut_kernel(at_ref, source, *refs):
    refs[-1][...] = source[...]


def cut(at, gathered, after):
    columns, rows = gathered.shape
    block = columns // 8
    return pl.pallas_call(
        cut_kernel,
        grid_spec=pltpu.PrefetchScalarGridSpec(
            num_scalar_prefetch=1,
            grid=(4,),
            in_specs=[pl.BlockSpec((block, rows), lambda i, at: (4 * at[0] + i, 0))]
            + [pl.BlockSpec(memory_space=pl.ANY)] * len(after),
            out_specs=pl.BlockSpec((block, rows), lambda i, at: (i, 0)),
        ),
        out_shape=jax.ShapeDtypeStruct((columns // 2, rows), gathered.dtype),
        compiler_params=kernel_params(),
        cost_estimate=pl.CostEstimate(flops=0, bytes_accessed=2 * columns * rows, transcendentals=0),
        name="cut_columns",
    )(at, gathered, *after)


def gate_kernel(value, *refs):
    refs[-1][...] = value[...]


def ordered(value, after):
    return pl.pallas_call(
        gate_kernel,
        in_specs=[pl.BlockSpec(memory_space=pltpu.VMEM)]
        + [pl.BlockSpec(memory_space=pl.ANY)] * len(after),
        out_specs=pl.BlockSpec(memory_space=pltpu.VMEM),
        out_shape=jax.ShapeDtypeStruct(value.shape, value.dtype),
        compiler_params=kernel_params(),
        name="ordered_copy",
    )(value, *after)


def stage_kernel(far, own, offset_ref, near_ref, *refs):
    refs = list(refs)
    weights = [refs.pop(0) for _ in range(4)]
    far_ins = [refs.pop(0) for _ in range(4 * far)]
    own_ins = [refs.pop(0) for _ in range(4 * own)]
    extra = [refs.pop(0) for _ in range(5 * own)]
    own_right = refs.pop() if own else None
    far_right = refs.pop() if far else None
    out = refs.pop() if own else None
    far_out = refs.pop() if far else None
    depth = weights[0].shape[1]
    width = 2 * depth

    def join(ins, right):
        for side in range(2):
            for k in range(2):
                right[side * width : (side + 1) * width, k * LANES : (k + 1) * LANES] = ins[2 * side + k][...]

    def half_sum(rows, right):
        total = 0.0
        for k in range(4):
            block = right[k * depth : (k + 1) * depth, :]
            total += jnp.dot(weights[k][rows, :], block, preferred_element_type=jnp.float32)
        return total

    @pl.when(pl.program_id(0) == 0)
    def _():
        if far:
            join(far_ins, far_right)
        if own:
            join(own_ins, own_right)
            out[...] = jnp.zeros_like(out)

    @pl.loop(0, TILE // STEP)
    def _(r):
        rows = pl.ds(pl.multiple_of(r * STEP, STEP), STEP)
        if far:
            far_out[rows, :] = half_sum(rows, far_right).astype(jnp.bfloat16)
        if own:
            came, gate_ref, up_ref, proj_gate, proj_up = extra
            rank_size = proj_gate.shape[0]
            total = half_sum(rows, own_right)
            hidden_grad = (total + came[rows, :].astype(jnp.float32)).astype(jnp.bfloat16)
            hidden_grad = hidden_grad.astype(jnp.float32)
            gate = gate_ref[rows, :].astype(jnp.float32)
            up = up_ref[rows, :].astype(jnp.float32)
            sigma = jax.nn.sigmoid(gate)
            grad_up = (hidden_grad * (gate * sigma)).astype(jnp.bfloat16)
            grad_gate = (hidden_grad * up * sigma * (1.0 + gate * (1.0 - sigma))).astype(jnp.bfloat16)
            out[:rank_size, :] += jnp.dot(proj_gate[:, rows], grad_gate, preferred_element_type=jnp.float32)
            out[rank_size:, :] += jnp.dot(proj_up[:, rows], grad_up, preferred_element_type=jnp.float32)


def stage(near_offset, near, tiles, far, own, weight, weight_near, after):
    begin, count = tiles
    width = weight_near.shape[1]
    depth = width // 2
    both = 2 * LANES
    arrays, specs, outs, shapes, rights = [], [], [], [], []

    def add(array, block, index):
        arrays.append(array)
        specs.append(pl.BlockSpec(block, index))

    for k in range(2):
        add(weight, (TILE, depth), lambda i, offset, near, k=k: (offset[0] + begin + i, k))
    for k in range(2):
        add(weight_near, (TILE, depth), lambda i, offset, near, k=k: (offset[0] + begin + i, k))
    for rows, base in ((far, 0), (own, 2)):
        if rows is not None:
            rights.append(pltpu.VMEM((2 * width, both), jnp.bfloat16))
            for k in range(4):
                side = k // 2
                add(
                    rows[k % 2],
                    (width, LANES),
                    lambda i, offset, near, side=side, base=base: (
                        base * near[1] + near[0] + side * (1 - 2 * near[0]),
                        0,
                    ),
                )
    if far is not None:
        outs.append(pl.BlockSpec((TILE, both), lambda i, offset, near: (i, 0)))
        shapes.append(jax.ShapeDtypeStruct((count * TILE, both), jnp.bfloat16))
    if own is not None:
        (came, first), gate, up, proj_gate, proj_up = own[2:]
        rank_size = proj_gate.shape[0]
        add(came, (TILE, both), lambda i, offset, near: (begin - first + i, 0))
        for array in (gate, up):
            add(array, (TILE, both), lambda i, offset, near: (begin + i, 0))
        for array in (proj_gate, proj_up):
            add(array, (rank_size, TILE), lambda i, offset, near: (0, offset[0] + begin + i))
        outs.append(pl.BlockSpec((2 * rank_size, both), lambda i, offset, near: (0, 0)))
        shapes.append(jax.ShapeDtypeStruct((2 * rank_size, both), jnp.float32))
    parts = len(rights)
    return pl.pallas_call(
        functools.partial(stage_kernel, far is not None, own is not None),
        grid_spec=pltpu.PrefetchScalarGridSpec(
            num_scalar_prefetch=2,
            grid=(count,),
            in_specs=specs + [pl.BlockSpec(memory_space=pl.ANY)] * len(after),
            out_specs=outs,
            scratch_shapes=rights,
        ),
        out_shape=shapes,
        compiler_params=kernel_params(),
        cost_estimate=pl.CostEstimate(
            flops=4 * parts * both * width * count * TILE,
            bytes_accessed=4 * width * count * TILE + 4 * parts * both * count * TILE,
            transcendentals=0,
        ),
        name="stage",
    )(near_offset, near, *arrays, *after)


def sum_over(array, axis):
    parts = [swap(array, axis, bits) for bits in (1, 2, 3)]
    return (array + parts[0]) + (parts[1] + parts[2])


def scatter_over(array, axis, dim):
    at = lax.axis_index(axis)
    size = array.shape[dim] // 4
    parts = [swap(take(array, (at ^ bits) * size, size, dim), axis, bits) for bits in (1, 2, 3)]
    return (take(array, at * size, size, dim) + parts[0]) + (parts[1] + parts[2])


def packed_scores(capacity, args):
    (
        layer_input,
        gate_pre,
        up_pre,
        grad_rows,
        grad_near,
        down_weight,
        proj_input,
        proj_hidden,
        proj_output,
        proj_gate,
        proj_up,
        rev_slot,
        own_lengths,
        near_lengths,
    ) = args
    ex_count, slot_len, width_local = layer_input.shape
    hidden_local = gate_pre.shape[2]
    row_total = ex_count * slot_len
    rank_size = proj_input.shape[0]
    rev_pairs = rev_slot.shape[0] // 2
    example_at = lax.axis_index("example")
    tensor_at = lax.axis_index("tensor")
    near, far = example_at % 2, example_at // 2
    half_hidden = hidden_local // 2
    half_rows = capacity // 2
    chunks = half_rows // LANES
    offset = (near * (half_hidden // TILE)).astype(jnp.int32).reshape(1)
    no_offset = jnp.zeros((1,), jnp.int32)

    both_lengths = jnp.concatenate([own_lengths, near_lengths])
    own_begin = near * jnp.sum(near_lengths)
    near_begin = (1 - near) * jnp.sum(own_lengths)
    offsets = jnp.concatenate(
        [
            own_begin + jnp.cumsum(own_lengths) - own_lengths,
            near_begin + jnp.cumsum(near_lengths) - near_lengths,
        ]
    )
    positions = jnp.arange(slot_len, dtype=jnp.int32)
    place = offsets[:, None] + positions[None, :] - near * half_rows
    place = jnp.where(place < 0, place + capacity, place)
    other_half = place >= half_rows
    at = jnp.where(other_half, place - half_rows, place)
    place = at + (at // LANES) * LANES + jnp.where(other_half, LANES, 0)
    place = jnp.where(positions[None, :] < both_lengths[:, None], place, -1).reshape(1, 2 * row_total)

    blocks = pack(chunks, LANES, grad_rows.shape[1], no_offset, place, grad_rows, grad_near)
    gathered = [lax.all_gather(blocks[k], "tensor", axis=0, tiled=True) for k in range(chunks)]
    near_at, far_at = near.astype(jnp.int32).reshape(1), far.astype(jnp.int32).reshape(1)
    near_far = jnp.concatenate([near_at, far_at])

    tile_count = half_hidden // TILE
    split = tile_count - tile_count // 2
    tile_parts = [(0, split), (split, tile_count - split)]

    def near_pair(rows):
        return rows, swap(rows, "example", 1)

    def run(h, far, own, after):
        return stage(offset, near_far, tile_parts[h], far, own, down_weight, weight_near, after)

    weight_near = swap(down_weight, "example", 1)
    gate_rows = gate_pre.reshape(row_total, hidden_local)
    up_rows = up_pre.reshape(row_total, hidden_local)
    gate_near, up_near = swap(gate_rows, "example", 1), swap(up_rows, "example", 1)
    away = cut(1 - far_at, gathered[0], ())
    far_pair = near_pair(swap(away, "example", 2))
    came, right, after = [], [], ()
    for h, tiles in enumerate(tile_parts):
        results = run(h, far_pair, None, after)
        came.append((swap(results[0], "example", 2), tiles[0]))
        after = (results[0],)
    for k in range(1, chunks):
        before = near_pair(gathered[k - 1])
        if k == 1:
            away = cut(1 - far_at, gathered[1], after)
            far_pair = near_pair(swap(away, "example", 2))
            gate_packed = pack(chunks, 2 * LANES, half_hidden, offset, place, gate_rows, gate_near, after=(away,))
            up_packed = pack(chunks, 2 * LANES, half_hidden, offset, place, up_rows, up_near, after=(away,))
            after = (gate_packed[0], up_packed[0])
        else:
            far_pair = near_pair(ordered(far_next, after))
        if k + 1 < chunks:
            next_away = cut(1 - far_at, gathered[k + 1], after)
            far_next = swap(next_away, "example", 2)
            after += (next_away,)
            if k == 1:
                middle = (next_away,)
        arrived, came = came, []
        for h, tiles in enumerate(tile_parts):
            own = (*before, arrived[h], gate_packed[k - 1], up_packed[k - 1])
            results = run(h, far_pair, (*own, proj_gate, proj_up), after)
            after = (results[0],)
            came.append((swap(results[0], "example", 2), tiles[0]))
            right.append(results[1])
    before = near_pair(gathered[-1])
    for h, tiles in enumerate(tile_parts):
        own = (*before, came[h], gate_packed[-1], up_packed[-1], proj_gate, proj_up)
        right += run(h, None, own, after)
        after = (right[-1],)
    right = jnp.concatenate([right[k] + right[k + 1] for k in range(0, 2 * chunks, 2)], axis=1)

    inputs_rows = layer_input.reshape(row_total, width_local)
    gate_values = gate_pre.reshape(row_total, hidden_local).astype(jnp.float32)
    up_values = up_pre.reshape(row_total, hidden_local).astype(jnp.float32)
    hidden = (gate_values * jax.nn.sigmoid(gate_values) * up_values).astype(jnp.bfloat16)
    early = jnp.concatenate(
        [
            contract(proj_input, inputs_rows),
            contract(proj_hidden, hidden),
            contract(proj_output, grad_rows),
        ]
    )
    early = scatter_over(ordered(early, middle), "tensor", 1)
    in_gate, in_down, out_down = (early[k * rank_size : (k + 1) * rank_size] for k in range(3))
    in_gate = jnp.stack([in_gate] + [swap(in_gate, "tensor", bits) for bits in (1, 2, 3)])
    in_gate = jnp.concatenate([take(in_gate, tensor_at ^ t, 1, 0)[0] for t in range(4)], axis=1)
    in_gate = jnp.concatenate([in_gate, swap(in_gate, "example", 1)], axis=1)
    slots_here = jnp.concatenate(
        [
            take(rev_slot, example_at * ex_count, ex_count, 0),
            take(rev_slot, (example_at ^ 1) * ex_count, ex_count, 0),
        ]
    )
    table = pairing_table(slots_here, rev_pairs)
    mask = (positions < take(own_lengths, tensor_at, 1, 0)).astype(jnp.float32)
    sketch_down = contract_exact(in_down * mask[None, :], out_down)
    sketch_down = take(table, tensor_at, 1, 1)[:, :, None] * sketch_down[None, :, :]
    select = jnp.arange(capacity, dtype=jnp.int32)[:, None] == place
    in_gate = contract_exact(in_gate, select.astype(jnp.float32))
    table_rows = contract(
        jnp.repeat(table, slot_len, axis=1).astype(jnp.bfloat16), select.astype(jnp.bfloat16)
    )
    left = (table_rows[:, None, :] * in_gate[None, :, :]).reshape(rev_pairs * rank_size, capacity)
    sketch_late = contract_exact(left, right).reshape(rev_pairs, rank_size, 2 * rank_size)
    return jnp.concatenate([sketch_late, sketch_down], axis=2)


def local_four(
    layer_input,
    gate_pre,
    up_pre,
    output_grad,
    down_weight,
    proj_input,
    proj_hidden,
    proj_output,
    proj_gate,
    proj_up,
    query_sketches,
    rev_lengths,
    rev_slot,
    query_slot,
):
    ex_count, slot_len, width_local = layer_input.shape
    row_total = ex_count * slot_len
    grad_rows = output_grad.reshape(row_total, width_local)
    grad_near = swap(grad_rows, "example", 1)
    others = [swap(rev_lengths, "example", bits) for bits in (1, 2, 3)]
    sums = jnp.stack([jnp.sum(rev_lengths) + jnp.sum(others[0]), jnp.sum(others[1]) + jnp.sum(others[2])])
    most = jnp.max(sums).reshape(1)
    count = lax.axis_size("group")
    for step in range(1, count):
        shifted = lax.ppermute(most, "group", [(i, (i + step) % count) for i in range(count)])
        most = jnp.maximum(most, shifted)
    full = 2 * row_total
    levels = [level for level in LEVELS if level < full] + [full]
    branch = jnp.sum((most[0] > jnp.array(levels[:-1], jnp.int32)).astype(jnp.int32))
    sketch = lax.switch(
        branch,
        [functools.partial(packed_scores, level) for level in levels],
        (
            layer_input,
            gate_pre,
            up_pre,
            grad_rows,
            grad_near,
            down_weight,
            proj_input,
            proj_hidden,
            proj_output,
            proj_gate,
            proj_up,
            rev_slot,
            rev_lengths,
            others[0],
        ),
    )
    rank_size = proj_input.shape[0]
    rev_pairs = rev_slot.shape[0] // 2
    revision_pairs = sum_over(scatter_over(sketch, "tensor", 1), "example")
    example_scores = contract_exact(
        revision_pairs.reshape(rev_pairs, -1), query_sketches.astype(jnp.float32)
    )
    query_pairs = query_slot.shape[0] * 4 // 2
    pair_terms = contract_exact(example_scores, pairing_table(query_slot, query_pairs))
    total = sum_over(scatter_over(pair_terms, "example", 1), "tensor")
    return total / jnp.float32(rank_size * rank_size)


def local_any(
    layer_input,
    gate_pre,
    up_pre,
    output_grad,
    down_weight,
    proj_input,
    proj_hidden,
    proj_output,
    proj_gate,
    proj_up,
    query_sketches,
    rev_lengths,
    rev_slot,
    query_slot,
):
    ex_count, slot_len, width_local = layer_input.shape
    hidden_local = gate_pre.shape[2]
    row_total = ex_count * slot_len
    rank_size = proj_input.shape[0]
    per_rank = rank_size // lax.axis_size("tensor")
    inputs_rows = layer_input.reshape(row_total, width_local)
    grad_rows = output_grad.reshape(row_total, width_local)
    gate_values = gate_pre.reshape(row_total, hidden_local).astype(jnp.float32)
    up_values = up_pre.reshape(row_total, hidden_local).astype(jnp.float32)
    grad_full = lax.all_gather(grad_rows, "tensor", axis=1, tiled=True)
    hidden_grad = contract(grad_full, lax.all_gather(down_weight, "example", axis=1, tiled=True))
    hidden_grad = lax.optimization_barrier(hidden_grad.astype(jnp.bfloat16)).astype(jnp.float32)
    sigma = jax.nn.sigmoid(gate_values)
    active = gate_values * sigma
    hidden = (active * up_values).astype(jnp.bfloat16)
    grad_up = (hidden_grad * active).astype(jnp.bfloat16)
    grad_gate = (hidden_grad * up_values * sigma * (1.0 + gate_values * (1.0 - sigma))).astype(
        jnp.bfloat16
    )
    partials = jnp.stack(
        [
            contract(inputs_rows, proj_input),
            contract(hidden, proj_hidden),
            contract(grad_gate, proj_gate),
            contract(grad_up, proj_up),
            contract(grad_rows, proj_output),
        ]
    )
    summed = lax.psum(partials, "tensor")
    begin = lax.axis_index("tensor") * per_rank
    left = lax.dynamic_slice_in_dim(summed[:2], begin, per_rank, 2)
    right = summed[2:]
    positions = jnp.arange(slot_len, dtype=jnp.int32)
    mask = (positions[None, :] < rev_lengths[:, None]).astype(jnp.float32).reshape(row_total)
    left = left * mask[None, :, None]
    left = jnp.stack([left[0], left[0], left[1]]).reshape(3, ex_count, slot_len, per_rank)
    right = right.reshape(3, ex_count, slot_len, rank_size)
    sketches = jnp.einsum("meti,metj->eimj", left, right, precision=lax.Precision.HIGHEST).reshape(
        ex_count, per_rank * 3 * rank_size
    )
    every_sketch = lax.all_gather(sketches, "example", axis=0, tiled=True)
    rev_pairs = rev_slot.shape[0] // 2
    revision_pairs = jnp.dot(
        pairing_table(rev_slot, rev_pairs), every_sketch, precision=lax.Precision.HIGHEST
    )
    example_scores = contract_exact(revision_pairs, query_sketches.astype(jnp.float32))
    query_pairs = query_slot.shape[0] * lax.axis_size("example") // 2
    pair_terms = contract_exact(example_scores, pairing_table(query_slot, query_pairs))
    owned = lax.psum_scatter(pair_terms, "example", scatter_dimension=1, tiled=True)
    total = lax.psum(owned, "tensor")
    return total / jnp.float32(rank_size * rank_size)


def solution(mesh):
    four = mesh.shape["tensor"] == 4 and mesh.shape["example"] == 4
    return jax.shard_map(
        local_four if four else local_any,
        mesh=mesh,
        in_specs=(
            P(("group", "example"), None, "tensor"),
            P(("group", "example"), None, "tensor"),
            P(("group", "example"), None, "tensor"),
            P(("group", "example"), None, "tensor"),
            P("tensor", "example"),
            P(None, "tensor"),
            P(None, "tensor"),
            P(None, "tensor"),
            P(None, "tensor"),
            P(None, "tensor"),
            P(("group", "example"), "tensor"),
            P(("group", "example")),
            P("group"),
            P(("group", "example")),
        ),
        out_specs=P("group", "example"),
        check_vma=False,
    )
```

```python
import functools

import jax
import jax.numpy as jnp
from jax import lax
from jax.experimental import pallas as pl
from jax.experimental.pallas import tpu as pltpu
from jax.sharding import PartitionSpec as P

LEVELS = (768,)
TILE = 512
STEP = 256
LANES = 128
VMEM_LIMIT = 58 * 1024 * 1024


def contract(left_side, right_side):
    return lax.dot_general(
        left_side, right_side, (((1,), (1,)), ((), ())), preferred_element_type=jnp.float32
    )


def contract_exact(left_side, right_side):
    return lax.dot_general(
        left_side,
        right_side,
        (((1,), (1,)), ((), ())),
        precision=lax.Precision.HIGHEST,
        preferred_element_type=jnp.float32,
    )


def pairing_table(slots, pairs):
    pair_index = slots // 2
    signs = (1 - 2 * (slots % 2)).astype(jnp.float32)
    targets = jnp.arange(pairs, dtype=jnp.int32)
    return jnp.where(targets[:, None] == pair_index[None, :], signs[None, :], jnp.float32(0.0))


def take(array, start, size, axis):
    return lax.dynamic_slice_in_dim(array, start, size, axis)


def swap(array, axis, bits):
    count = lax.axis_size(axis)
    return lax.ppermute(array, axis, [(i, i ^ bits) for i in range(count)])


def kernel_params():
    return pltpu.CompilerParams(vmem_limit_bytes=VMEM_LIMIT)


def pack_kernel(size, count, near_ref, place_ref, own_ref, other_ref, *refs):
    outs, select = refs[-1 - count : -1], refs[-1]
    rows_own = own_ref.shape[0]

    @pl.when(pl.program_id(0) == 0)
    def _():
        @pl.loop(0, count)
        def _(c):
            at = lax.broadcasted_iota(jnp.int32, (size, select.shape[1]), 0) + c * 2 * LANES
            chosen = jnp.where(at == place_ref[...], 1.0, 0.0).astype(jnp.bfloat16)
            select[pl.ds(pl.multiple_of(c * size, size), size), :] = chosen

    for c in range(count):
        rows = slice(c * size, (c + 1) * size)
        total = jnp.dot(select[rows, :rows_own], own_ref[...], preferred_element_type=jnp.float32)
        total += jnp.dot(select[rows, rows_own:], other_ref[...], preferred_element_type=jnp.float32)
        outs[c][...] = total.astype(jnp.bfloat16).T


def pack(count, size, columns, near_offset, place, own, other, after=()):
    rows = own.shape[0]
    total = count * size
    return pl.pallas_call(
        functools.partial(pack_kernel, size, count),
        grid_spec=pltpu.PrefetchScalarGridSpec(
            num_scalar_prefetch=1,
            grid=(columns // TILE,),
            in_specs=[
                pl.BlockSpec((1, 2 * rows), lambda i, near: (0, 0)),
                pl.BlockSpec((rows, TILE), lambda i, near: (0, near[0] + i)),
                pl.BlockSpec((rows, TILE), lambda i, near: (0, near[0] + i)),
            ]
            + [pl.BlockSpec(memory_space=pl.ANY)] * len(after),
            out_specs=[pl.BlockSpec((TILE, size), lambda i, near: (i, 0))] * count,
            scratch_shapes=[pltpu.VMEM((total, 2 * rows), jnp.bfloat16)],
        ),
        out_shape=[jax.ShapeDtypeStruct((columns, size), jnp.bfloat16)] * count,
        compiler_params=kernel_params(),
        cost_estimate=pl.CostEstimate(
            flops=4 * total * rows * columns,
            bytes_accessed=(4 * rows + 2 * total) * columns,
            transcendentals=0,
        ),
        name="pack_rows",
    )(near_offset, place, own, other, *after)


def cut_kernel(at_ref, source, *refs):
    refs[-1][...] = source[...]


def cut(at, gathered, after):
    columns, rows = gathered.shape
    block = columns // 8
    return pl.pallas_call(
        cut_kernel,
        grid_spec=pltpu.PrefetchScalarGridSpec(
            num_scalar_prefetch=1,
            grid=(4,),
            in_specs=[pl.BlockSpec((block, rows), lambda i, at: (4 * at[0] + i, 0))]
            + [pl.BlockSpec(memory_space=pl.ANY)] * len(after),
            out_specs=pl.BlockSpec((block, rows), lambda i, at: (i, 0)),
        ),
        out_shape=jax.ShapeDtypeStruct((columns // 2, rows), gathered.dtype),
        compiler_params=kernel_params(),
        cost_estimate=pl.CostEstimate(flops=0, bytes_accessed=2 * columns * rows, transcendentals=0),
        name="cut_columns",
    )(at, gathered, *after)


def gate_kernel(value, *refs):
    refs[-1][...] = value[...]


def ordered(value, after):
    return pl.pallas_call(
        gate_kernel,
        in_specs=[pl.BlockSpec(memory_space=pltpu.VMEM)]
        + [pl.BlockSpec(memory_space=pl.ANY)] * len(after),
        out_specs=pl.BlockSpec(memory_space=pltpu.VMEM),
        out_shape=jax.ShapeDtypeStruct(value.shape, value.dtype),
        compiler_params=kernel_params(),
        name="ordered_copy",
    )(value, *after)


def stage_kernel(far, own, offset_ref, near_ref, *refs):
    refs = list(refs)
    weights = [refs.pop(0) for _ in range(4)]
    far_ins = [refs.pop(0) for _ in range(4 * far)]
    own_ins = [refs.pop(0) for _ in range(4 * own)]
    extra = [refs.pop(0) for _ in range(5 * own)]
    own_right = refs.pop() if own else None
    far_right = refs.pop() if far else None
    out = refs.pop() if own else None
    far_out = refs.pop() if far else None
    depth = weights[0].shape[1]
    width = 2 * depth

    def join(ins, right):
        for side in range(2):
            for k in range(2):
                right[side * width : (side + 1) * width, k * LANES : (k + 1) * LANES] = ins[2 * side + k][...]

    def half_sum(rows, right):
        total = 0.0
        for k in range(4):
            block = right[k * depth : (k + 1) * depth, :]
            total += jnp.dot(weights[k][rows, :], block, preferred_element_type=jnp.float32)
        return total

    @pl.when(pl.program_id(0) == 0)
    def _():
        if far:
            join(far_ins, far_right)
        if own:
            join(own_ins, own_right)
            out[...] = jnp.zeros_like(out)

    @pl.loop(0, TILE // STEP)
    def _(r):
        rows = pl.ds(pl.multiple_of(r * STEP, STEP), STEP)
        if far:
            far_out[rows, :] = half_sum(rows, far_right).astype(jnp.bfloat16)
        if own:
            came, gate_ref, up_ref, proj_gate, proj_up = extra
            rank_size = proj_gate.shape[0]
            total = half_sum(rows, own_right)
            hidden_grad = (total + came[rows, :].astype(jnp.float32)).astype(jnp.bfloat16)
            hidden_grad = hidden_grad.astype(jnp.float32)
            gate = gate_ref[rows, :].astype(jnp.float32)
            up = up_ref[rows, :].astype(jnp.float32)
            sigma = jax.nn.sigmoid(gate)
            grad_up = (hidden_grad * (gate * sigma)).astype(jnp.bfloat16)
            grad_gate = (hidden_grad * up * sigma * (1.0 + gate * (1.0 - sigma))).astype(jnp.bfloat16)
            out[:rank_size, :] += jnp.dot(proj_gate[:, rows], grad_gate, preferred_element_type=jnp.float32)
            out[rank_size:, :] += jnp.dot(proj_up[:, rows], grad_up, preferred_element_type=jnp.float32)


def stage(near_offset, near, tiles, far, own, weight, weight_near, after):
    begin, count = tiles
    width = weight_near.shape[1]
    depth = width // 2
    both = 2 * LANES
    arrays, specs, outs, shapes, rights = [], [], [], [], []

    def add(array, block, index):
        arrays.append(array)
        specs.append(pl.BlockSpec(block, index))

    for k in range(2):
        add(weight, (TILE, depth), lambda i, offset, near, k=k: (offset[0] + begin + i, k))
    for k in range(2):
        add(weight_near, (TILE, depth), lambda i, offset, near, k=k: (offset[0] + begin + i, k))
    for rows, base in ((far, 0), (own, 2)):
        if rows is not None:
            rights.append(pltpu.VMEM((2 * width, both), jnp.bfloat16))
            for k in range(4):
                side = k // 2
                add(
                    rows[k % 2],
                    (width, LANES),
                    lambda i, offset, near, side=side, base=base: (
                        base * near[1] + near[0] + side * (1 - 2 * near[0]),
                        0,
                    ),
                )
    if far is not None:
        outs.append(pl.BlockSpec((TILE, both), lambda i, offset, near: (i, 0)))
        shapes.append(jax.ShapeDtypeStruct((count * TILE, both), jnp.bfloat16))
    if own is not None:
        (came, first), gate, up, proj_gate, proj_up = own[2:]
        rank_size = proj_gate.shape[0]
        add(came, (TILE, both), lambda i, offset, near: (begin - first + i, 0))
        for array in (gate, up):
            add(array, (TILE, both), lambda i, offset, near: (begin + i, 0))
        for array in (proj_gate, proj_up):
            add(array, (rank_size, TILE), lambda i, offset, near: (0, offset[0] + begin + i))
        outs.append(pl.BlockSpec((2 * rank_size, both), lambda i, offset, near: (0, 0)))
        shapes.append(jax.ShapeDtypeStruct((2 * rank_size, both), jnp.float32))
    parts = len(rights)
    return pl.pallas_call(
        functools.partial(stage_kernel, far is not None, own is not None),
        grid_spec=pltpu.PrefetchScalarGridSpec(
            num_scalar_prefetch=2,
            grid=(count,),
            in_specs=specs + [pl.BlockSpec(memory_space=pl.ANY)] * len(after),
            out_specs=outs,
            scratch_shapes=rights,
        ),
        out_shape=shapes,
        compiler_params=kernel_params(),
        cost_estimate=pl.CostEstimate(
            flops=4 * parts * both * width * count * TILE,
            bytes_accessed=4 * width * count * TILE + 4 * parts * both * count * TILE,
            transcendentals=0,
        ),
        name="stage",
    )(near_offset, near, *arrays, *after)


def sum_over(array, axis):
    parts = [swap(array, axis, bits) for bits in (1, 2, 3)]
    return (array + parts[0]) + (parts[1] + parts[2])


def scatter_over(array, axis, dim):
    at = lax.axis_index(axis)
    size = array.shape[dim] // 4
    parts = [swap(take(array, (at ^ bits) * size, size, dim), axis, bits) for bits in (1, 2, 3)]
    return (take(array, at * size, size, dim) + parts[0]) + (parts[1] + parts[2])


def packed_scores(capacity, args):
    (
        layer_input,
        gate_pre,
        up_pre,
        grad_rows,
        blocks,
        gathered,
        place,
        down_weight,
        weight_near,
        proj_input,
        proj_hidden,
        proj_output,
        proj_gate,
        proj_up,
        rev_slot,
        own_lengths,
    ) = args
    ex_count, slot_len, width_local = layer_input.shape
    hidden_local = gate_pre.shape[2]
    row_total = ex_count * slot_len
    rank_size = proj_input.shape[0]
    rev_pairs = rev_slot.shape[0] // 2
    example_at = lax.axis_index("example")
    tensor_at = lax.axis_index("tensor")
    near, far = example_at % 2, example_at // 2
    half_hidden = hidden_local // 2
    chunks = capacity // (2 * LANES)
    offset = (near * (half_hidden // TILE)).astype(jnp.int32).reshape(1)
    near_at, far_at = near.astype(jnp.int32).reshape(1), far.astype(jnp.int32).reshape(1)
    near_far = jnp.concatenate([near_at, far_at])
    gathered = [gathered] + [lax.all_gather(blocks[k], "tensor", axis=0, tiled=True) for k in range(1, chunks)]

    tile_count = half_hidden // TILE
    split = tile_count - tile_count // 2
    tile_parts = [(0, split), (split, tile_count - split)]

    def near_pair(rows):
        return rows, swap(rows, "example", 1)

    def run(h, far, own, after):
        return stage(offset, near_far, tile_parts[h], far, own, down_weight, weight_near, after)

    gate_rows = gate_pre.reshape(row_total, hidden_local)
    up_rows = up_pre.reshape(row_total, hidden_local)
    gate_near, up_near = swap(gate_rows, "example", 1), swap(up_rows, "example", 1)
    away = cut(1 - far_at, gathered[0], ())
    inputs_rows = layer_input.reshape(row_total, width_local)
    gate_values = gate_rows.astype(jnp.float32)
    up_values = up_rows.astype(jnp.float32)
    hidden = (gate_values * jax.nn.sigmoid(gate_values) * up_values).astype(jnp.bfloat16)
    early = jnp.concatenate(
        [
            contract(proj_input, inputs_rows),
            contract(proj_hidden, hidden),
            contract(proj_output, grad_rows),
        ]
    )
    early = scatter_over(early, "tensor", 1)
    in_gate, in_down, out_down = (early[k * rank_size : (k + 1) * rank_size] for k in range(3))
    in_gate = jnp.stack([in_gate] + [swap(in_gate, "tensor", bits) for bits in (1, 2, 3)])
    in_gate = jnp.concatenate([take(in_gate, tensor_at ^ t, 1, 0)[0] for t in range(4)], axis=1)
    in_gate_near = swap(in_gate, "example", 1)

    far_pair = near_pair(swap(away, "example", 2))
    gate_packed = pack(chunks, 2 * LANES, half_hidden, offset, place, gate_rows, gate_near, after=(away,))
    up_packed = pack(chunks, 2 * LANES, half_hidden, offset, place, up_rows, up_near, after=(away,))
    came, right, after = [], [], (gate_packed[0], up_packed[0])
    for h, tiles in enumerate(tile_parts):
        results = run(h, far_pair, None, after)
        came.append((swap(results[0], "example", 2), tiles[0]))
        after = (results[0],)
    for k in range(1, chunks):
        before = near_pair(gathered[k - 1])
        if k == 1:
            away = cut(1 - far_at, gathered[1], after)
            far_pair = near_pair(swap(away, "example", 2))
            after = (in_gate_near, early)
        else:
            far_pair = near_pair(ordered(far_next, after))
        if k + 1 < chunks:
            next_away = cut(1 - far_at, gathered[k + 1], after if k > 1 else (away,))
            far_next = swap(next_away, "example", 2)
            after += (next_away,)
        arrived, came = came, []
        for h, tiles in enumerate(tile_parts):
            own = (*before, arrived[h], gate_packed[k - 1], up_packed[k - 1])
            results = run(h, far_pair, (*own, proj_gate, proj_up), after)
            after = (results[0],)
            came.append((swap(results[0], "example", 2), tiles[0]))
            right.append(results[1])
    before = near_pair(gathered[-1])
    for h, tiles in enumerate(tile_parts):
        own = (*before, came[h], gate_packed[-1], up_packed[-1], proj_gate, proj_up)
        right += run(h, None, own, after)
        after = (right[-1],)
    right = jnp.concatenate([right[k] + right[k + 1] for k in range(0, 2 * chunks, 2)], axis=1)

    slots_here = jnp.concatenate(
        [
            take(rev_slot, example_at * ex_count, ex_count, 0),
            take(rev_slot, (example_at ^ 1) * ex_count, ex_count, 0),
        ]
    )
    table = pairing_table(slots_here, rev_pairs)
    positions = jnp.arange(slot_len, dtype=jnp.int32)
    mask = (positions < take(own_lengths, tensor_at, 1, 0)).astype(jnp.float32)
    sketch_down = contract_exact(in_down * mask[None, :], out_down)
    sketch_down = take(table, tensor_at, 1, 1)[:, :, None] * sketch_down[None, :, :]
    select = jnp.arange(capacity, dtype=jnp.int32)[:, None] == place
    in_gate = jnp.concatenate([in_gate, in_gate_near], axis=1)
    in_gate = contract_exact(in_gate, select.astype(jnp.float32))
    table_rows = contract(
        jnp.repeat(table, slot_len, axis=1).astype(jnp.bfloat16), select.astype(jnp.bfloat16)
    )
    left = (table_rows[:, None, :] * in_gate[None, :, :]).reshape(rev_pairs * rank_size, capacity)
    sketch_late = contract_exact(left, right).reshape(rev_pairs, rank_size, 2 * rank_size)
    return jnp.concatenate([sketch_late, sketch_down], axis=2)


def local_four(
    layer_input,
    gate_pre,
    up_pre,
    output_grad,
    down_weight,
    proj_input,
    proj_hidden,
    proj_output,
    proj_gate,
    proj_up,
    query_sketches,
    rev_lengths,
    rev_slot,
    query_slot,
):
    ex_count, slot_len, width_local = layer_input.shape
    row_total = ex_count * slot_len
    grad_rows = output_grad.reshape(row_total, width_local)
    grad_near = swap(grad_rows, "example", 1)
    others = [swap(rev_lengths, "example", bits) for bits in (1, 2, 3)]

    near = lax.axis_index("example") % 2
    both_lengths = jnp.concatenate([rev_lengths, others[0]])
    own_begin = near * jnp.sum(others[0])
    near_begin = (1 - near) * jnp.sum(rev_lengths)
    offsets = jnp.concatenate(
        [
            own_begin + jnp.cumsum(rev_lengths) - rev_lengths,
            near_begin + jnp.cumsum(others[0]) - others[0],
        ]
    )
    positions = jnp.arange(slot_len, dtype=jnp.int32)
    place = (offsets[:, None] + positions[None, :]) ^ (near * LANES)
    place = jnp.where(positions[None, :] < both_lengths[:, None], place, -1).reshape(1, 2 * row_total)
    no_offset = jnp.zeros((1,), jnp.int32)
    full = 2 * row_total
    blocks = pack(full // (2 * LANES), LANES, width_local, no_offset, place, grad_rows, grad_near)
    gathered = lax.all_gather(blocks[0], "tensor", axis=0, tiled=True)
    weight_near = swap(down_weight, "example", 1)
    sums = jnp.stack([jnp.sum(rev_lengths) + jnp.sum(others[0]), jnp.sum(others[1]) + jnp.sum(others[2])])
    most = jnp.max(sums).reshape(1)
    count = lax.axis_size("group")
    for step in range(1, count):
        shifted = lax.ppermute(most, "group", [(i, (i + step) % count) for i in range(count)])
        most = jnp.maximum(most, shifted)
    levels = [level for level in LEVELS if level < full] + [full]
    branch = jnp.sum((most[0] > jnp.array(levels[:-1], jnp.int32)).astype(jnp.int32))
    sketch = lax.switch(
        branch,
        [functools.partial(packed_scores, level) for level in levels],
        (
            layer_input,
            gate_pre,
            up_pre,
            grad_rows,
            blocks,
            gathered,
            place,
            down_weight,
            weight_near,
            proj_input,
            proj_hidden,
            proj_output,
            proj_gate,
            proj_up,
            rev_slot,
            rev_lengths,
        ),
    )
    rank_size = proj_input.shape[0]
    rev_pairs = rev_slot.shape[0] // 2
    revision_pairs = sum_over(scatter_over(sketch, "tensor", 1), "example")
    example_scores = contract_exact(
        revision_pairs.reshape(rev_pairs, -1), query_sketches.astype(jnp.float32)
    )
    query_pairs = query_slot.shape[0] * 4 // 2
    pair_terms = contract_exact(example_scores, pairing_table(query_slot, query_pairs))
    total = sum_over(scatter_over(pair_terms, "example", 1), "tensor")
    return total / jnp.float32(rank_size * rank_size)


def local_any(
    layer_input,
    gate_pre,
    up_pre,
    output_grad,
    down_weight,
    proj_input,
    proj_hidden,
    proj_output,
    proj_gate,
    proj_up,
    query_sketches,
    rev_lengths,
    rev_slot,
    query_slot,
):
    ex_count, slot_len, width_local = layer_input.shape
    hidden_local = gate_pre.shape[2]
    row_total = ex_count * slot_len
    rank_size = proj_input.shape[0]
    per_rank = rank_size // lax.axis_size("tensor")
    inputs_rows = layer_input.reshape(row_total, width_local)
    grad_rows = output_grad.reshape(row_total, width_local)
    gate_values = gate_pre.reshape(row_total, hidden_local).astype(jnp.float32)
    up_values = up_pre.reshape(row_total, hidden_local).astype(jnp.float32)
    grad_full = lax.all_gather(grad_rows, "tensor", axis=1, tiled=True)
    hidden_grad = contract(grad_full, lax.all_gather(down_weight, "example", axis=1, tiled=True))
    hidden_grad = lax.optimization_barrier(hidden_grad.astype(jnp.bfloat16)).astype(jnp.float32)
    sigma = jax.nn.sigmoid(gate_values)
    active = gate_values * sigma
    hidden = (active * up_values).astype(jnp.bfloat16)
    grad_up = (hidden_grad * active).astype(jnp.bfloat16)
    grad_gate = (hidden_grad * up_values * sigma * (1.0 + gate_values * (1.0 - sigma))).astype(
        jnp.bfloat16
    )
    partials = jnp.stack(
        [
            contract(inputs_rows, proj_input),
            contract(hidden, proj_hidden),
            contract(grad_gate, proj_gate),
            contract(grad_up, proj_up),
            contract(grad_rows, proj_output),
        ]
    )
    summed = lax.psum(partials, "tensor")
    begin = lax.axis_index("tensor") * per_rank
    left = lax.dynamic_slice_in_dim(summed[:2], begin, per_rank, 2)
    right = summed[2:]
    positions = jnp.arange(slot_len, dtype=jnp.int32)
    mask = (positions[None, :] < rev_lengths[:, None]).astype(jnp.float32).reshape(row_total)
    left = left * mask[None, :, None]
    left = jnp.stack([left[0], left[0], left[1]]).reshape(3, ex_count, slot_len, per_rank)
    right = right.reshape(3, ex_count, slot_len, rank_size)
    sketches = jnp.einsum("meti,metj->eimj", left, right, precision=lax.Precision.HIGHEST).reshape(
        ex_count, per_rank * 3 * rank_size
    )
    every_sketch = lax.all_gather(sketches, "example", axis=0, tiled=True)
    rev_pairs = rev_slot.shape[0] // 2
    revision_pairs = jnp.dot(
        pairing_table(rev_slot, rev_pairs), every_sketch, precision=lax.Precision.HIGHEST
    )
    example_scores = contract_exact(revision_pairs, query_sketches.astype(jnp.float32))
    query_pairs = query_slot.shape[0] * lax.axis_size("example") // 2
    pair_terms = contract_exact(example_scores, pairing_table(query_slot, query_pairs))
    owned = lax.psum_scatter(pair_terms, "example", scatter_dimension=1, tiled=True)
    total = lax.psum(owned, "tensor")
    return total / jnp.float32(rank_size * rank_size)


def solution(mesh):
    four = mesh.shape["tensor"] == 4 and mesh.shape["example"] == 4
    return jax.shard_map(
        local_four if four else local_any,
        mesh=mesh,
        in_specs=(
            P(("group", "example"), None, "tensor"),
            P(("group", "example"), None, "tensor"),
            P(("group", "example"), None, "tensor"),
            P(("group", "example"), None, "tensor"),
            P("tensor", "example"),
            P(None, "tensor"),
            P(None, "tensor"),
            P(None, "tensor"),
            P(None, "tensor"),
            P(None, "tensor"),
            P(("group", "example"), "tensor"),
            P(("group", "example")),
            P("group"),
            P(("group", "example")),
        ),
        out_specs=P("group", "example"),
        check_vma=False,
    )
```

```python
import functools

import jax
import jax.numpy as jnp
from jax import lax
from jax.experimental import pallas as pl
from jax.experimental.pallas import tpu as pltpu
from jax.sharding import PartitionSpec as P

LEVELS = (768,)
TILE = 512
STEP = 256
LANES = 128
VMEM_LIMIT = 58 * 1024 * 1024


def contract(left_side, right_side):
    return lax.dot_general(
        left_side, right_side, (((1,), (1,)), ((), ())), preferred_element_type=jnp.float32
    )


def contract_exact(left_side, right_side):
    return lax.dot_general(
        left_side,
        right_side,
        (((1,), (1,)), ((), ())),
        precision=lax.Precision.HIGHEST,
        preferred_element_type=jnp.float32,
    )


def pairing_table(slots, pairs):
    pair_index = slots // 2
    signs = (1 - 2 * (slots % 2)).astype(jnp.float32)
    targets = jnp.arange(pairs, dtype=jnp.int32)
    return jnp.where(targets[:, None] == pair_index[None, :], signs[None, :], jnp.float32(0.0))


def take(array, start, size, axis):
    return lax.dynamic_slice_in_dim(array, start, size, axis)


def swap(array, axis, bits):
    count = lax.axis_size(axis)
    return lax.ppermute(array, axis, [(i, i ^ bits) for i in range(count)])


def kernel_params():
    return pltpu.CompilerParams(vmem_limit_bytes=VMEM_LIMIT)


def pack_kernel(size, count, near_ref, place_ref, own_ref, other_ref, *refs):
    outs, select = refs[-1 - count : -1], refs[-1]
    rows_own = own_ref.shape[0]

    @pl.when(pl.program_id(0) == 0)
    def _():
        @pl.loop(0, count)
        def _(c):
            at = lax.broadcasted_iota(jnp.int32, (size, select.shape[1]), 0) + c * 2 * LANES
            chosen = jnp.where(at == place_ref[...], 1.0, 0.0).astype(jnp.bfloat16)
            select[pl.ds(pl.multiple_of(c * size, size), size), :] = chosen

    for c in range(count):
        rows = slice(c * size, (c + 1) * size)
        total = jnp.dot(select[rows, :rows_own], own_ref[...], preferred_element_type=jnp.float32)
        total += jnp.dot(select[rows, rows_own:], other_ref[...], preferred_element_type=jnp.float32)
        outs[c][...] = total.astype(jnp.bfloat16).T


def pack(count, size, columns, near_offset, place, own, other, after=()):
    rows = own.shape[0]
    total = count * size
    return pl.pallas_call(
        functools.partial(pack_kernel, size, count),
        grid_spec=pltpu.PrefetchScalarGridSpec(
            num_scalar_prefetch=1,
            grid=(columns // TILE,),
            in_specs=[
                pl.BlockSpec((1, 2 * rows), lambda i, near: (0, 0)),
                pl.BlockSpec((rows, TILE), lambda i, near: (0, near[0] + i)),
                pl.BlockSpec((rows, TILE), lambda i, near: (0, near[0] + i)),
            ]
            + [pl.BlockSpec(memory_space=pl.ANY)] * len(after),
            out_specs=[pl.BlockSpec((TILE, size), lambda i, near: (i, 0))] * count,
            scratch_shapes=[pltpu.VMEM((total, 2 * rows), jnp.bfloat16)],
        ),
        out_shape=[jax.ShapeDtypeStruct((columns, size), jnp.bfloat16)] * count,
        compiler_params=kernel_params(),
        cost_estimate=pl.CostEstimate(
            flops=4 * total * rows * columns,
            bytes_accessed=(4 * rows + 2 * total) * columns,
            transcendentals=0,
        ),
        name="pack_rows",
    )(near_offset, place, own, other, *after)


def cut_kernel(at_ref, source, *refs):
    refs[-1][...] = source[...]


def cut(at, gathered, after):
    columns, rows = gathered.shape
    block = columns // 8
    return pl.pallas_call(
        cut_kernel,
        grid_spec=pltpu.PrefetchScalarGridSpec(
            num_scalar_prefetch=1,
            grid=(4,),
            in_specs=[pl.BlockSpec((block, rows), lambda i, at: (4 * at[0] + i, 0))]
            + [pl.BlockSpec(memory_space=pl.ANY)] * len(after),
            out_specs=pl.BlockSpec((block, rows), lambda i, at: (i, 0)),
        ),
        out_shape=jax.ShapeDtypeStruct((columns // 2, rows), gathered.dtype),
        compiler_params=kernel_params(),
        cost_estimate=pl.CostEstimate(flops=0, bytes_accessed=2 * columns * rows, transcendentals=0),
        name="cut_columns",
    )(at, gathered, *after)


def gate_kernel(value, *refs):
    refs[-1][...] = value[...]


def ordered(value, after):
    return pl.pallas_call(
        gate_kernel,
        in_specs=[pl.BlockSpec(memory_space=pltpu.VMEM)]
        + [pl.BlockSpec(memory_space=pl.ANY)] * len(after),
        out_specs=pl.BlockSpec(memory_space=pltpu.VMEM),
        out_shape=jax.ShapeDtypeStruct(value.shape, value.dtype),
        compiler_params=kernel_params(),
        name="ordered_copy",
    )(value, *after)


def sum_kernel(a, b, c, d, *refs):
    refs[-1][...] = (a[...] + b[...]) + (c[...] + d[...])


def sum_parts(parts, after):
    return pl.pallas_call(
        sum_kernel,
        in_specs=[pl.BlockSpec(memory_space=pltpu.VMEM)] * 4
        + [pl.BlockSpec(memory_space=pl.ANY)] * len(after),
        out_specs=pl.BlockSpec(memory_space=pltpu.VMEM),
        out_shape=jax.ShapeDtypeStruct(parts[0].shape, parts[0].dtype),
        compiler_params=kernel_params(),
        name="sum_parts",
    )(*parts, *after)


def join_kernel(at_ref, a, b, c, d, *refs):
    out = refs[-1]
    size = a.shape[1]
    for bits, part in enumerate((a, b, c, d)):
        begin = pl.multiple_of((at_ref[0] ^ bits) * size, size)
        out[:, pl.ds(begin, size)] = part[...]


def join_parts(at, parts, after):
    rows, size = parts[0].shape
    return pl.pallas_call(
        join_kernel,
        in_specs=[pl.BlockSpec(memory_space=pltpu.SMEM)]
        + [pl.BlockSpec(memory_space=pltpu.VMEM)] * 4
        + [pl.BlockSpec(memory_space=pl.ANY)] * len(after),
        out_specs=pl.BlockSpec(memory_space=pltpu.VMEM),
        out_shape=jax.ShapeDtypeStruct((rows, 4 * size), parts[0].dtype),
        compiler_params=kernel_params(),
        name="join_parts",
    )(at, *parts, *after)


def stage_kernel(far, own, offset_ref, near_ref, *refs):
    refs = list(refs)
    weights = [refs.pop(0) for _ in range(4)]
    far_ins = [refs.pop(0) for _ in range(4 * far)]
    own_ins = [refs.pop(0) for _ in range(4 * own)]
    extra = [refs.pop(0) for _ in range(5 * own)]
    own_right = refs.pop() if own else None
    far_right = refs.pop() if far else None
    out = refs.pop() if own else None
    far_out = refs.pop() if far else None
    depth = weights[0].shape[1]
    width = 2 * depth

    def join(ins, right):
        for side in range(2):
            for k in range(2):
                right[side * width : (side + 1) * width, k * LANES : (k + 1) * LANES] = ins[2 * side + k][...]

    def half_sum(rows, right):
        total = 0.0
        for k in range(4):
            block = right[k * depth : (k + 1) * depth, :]
            total += jnp.dot(weights[k][rows, :], block, preferred_element_type=jnp.float32)
        return total

    @pl.when(pl.program_id(0) == 0)
    def _():
        if far:
            join(far_ins, far_right)
        if own:
            join(own_ins, own_right)
            out[...] = jnp.zeros_like(out)

    @pl.loop(0, TILE // STEP)
    def _(r):
        rows = pl.ds(pl.multiple_of(r * STEP, STEP), STEP)
        if far:
            far_out[rows, :] = half_sum(rows, far_right).astype(jnp.bfloat16)
        if own:
            came, gate_ref, up_ref, proj_gate, proj_up = extra
            rank_size = proj_gate.shape[0]
            total = half_sum(rows, own_right)
            hidden_grad = (total + came[rows, :].astype(jnp.float32)).astype(jnp.bfloat16)
            hidden_grad = hidden_grad.astype(jnp.float32)
            gate = gate_ref[rows, :].astype(jnp.float32)
            up = up_ref[rows, :].astype(jnp.float32)
            sigma = jax.nn.sigmoid(gate)
            grad_up = (hidden_grad * (gate * sigma)).astype(jnp.bfloat16)
            grad_gate = (hidden_grad * up * sigma * (1.0 + gate * (1.0 - sigma))).astype(jnp.bfloat16)
            out[:rank_size, :] += jnp.dot(proj_gate[:, rows], grad_gate, preferred_element_type=jnp.float32)
            out[rank_size:, :] += jnp.dot(proj_up[:, rows], grad_up, preferred_element_type=jnp.float32)


def stage(near_offset, near, tiles, far, own, weight, weight_near, after):
    begin, count = tiles
    width = weight_near.shape[1]
    depth = width // 2
    both = 2 * LANES
    arrays, specs, outs, shapes, rights = [], [], [], [], []

    def add(array, block, index):
        arrays.append(array)
        specs.append(pl.BlockSpec(block, index))

    for k in range(2):
        add(weight, (TILE, depth), lambda i, offset, near, k=k: (offset[0] + begin + i, k))
    for k in range(2):
        add(weight_near, (TILE, depth), lambda i, offset, near, k=k: (offset[0] + begin + i, k))
    for rows, base in ((far, 0), (own, 2)):
        if rows is not None:
            rights.append(pltpu.VMEM((2 * width, both), jnp.bfloat16))
            for k in range(4):
                side = k // 2
                add(
                    rows[k % 2],
                    (width, LANES),
                    lambda i, offset, near, side=side, base=base: (
                        base * near[1] + near[0] + side * (1 - 2 * near[0]),
                        0,
                    ),
                )
    if far is not None:
        outs.append(pl.BlockSpec((TILE, both), lambda i, offset, near: (i, 0)))
        shapes.append(jax.ShapeDtypeStruct((count * TILE, both), jnp.bfloat16))
    if own is not None:
        (came, first), gate, up, proj_gate, proj_up = own[2:]
        rank_size = proj_gate.shape[0]
        add(came, (TILE, both), lambda i, offset, near: (begin - first + i, 0))
        for array in (gate, up):
            add(array, (TILE, both), lambda i, offset, near: (begin + i, 0))
        for array in (proj_gate, proj_up):
            add(array, (rank_size, TILE), lambda i, offset, near: (0, offset[0] + begin + i))
        outs.append(pl.BlockSpec((2 * rank_size, both), lambda i, offset, near: (0, 0)))
        shapes.append(jax.ShapeDtypeStruct((2 * rank_size, both), jnp.float32))
    parts = len(rights)
    return pl.pallas_call(
        functools.partial(stage_kernel, far is not None, own is not None),
        grid_spec=pltpu.PrefetchScalarGridSpec(
            num_scalar_prefetch=2,
            grid=(count,),
            in_specs=specs + [pl.BlockSpec(memory_space=pl.ANY)] * len(after),
            out_specs=outs,
            scratch_shapes=rights,
        ),
        out_shape=shapes,
        compiler_params=kernel_params(),
        cost_estimate=pl.CostEstimate(
            flops=4 * parts * both * width * count * TILE,
            bytes_accessed=4 * width * count * TILE + 4 * parts * both * count * TILE,
            transcendentals=0,
        ),
        name="stage",
    )(near_offset, near, *arrays, *after)


def sum_over(array, axis):
    parts = [swap(array, axis, bits) for bits in (1, 2, 3)]
    return (array + parts[0]) + (parts[1] + parts[2])


def scatter_over(array, axis, dim):
    at = lax.axis_index(axis)
    size = array.shape[dim] // 4
    parts = [swap(take(array, (at ^ bits) * size, size, dim), axis, bits) for bits in (1, 2, 3)]
    return (take(array, at * size, size, dim) + parts[0]) + (parts[1] + parts[2])


def packed_scores(capacity, args):
    (
        layer_input,
        gate_pre,
        up_pre,
        grad_rows,
        blocks,
        place,
        down_weight,
        proj_input,
        proj_hidden,
        proj_output,
        proj_gate,
        proj_up,
        rev_slot,
        own_lengths,
    ) = args
    ex_count, slot_len, width_local = layer_input.shape
    hidden_local = gate_pre.shape[2]
    row_total = ex_count * slot_len
    rank_size = proj_input.shape[0]
    rev_pairs = rev_slot.shape[0] // 2
    example_at = lax.axis_index("example")
    tensor_at = lax.axis_index("tensor")
    near, far = example_at % 2, example_at // 2
    half_hidden = hidden_local // 2
    chunks = capacity // (2 * LANES)
    offset = (near * (half_hidden // TILE)).astype(jnp.int32).reshape(1)
    near_at, far_at = near.astype(jnp.int32).reshape(1), far.astype(jnp.int32).reshape(1)
    near_far = jnp.concatenate([near_at, far_at])
    gathered = [lax.all_gather(blocks[k], "tensor", axis=0, tiled=True) for k in range(chunks)]

    tile_count = half_hidden // TILE
    split = tile_count - tile_count // 2
    tile_parts = [(0, split), (split, tile_count - split)]

    def near_pair(rows):
        return rows, swap(rows, "example", 1)

    def run(h, far, own, after):
        return stage(offset, near_far, tile_parts[h], far, own, down_weight, weight_near, after)

    weight_near = swap(down_weight, "example", 1)
    gate_rows = gate_pre.reshape(row_total, hidden_local)
    up_rows = up_pre.reshape(row_total, hidden_local)
    gate_near, up_near = swap(gate_rows, "example", 1), swap(up_rows, "example", 1)
    away = cut(1 - far_at, gathered[0], ())
    inputs_rows = layer_input.reshape(row_total, width_local)
    gate_values = gate_rows.astype(jnp.float32)
    up_values = up_rows.astype(jnp.float32)
    hidden = (gate_values * jax.nn.sigmoid(gate_values) * up_values).astype(jnp.bfloat16)
    early = jnp.concatenate(
        [
            contract(proj_input, inputs_rows),
            contract(proj_hidden, hidden),
            contract(proj_output, grad_rows),
        ]
    )
    def quarter(bits):
        return take(early, (tensor_at ^ bits) * slot_len, slot_len, 1)

    sums = [quarter(0)] + [swap(quarter(bits), "tensor", bits) for bits in (1, 2, 3)]
    far_pair = near_pair(swap(away, "example", 2))
    came, right, after = [], [], ()
    for h, tiles in enumerate(tile_parts):
        results = run(h, far_pair, None, after)
        came.append((swap(results[0], "example", 2), tiles[0]))
        after = (results[0],)
    for k in range(1, chunks):
        before = near_pair(gathered[k - 1])
        if k == 1:
            away = cut(1 - far_at, gathered[1], after)
            far_pair = near_pair(swap(away, "example", 2))
            gate_packed = pack(chunks, 2 * LANES, half_hidden, offset, place, gate_rows, gate_near, after=(away,))
            up_packed = pack(chunks, 2 * LANES, half_hidden, offset, place, up_rows, up_near, after=(away,))
            after = (gate_packed[0], up_packed[0])
        else:
            far_pair = near_pair(ordered(far_next, after))
        if k + 1 < chunks:
            next_away = cut(1 - far_at, gathered[k + 1], after)
            far_next = swap(next_away, "example", 2)
            after += (next_away,)
        arrived, came = came, []
        for h, tiles in enumerate(tile_parts):
            own = (*before, arrived[h], gate_packed[k - 1], up_packed[k - 1])
            results = run(h, far_pair, (*own, proj_gate, proj_up), after)
            after = (results[0],)
            came.append((swap(results[0], "example", 2), tiles[0]))
            right.append(results[1])
            if (k, h) == (1, 0):
                sums = sum_parts(sums, after)
                after += (sums,)
                in_gate, in_down, out_down = (sums[j * rank_size : (j + 1) * rank_size] for j in range(3))
                in_gate = [in_gate] + [swap(in_gate, "tensor", bits) for bits in (1, 2, 3)]
            if (k, h) == (1, 1):
                in_gate = join_parts(tensor_at.astype(jnp.int32).reshape(1), in_gate, after)
                after += (in_gate,)
                in_gate_near = swap(in_gate, "example", 1)
    before = near_pair(gathered[-1])
    for h, tiles in enumerate(tile_parts):
        own = (*before, came[h], gate_packed[-1], up_packed[-1], proj_gate, proj_up)
        right += run(h, None, own, after)
        after = (right[-1],)
    right = jnp.concatenate([right[k] + right[k + 1] for k in range(0, 2 * chunks, 2)], axis=1)

    slots_here = jnp.concatenate(
        [
            take(rev_slot, example_at * ex_count, ex_count, 0),
            take(rev_slot, (example_at ^ 1) * ex_count, ex_count, 0),
        ]
    )
    table = pairing_table(slots_here, rev_pairs)
    positions = jnp.arange(slot_len, dtype=jnp.int32)
    mask = (positions < take(own_lengths, tensor_at, 1, 0)).astype(jnp.float32)
    sketch_down = contract_exact(in_down * mask[None, :], out_down)
    sketch_down = take(table, tensor_at, 1, 1)[:, :, None] * sketch_down[None, :, :]
    select = jnp.arange(capacity, dtype=jnp.int32)[:, None] == place
    in_gate = jnp.concatenate([in_gate, in_gate_near], axis=1)
    in_gate = contract_exact(in_gate, select.astype(jnp.float32))
    table_rows = contract(
        jnp.repeat(table, slot_len, axis=1).astype(jnp.bfloat16), select.astype(jnp.bfloat16)
    )
    left = (table_rows[:, None, :] * in_gate[None, :, :]).reshape(rev_pairs * rank_size, capacity)
    sketch_late = contract_exact(left, right).reshape(rev_pairs, rank_size, 2 * rank_size)
    return jnp.concatenate([sketch_late, sketch_down], axis=2)


def local_four(
    layer_input,
    gate_pre,
    up_pre,
    output_grad,
    down_weight,
    proj_input,
    proj_hidden,
    proj_output,
    proj_gate,
    proj_up,
    query_sketches,
    rev_lengths,
    rev_slot,
    query_slot,
):
    ex_count, slot_len, width_local = layer_input.shape
    row_total = ex_count * slot_len
    grad_rows = output_grad.reshape(row_total, width_local)
    grad_near = swap(grad_rows, "example", 1)
    others = [swap(rev_lengths, "example", bits) for bits in (1, 2, 3)]

    near = lax.axis_index("example") % 2
    both_lengths = jnp.concatenate([rev_lengths, others[0]])
    own_begin = near * jnp.sum(others[0])
    near_begin = (1 - near) * jnp.sum(rev_lengths)
    offsets = jnp.concatenate(
        [
            own_begin + jnp.cumsum(rev_lengths) - rev_lengths,
            near_begin + jnp.cumsum(others[0]) - others[0],
        ]
    )
    positions = jnp.arange(slot_len, dtype=jnp.int32)
    place = (offsets[:, None] + positions[None, :]) ^ (near * LANES)
    place = jnp.where(positions[None, :] < both_lengths[:, None], place, -1).reshape(1, 2 * row_total)
    no_offset = jnp.zeros((1,), jnp.int32)
    full = 2 * row_total
    blocks = pack(full // (2 * LANES), LANES, width_local, no_offset, place, grad_rows, grad_near)
    sums = jnp.stack([jnp.sum(rev_lengths) + jnp.sum(others[0]), jnp.sum(others[1]) + jnp.sum(others[2])])
    most = jnp.max(sums).reshape(1)
    count = lax.axis_size("group")
    for step in range(1, count):
        shifted = lax.ppermute(most, "group", [(i, (i + step) % count) for i in range(count)])
        most = jnp.maximum(most, shifted)
    levels = [level for level in LEVELS if level < full] + [full]
    branch = jnp.sum((most[0] > jnp.array(levels[:-1], jnp.int32)).astype(jnp.int32))
    sketch = lax.switch(
        branch,
        [functools.partial(packed_scores, level) for level in levels],
        (
            layer_input,
            gate_pre,
            up_pre,
            grad_rows,
            blocks,
            place,
            down_weight,
            proj_input,
            proj_hidden,
            proj_output,
            proj_gate,
            proj_up,
            rev_slot,
            rev_lengths,
        ),
    )
    rank_size = proj_input.shape[0]
    rev_pairs = rev_slot.shape[0] // 2
    revision_pairs = sum_over(scatter_over(sketch, "tensor", 1), "example")
    example_scores = contract_exact(
        revision_pairs.reshape(rev_pairs, -1), query_sketches.astype(jnp.float32)
    )
    query_pairs = query_slot.shape[0] * 4 // 2
    pair_terms = contract_exact(example_scores, pairing_table(query_slot, query_pairs))
    total = sum_over(scatter_over(pair_terms, "example", 1), "tensor")
    return total / jnp.float32(rank_size * rank_size)


def local_any(
    layer_input,
    gate_pre,
    up_pre,
    output_grad,
    down_weight,
    proj_input,
    proj_hidden,
    proj_output,
    proj_gate,
    proj_up,
    query_sketches,
    rev_lengths,
    rev_slot,
    query_slot,
):
    ex_count, slot_len, width_local = layer_input.shape
    hidden_local = gate_pre.shape[2]
    row_total = ex_count * slot_len
    rank_size = proj_input.shape[0]
    per_rank = rank_size // lax.axis_size("tensor")
    inputs_rows = layer_input.reshape(row_total, width_local)
    grad_rows = output_grad.reshape(row_total, width_local)
    gate_values = gate_pre.reshape(row_total, hidden_local).astype(jnp.float32)
    up_values = up_pre.reshape(row_total, hidden_local).astype(jnp.float32)
    grad_full = lax.all_gather(grad_rows, "tensor", axis=1, tiled=True)
    hidden_grad = contract(grad_full, lax.all_gather(down_weight, "example", axis=1, tiled=True))
    hidden_grad = lax.optimization_barrier(hidden_grad.astype(jnp.bfloat16)).astype(jnp.float32)
    sigma = jax.nn.sigmoid(gate_values)
    active = gate_values * sigma
    hidden = (active * up_values).astype(jnp.bfloat16)
    grad_up = (hidden_grad * active).astype(jnp.bfloat16)
    grad_gate = (hidden_grad * up_values * sigma * (1.0 + gate_values * (1.0 - sigma))).astype(
        jnp.bfloat16
    )
    partials = jnp.stack(
        [
            contract(inputs_rows, proj_input),
            contract(hidden, proj_hidden),
            contract(grad_gate, proj_gate),
            contract(grad_up, proj_up),
            contract(grad_rows, proj_output),
        ]
    )
    summed = lax.psum(partials, "tensor")
    begin = lax.axis_index("tensor") * per_rank
    left = lax.dynamic_slice_in_dim(summed[:2], begin, per_rank, 2)
    right = summed[2:]
    positions = jnp.arange(slot_len, dtype=jnp.int32)
    mask = (positions[None, :] < rev_lengths[:, None]).astype(jnp.float32).reshape(row_total)
    left = left * mask[None, :, None]
    left = jnp.stack([left[0], left[0], left[1]]).reshape(3, ex_count, slot_len, per_rank)
    right = right.reshape(3, ex_count, slot_len, rank_size)
    sketches = jnp.einsum("meti,metj->eimj", left, right, precision=lax.Precision.HIGHEST).reshape(
        ex_count, per_rank * 3 * rank_size
    )
    every_sketch = lax.all_gather(sketches, "example", axis=0, tiled=True)
    rev_pairs = rev_slot.shape[0] // 2
    revision_pairs = jnp.dot(
        pairing_table(rev_slot, rev_pairs), every_sketch, precision=lax.Precision.HIGHEST
    )
    example_scores = contract_exact(revision_pairs, query_sketches.astype(jnp.float32))
    query_pairs = query_slot.shape[0] * lax.axis_size("example") // 2
    pair_terms = contract_exact(example_scores, pairing_table(query_slot, query_pairs))
    owned = lax.psum_scatter(pair_terms, "example", scatter_dimension=1, tiled=True)
    total = lax.psum(owned, "tensor")
    return total / jnp.float32(rank_size * rank_size)


def solution(mesh):
    four = mesh.shape["tensor"] == 4 and mesh.shape["example"] == 4
    return jax.shard_map(
        local_four if four else local_any,
        mesh=mesh,
        in_specs=(
            P(("group", "example"), None, "tensor"),
            P(("group", "example"), None, "tensor"),
            P(("group", "example"), None, "tensor"),
            P(("group", "example"), None, "tensor"),
            P("tensor", "example"),
            P(None, "tensor"),
            P(None, "tensor"),
            P(None, "tensor"),
            P(None, "tensor"),
            P(None, "tensor"),
            P(("group", "example"), "tensor"),
            P(("group", "example")),
            P("group"),
            P(("group", "example")),
        ),
        out_specs=P("group", "example"),
        check_vma=False,
    )
```

```python
import functools

import jax
import jax.numpy as jnp
from jax import lax
from jax.experimental import pallas as pl
from jax.experimental.pallas import tpu as pltpu
from jax.sharding import PartitionSpec as P

LEVELS = (768,)
TILE = 512
STEP = 256
LANES = 128
VMEM_LIMIT = 58 * 1024 * 1024


def contract(left_side, right_side):
    return lax.dot_general(
        left_side, right_side, (((1,), (1,)), ((), ())), preferred_element_type=jnp.float32
    )


def contract_exact(left_side, right_side):
    return lax.dot_general(
        left_side,
        right_side,
        (((1,), (1,)), ((), ())),
        precision=lax.Precision.HIGHEST,
        preferred_element_type=jnp.float32,
    )


def pairing_table(slots, pairs):
    pair_index = slots // 2
    signs = (1 - 2 * (slots % 2)).astype(jnp.float32)
    targets = jnp.arange(pairs, dtype=jnp.int32)
    return jnp.where(targets[:, None] == pair_index[None, :], signs[None, :], jnp.float32(0.0))


def take(array, start, size, axis):
    return lax.dynamic_slice_in_dim(array, start, size, axis)


def swap(array, axis, bits):
    count = lax.axis_size(axis)
    return lax.ppermute(array, axis, [(i, i ^ bits) for i in range(count)])


def kernel_params():
    return pltpu.CompilerParams(vmem_limit_bytes=VMEM_LIMIT)


def pack_kernel(size, count, near_ref, place_ref, own_ref, other_ref, *refs):
    outs, select = refs[-1 - count : -1], refs[-1]
    rows_own = own_ref.shape[0]

    @pl.when(pl.program_id(0) == 0)
    def _():
        @pl.loop(0, count)
        def _(c):
            at = lax.broadcasted_iota(jnp.int32, (size, select.shape[1]), 0) + c * 2 * LANES
            chosen = jnp.where(at == place_ref[...], 1.0, 0.0).astype(jnp.bfloat16)
            select[pl.ds(pl.multiple_of(c * size, size), size), :] = chosen

    for c in range(count):
        rows = slice(c * size, (c + 1) * size)
        total = jnp.dot(select[rows, :rows_own], own_ref[...], preferred_element_type=jnp.float32)
        total += jnp.dot(select[rows, rows_own:], other_ref[...], preferred_element_type=jnp.float32)
        outs[c][...] = total.astype(jnp.bfloat16).T


def pack(count, size, columns, near_offset, place, own, other, after=()):
    rows = own.shape[0]
    total = count * size
    return pl.pallas_call(
        functools.partial(pack_kernel, size, count),
        grid_spec=pltpu.PrefetchScalarGridSpec(
            num_scalar_prefetch=1,
            grid=(columns // TILE,),
            in_specs=[
                pl.BlockSpec((1, 2 * rows), lambda i, near: (0, 0)),
                pl.BlockSpec((rows, TILE), lambda i, near: (0, near[0] + i)),
                pl.BlockSpec((rows, TILE), lambda i, near: (0, near[0] + i)),
            ]
            + [pl.BlockSpec(memory_space=pl.ANY)] * len(after),
            out_specs=[pl.BlockSpec((TILE, size), lambda i, near: (i, 0))] * count,
            scratch_shapes=[pltpu.VMEM((total, 2 * rows), jnp.bfloat16)],
        ),
        out_shape=[jax.ShapeDtypeStruct((columns, size), jnp.bfloat16)] * count,
        compiler_params=kernel_params(),
        cost_estimate=pl.CostEstimate(
            flops=4 * total * rows * columns,
            bytes_accessed=(4 * rows + 2 * total) * columns,
            transcendentals=0,
        ),
        name="pack_rows",
    )(near_offset, place, own, other, *after)


def cut_kernel(at_ref, source, *refs):
    refs[-1][...] = source[...]


def cut(at, gathered, after):
    columns, rows = gathered.shape
    block = columns // 8
    return pl.pallas_call(
        cut_kernel,
        grid_spec=pltpu.PrefetchScalarGridSpec(
            num_scalar_prefetch=1,
            grid=(4,),
            in_specs=[pl.BlockSpec((block, rows), lambda i, at: (4 * at[0] + i, 0))]
            + [pl.BlockSpec(memory_space=pl.ANY)] * len(after),
            out_specs=pl.BlockSpec((block, rows), lambda i, at: (i, 0)),
        ),
        out_shape=jax.ShapeDtypeStruct((columns // 2, rows), gathered.dtype),
        compiler_params=kernel_params(),
        cost_estimate=pl.CostEstimate(flops=0, bytes_accessed=2 * columns * rows, transcendentals=0),
        name="cut_columns",
    )(at, gathered, *after)


def gate_kernel(value, *refs):
    refs[-1][...] = value[...]


def ordered(value, after):
    return pl.pallas_call(
        gate_kernel,
        in_specs=[pl.BlockSpec(memory_space=pltpu.VMEM)]
        + [pl.BlockSpec(memory_space=pl.ANY)] * len(after),
        out_specs=pl.BlockSpec(memory_space=pltpu.VMEM),
        out_shape=jax.ShapeDtypeStruct(value.shape, value.dtype),
        compiler_params=kernel_params(),
        name="ordered_copy",
    )(value, *after)


def sum_kernel(a, b, c, d, *refs):
    refs[-1][...] = (a[...] + b[...]) + (c[...] + d[...])


def sum_parts(parts, after):
    return pl.pallas_call(
        sum_kernel,
        in_specs=[pl.BlockSpec(memory_space=pltpu.VMEM)] * 4
        + [pl.BlockSpec(memory_space=pl.ANY)] * len(after),
        out_specs=pl.BlockSpec(memory_space=pltpu.VMEM),
        out_shape=jax.ShapeDtypeStruct(parts[0].shape, parts[0].dtype),
        compiler_params=kernel_params(),
        name="sum_parts",
    )(*parts, *after)


def join_kernel(at_ref, a, b, c, d, *refs):
    out = refs[-1]
    size = a.shape[1]
    for bits, part in enumerate((a, b, c, d)):
        begin = pl.multiple_of((at_ref[0] ^ bits) * size, size)
        out[:, pl.ds(begin, size)] = part[...]


def join_parts(at, parts, after):
    rows, size = parts[0].shape
    return pl.pallas_call(
        join_kernel,
        in_specs=[pl.BlockSpec(memory_space=pltpu.SMEM)]
        + [pl.BlockSpec(memory_space=pltpu.VMEM)] * 4
        + [pl.BlockSpec(memory_space=pl.ANY)] * len(after),
        out_specs=pl.BlockSpec(memory_space=pltpu.VMEM),
        out_shape=jax.ShapeDtypeStruct((rows, 4 * size), parts[0].dtype),
        compiler_params=kernel_params(),
        name="join_parts",
    )(at, *parts, *after)


def stage_kernel(far, own, offset_ref, near_ref, *refs):
    refs = list(refs)
    weights = [refs.pop(0) for _ in range(4)]
    far_ins = [refs.pop(0) for _ in range(4 * far)]
    own_ins = [refs.pop(0) for _ in range(4 * own)]
    extra = [refs.pop(0) for _ in range(5 * own)]
    own_right = refs.pop() if own else None
    far_right = refs.pop() if far else None
    out = refs.pop() if own else None
    far_out = refs.pop() if far else None
    depth = weights[0].shape[1]
    width = 2 * depth

    def join(ins, right):
        for side in range(2):
            for k in range(2):
                right[side * width : (side + 1) * width, k * LANES : (k + 1) * LANES] = ins[2 * side + k][...]

    def half_sum(rows, right):
        total = 0.0
        for k in range(4):
            block = right[k * depth : (k + 1) * depth, :]
            total += jnp.dot(weights[k][rows, :], block, preferred_element_type=jnp.float32)
        return total

    @pl.when(pl.program_id(0) == 0)
    def _():
        if far:
            join(far_ins, far_right)
        if own:
            join(own_ins, own_right)
            out[...] = jnp.zeros_like(out)

    @pl.loop(0, TILE // STEP)
    def _(r):
        rows = pl.ds(pl.multiple_of(r * STEP, STEP), STEP)
        if far:
            far_out[rows, :] = half_sum(rows, far_right).astype(jnp.bfloat16)
        if own:
            came, gate_ref, up_ref, proj_gate, proj_up = extra
            rank_size = proj_gate.shape[0]
            total = half_sum(rows, own_right)
            hidden_grad = (total + came[rows, :].astype(jnp.float32)).astype(jnp.bfloat16)
            hidden_grad = hidden_grad.astype(jnp.float32)
            gate = gate_ref[rows, :].astype(jnp.float32)
            up = up_ref[rows, :].astype(jnp.float32)
            sigma = jax.nn.sigmoid(gate)
            grad_up = (hidden_grad * (gate * sigma)).astype(jnp.bfloat16)
            grad_gate = (hidden_grad * up * sigma * (1.0 + gate * (1.0 - sigma))).astype(jnp.bfloat16)
            out[:rank_size, :] += jnp.dot(proj_gate[:, rows], grad_gate, preferred_element_type=jnp.float32)
            out[rank_size:, :] += jnp.dot(proj_up[:, rows], grad_up, preferred_element_type=jnp.float32)


def stage(near_offset, near, tiles, far, own, weight, weight_near, after):
    begin, count = tiles
    width = weight_near.shape[1]
    depth = width // 2
    both = 2 * LANES
    arrays, specs, outs, shapes, rights = [], [], [], [], []

    def add(array, block, index):
        arrays.append(array)
        specs.append(pl.BlockSpec(block, index))

    for k in range(2):
        add(weight, (TILE, depth), lambda i, offset, near, k=k: (offset[0] + begin + i, k))
    for k in range(2):
        add(weight_near, (TILE, depth), lambda i, offset, near, k=k: (offset[0] + begin + i, k))
    for rows, base in ((far, 0), (own, 2)):
        if rows is not None:
            rights.append(pltpu.VMEM((2 * width, both), jnp.bfloat16))
            for k in range(4):
                side = k // 2
                add(
                    rows[k % 2],
                    (width, LANES),
                    lambda i, offset, near, side=side, base=base: (
                        base * near[1] + near[0] + side * (1 - 2 * near[0]),
                        0,
                    ),
                )
    if far is not None:
        outs.append(pl.BlockSpec((TILE, both), lambda i, offset, near: (i, 0)))
        shapes.append(jax.ShapeDtypeStruct((count * TILE, both), jnp.bfloat16))
    if own is not None:
        (came, first), gate, up, proj_gate, proj_up = own[2:]
        rank_size = proj_gate.shape[0]
        add(came, (TILE, both), lambda i, offset, near: (begin - first + i, 0))
        for array in (gate, up):
            add(array, (TILE, both), lambda i, offset, near: (begin + i, 0))
        for array in (proj_gate, proj_up):
            add(array, (rank_size, TILE), lambda i, offset, near: (0, offset[0] + begin + i))
        outs.append(pl.BlockSpec((2 * rank_size, both), lambda i, offset, near: (0, 0)))
        shapes.append(jax.ShapeDtypeStruct((2 * rank_size, both), jnp.float32))
    parts = len(rights)
    return pl.pallas_call(
        functools.partial(stage_kernel, far is not None, own is not None),
        grid_spec=pltpu.PrefetchScalarGridSpec(
            num_scalar_prefetch=2,
            grid=(count,),
            in_specs=specs + [pl.BlockSpec(memory_space=pl.ANY)] * len(after),
            out_specs=outs,
            scratch_shapes=rights,
        ),
        out_shape=shapes,
        compiler_params=kernel_params(),
        cost_estimate=pl.CostEstimate(
            flops=4 * parts * both * width * count * TILE,
            bytes_accessed=4 * width * count * TILE + 4 * parts * both * count * TILE,
            transcendentals=0,
        ),
        name="stage",
    )(near_offset, near, *arrays, *after)


def sum_over(array, axis):
    parts = [swap(array, axis, bits) for bits in (1, 2, 3)]
    return (array + parts[0]) + (parts[1] + parts[2])


def scatter_over(array, axis, dim):
    at = lax.axis_index(axis)
    size = array.shape[dim] // 4
    parts = [swap(take(array, (at ^ bits) * size, size, dim), axis, bits) for bits in (1, 2, 3)]
    return (take(array, at * size, size, dim) + parts[0]) + (parts[1] + parts[2])


def packed_scores(capacity, args):
    (
        layer_input,
        gate_pre,
        up_pre,
        grad_rows,
        blocks,
        place,
        down_weight,
        proj_input,
        proj_hidden,
        proj_output,
        proj_gate,
        proj_up,
        rev_slot,
        own_lengths,
    ) = args
    ex_count, slot_len, width_local = layer_input.shape
    hidden_local = gate_pre.shape[2]
    row_total = ex_count * slot_len
    rank_size = proj_input.shape[0]
    rev_pairs = rev_slot.shape[0] // 2
    example_at = lax.axis_index("example")
    tensor_at = lax.axis_index("tensor")
    near, far = example_at % 2, example_at // 2
    half_hidden = hidden_local // 2
    chunks = capacity // (2 * LANES)
    offset = (near * (half_hidden // TILE)).astype(jnp.int32).reshape(1)
    near_at, far_at = near.astype(jnp.int32).reshape(1), far.astype(jnp.int32).reshape(1)
    near_far = jnp.concatenate([near_at, far_at])
    gathered = [lax.all_gather(blocks[k], "tensor", axis=0, tiled=True) for k in range(chunks)]

    tile_count = half_hidden // TILE
    split = tile_count - tile_count // 2
    tile_parts = [(0, split), (split, tile_count - split)]

    def near_pair(rows):
        return rows, swap(rows, "example", 1)

    def run(h, far, own, after):
        return stage(offset, near_far, tile_parts[h], far, own, down_weight, weight_near, after)

    weight_near = swap(down_weight, "example", 1)
    gate_rows = gate_pre.reshape(row_total, hidden_local)
    up_rows = up_pre.reshape(row_total, hidden_local)
    gate_near, up_near = swap(gate_rows, "example", 1), swap(up_rows, "example", 1)
    away = cut(1 - far_at, gathered[0], ())
    inputs_rows = layer_input.reshape(row_total, width_local)
    gate_values = gate_rows.astype(jnp.float32)
    up_values = up_rows.astype(jnp.float32)
    hidden = (gate_values * jax.nn.sigmoid(gate_values) * up_values).astype(jnp.bfloat16)
    early = jnp.concatenate(
        [
            contract(proj_input, inputs_rows),
            contract(proj_hidden, hidden),
            contract(proj_output, grad_rows),
        ]
    )
    def quarter(bits):
        return take(early, (tensor_at ^ bits) * slot_len, slot_len, 1)

    sums = [quarter(0)] + [swap(quarter(bits), "tensor", bits) for bits in (1, 2, 3)]
    far_pair = near_pair(swap(away, "example", 2))
    came, right, after = [], [], ()
    for h, tiles in enumerate(tile_parts):
        results = run(h, far_pair, None, after)
        came.append((swap(results[0], "example", 2), tiles[0]))
        after = (results[0],)
    for k in range(1, chunks):
        before = near_pair(gathered[k - 1])
        if k == 1:
            away = cut(1 - far_at, gathered[1], after)
            far_next = swap(away, "example", 2)
            after = (away, came[0][0])
            gate_packed = pack(chunks, 2 * LANES, half_hidden, offset, place, gate_rows, gate_near, after)
            up_packed = pack(chunks, 2 * LANES, half_hidden, offset, place, up_rows, up_near, after)
            after = (gate_packed[0], up_packed[0])
        far_pair = near_pair(ordered(far_next, after))
        if k + 1 < chunks:
            next_away = cut(1 - far_at, gathered[k + 1], after)
            far_next = swap(next_away, "example", 2)
            after += (next_away,)
        arrived, came = came, []
        for h, tiles in enumerate(tile_parts):
            own = (*before, arrived[h], gate_packed[k - 1], up_packed[k - 1])
            results = run(h, far_pair, (*own, proj_gate, proj_up), after)
            after = (results[0],)
            came.append((swap(results[0], "example", 2), tiles[0]))
            right.append(results[1])
            if (k, h) == (1, 0):
                sums = sum_parts(sums, after)
                after += (sums,)
                in_gate, in_down, out_down = (sums[j * rank_size : (j + 1) * rank_size] for j in range(3))
                in_gate = [in_gate] + [swap(in_gate, "tensor", bits) for bits in (1, 2, 3)]
            if (k, h) == (1, 1):
                in_gate = join_parts(tensor_at.astype(jnp.int32).reshape(1), in_gate, after)
                after += (in_gate,)
                in_gate_near = swap(in_gate, "example", 1)
    before = near_pair(gathered[-1])
    for h, tiles in enumerate(tile_parts):
        own = (*before, came[h], gate_packed[-1], up_packed[-1], proj_gate, proj_up)
        right += run(h, None, own, after)
        after = (right[-1],)
    right = jnp.concatenate([right[k] + right[k + 1] for k in range(0, 2 * chunks, 2)], axis=1)

    slots_here = jnp.concatenate(
        [
            take(rev_slot, example_at * ex_count, ex_count, 0),
            take(rev_slot, (example_at ^ 1) * ex_count, ex_count, 0),
        ]
    )
    table = pairing_table(slots_here, rev_pairs)
    positions = jnp.arange(slot_len, dtype=jnp.int32)
    mask = (positions < take(own_lengths, tensor_at, 1, 0)).astype(jnp.float32)
    sketch_down = contract_exact(in_down * mask[None, :], out_down)
    sketch_down = take(table, tensor_at, 1, 1)[:, :, None] * sketch_down[None, :, :]
    select = jnp.arange(capacity, dtype=jnp.int32)[:, None] == place
    in_gate = jnp.concatenate([in_gate, in_gate_near], axis=1)
    in_gate = contract_exact(in_gate, select.astype(jnp.float32))
    table_rows = contract(
        jnp.repeat(table, slot_len, axis=1).astype(jnp.bfloat16), select.astype(jnp.bfloat16)
    )
    left = (table_rows[:, None, :] * in_gate[None, :, :]).reshape(rev_pairs * rank_size, capacity)
    sketch_late = contract_exact(left, right).reshape(rev_pairs, rank_size, 2 * rank_size)
    return jnp.concatenate([sketch_late, sketch_down], axis=2)


def local_four(
    layer_input,
    gate_pre,
    up_pre,
    output_grad,
    down_weight,
    proj_input,
    proj_hidden,
    proj_output,
    proj_gate,
    proj_up,
    query_sketches,
    rev_lengths,
    rev_slot,
    query_slot,
):
    ex_count, slot_len, width_local = layer_input.shape
    row_total = ex_count * slot_len
    grad_rows = output_grad.reshape(row_total, width_local)
    grad_near = swap(grad_rows, "example", 1)
    others = [swap(rev_lengths, "example", bits) for bits in (1, 2, 3)]

    near = lax.axis_index("example") % 2
    both_lengths = jnp.concatenate([rev_lengths, others[0]])
    own_begin = near * jnp.sum(others[0])
    near_begin = (1 - near) * jnp.sum(rev_lengths)
    offsets = jnp.concatenate(
        [
            own_begin + jnp.cumsum(rev_lengths) - rev_lengths,
            near_begin + jnp.cumsum(others[0]) - others[0],
        ]
    )
    positions = jnp.arange(slot_len, dtype=jnp.int32)
    place = (offsets[:, None] + positions[None, :]) ^ (near * LANES)
    place = jnp.where(positions[None, :] < both_lengths[:, None], place, -1).reshape(1, 2 * row_total)
    no_offset = jnp.zeros((1,), jnp.int32)
    full = 2 * row_total
    blocks = pack(full // (2 * LANES), LANES, width_local, no_offset, place, grad_rows, grad_near)
    sums = jnp.stack([jnp.sum(rev_lengths) + jnp.sum(others[0]), jnp.sum(others[1]) + jnp.sum(others[2])])
    most = jnp.max(sums).reshape(1)
    count = lax.axis_size("group")
    for step in range(1, count):
        shifted = lax.ppermute(most, "group", [(i, (i + step) % count) for i in range(count)])
        most = jnp.maximum(most, shifted)
    levels = [level for level in LEVELS if level < full] + [full]
    branch = jnp.sum((most[0] > jnp.array(levels[:-1], jnp.int32)).astype(jnp.int32))
    sketch = lax.switch(
        branch,
        [functools.partial(packed_scores, level) for level in levels],
        (
            layer_input,
            gate_pre,
            up_pre,
            grad_rows,
            blocks,
            place,
            down_weight,
            proj_input,
            proj_hidden,
            proj_output,
            proj_gate,
            proj_up,
            rev_slot,
            rev_lengths,
        ),
    )
    rank_size = proj_input.shape[0]
    rev_pairs = rev_slot.shape[0] // 2
    revision_pairs = sum_over(scatter_over(sketch, "tensor", 1), "example")
    example_scores = contract_exact(
        revision_pairs.reshape(rev_pairs, -1), query_sketches.astype(jnp.float32)
    )
    query_pairs = query_slot.shape[0] * 4 // 2
    pair_terms = contract_exact(example_scores, pairing_table(query_slot, query_pairs))
    total = sum_over(scatter_over(pair_terms, "example", 1), "tensor")
    return total / jnp.float32(rank_size * rank_size)


def local_any(
    layer_input,
    gate_pre,
    up_pre,
    output_grad,
    down_weight,
    proj_input,
    proj_hidden,
    proj_output,
    proj_gate,
    proj_up,
    query_sketches,
    rev_lengths,
    rev_slot,
    query_slot,
):
    ex_count, slot_len, width_local = layer_input.shape
    hidden_local = gate_pre.shape[2]
    row_total = ex_count * slot_len
    rank_size = proj_input.shape[0]
    per_rank = rank_size // lax.axis_size("tensor")
    inputs_rows = layer_input.reshape(row_total, width_local)
    grad_rows = output_grad.reshape(row_total, width_local)
    gate_values = gate_pre.reshape(row_total, hidden_local).astype(jnp.float32)
    up_values = up_pre.reshape(row_total, hidden_local).astype(jnp.float32)
    grad_full = lax.all_gather(grad_rows, "tensor", axis=1, tiled=True)
    hidden_grad = contract(grad_full, lax.all_gather(down_weight, "example", axis=1, tiled=True))
    hidden_grad = lax.optimization_barrier(hidden_grad.astype(jnp.bfloat16)).astype(jnp.float32)
    sigma = jax.nn.sigmoid(gate_values)
    active = gate_values * sigma
    hidden = (active * up_values).astype(jnp.bfloat16)
    grad_up = (hidden_grad * active).astype(jnp.bfloat16)
    grad_gate = (hidden_grad * up_values * sigma * (1.0 + gate_values * (1.0 - sigma))).astype(
        jnp.bfloat16
    )
    partials = jnp.stack(
        [
            contract(inputs_rows, proj_input),
            contract(hidden, proj_hidden),
            contract(grad_gate, proj_gate),
            contract(grad_up, proj_up),
            contract(grad_rows, proj_output),
        ]
    )
    summed = lax.psum(partials, "tensor")
    begin = lax.axis_index("tensor") * per_rank
    left = lax.dynamic_slice_in_dim(summed[:2], begin, per_rank, 2)
    right = summed[2:]
    positions = jnp.arange(slot_len, dtype=jnp.int32)
    mask = (positions[None, :] < rev_lengths[:, None]).astype(jnp.float32).reshape(row_total)
    left = left * mask[None, :, None]
    left = jnp.stack([left[0], left[0], left[1]]).reshape(3, ex_count, slot_len, per_rank)
    right = right.reshape(3, ex_count, slot_len, rank_size)
    sketches = jnp.einsum("meti,metj->eimj", left, right, precision=lax.Precision.HIGHEST).reshape(
        ex_count, per_rank * 3 * rank_size
    )
    every_sketch = lax.all_gather(sketches, "example", axis=0, tiled=True)
    rev_pairs = rev_slot.shape[0] // 2
    revision_pairs = jnp.dot(
        pairing_table(rev_slot, rev_pairs), every_sketch, precision=lax.Precision.HIGHEST
    )
    example_scores = contract_exact(revision_pairs, query_sketches.astype(jnp.float32))
    query_pairs = query_slot.shape[0] * lax.axis_size("example") // 2
    pair_terms = contract_exact(example_scores, pairing_table(query_slot, query_pairs))
    owned = lax.psum_scatter(pair_terms, "example", scatter_dimension=1, tiled=True)
    total = lax.psum(owned, "tensor")
    return total / jnp.float32(rank_size * rank_size)


def solution(mesh):
    four = mesh.shape["tensor"] == 4 and mesh.shape["example"] == 4
    return jax.shard_map(
        local_four if four else local_any,
        mesh=mesh,
        in_specs=(
            P(("group", "example"), None, "tensor"),
            P(("group", "example"), None, "tensor"),
            P(("group", "example"), None, "tensor"),
            P(("group", "example"), None, "tensor"),
            P("tensor", "example"),
            P(None, "tensor"),
            P(None, "tensor"),
            P(None, "tensor"),
            P(None, "tensor"),
            P(None, "tensor"),
            P(("group", "example"), "tensor"),
            P(("group", "example")),
            P("group"),
            P(("group", "example")),
        ),
        out_specs=P("group", "example"),
        check_vma=False,
    )
```

```python
import functools

import jax
import jax.numpy as jnp
from jax import lax
from jax.experimental import pallas as pl
from jax.experimental.pallas import tpu as pltpu
from jax.sharding import PartitionSpec as P

LEVELS = (768,)
TILE = 512
STEP = 256
LANES = 128
VMEM_LIMIT = 58 * 1024 * 1024


def contract(left_side, right_side):
    return lax.dot_general(
        left_side, right_side, (((1,), (1,)), ((), ())), preferred_element_type=jnp.float32
    )


def contract_exact(left_side, right_side):
    return lax.dot_general(
        left_side,
        right_side,
        (((1,), (1,)), ((), ())),
        precision=lax.Precision.HIGHEST,
        preferred_element_type=jnp.float32,
    )


def pairing_table(slots, pairs):
    pair_index = slots // 2
    signs = (1 - 2 * (slots % 2)).astype(jnp.float32)
    targets = jnp.arange(pairs, dtype=jnp.int32)
    return jnp.where(targets[:, None] == pair_index[None, :], signs[None, :], jnp.float32(0.0))


def take(array, start, size, axis):
    return lax.dynamic_slice_in_dim(array, start, size, axis)


def swap(array, axis, bits):
    count = lax.axis_size(axis)
    return lax.ppermute(array, axis, [(i, i ^ bits) for i in range(count)])


def chain_pairs(rule):
    pairs = []
    for t in range(4):
        for e in range(4):
            goal = rule(3 - t if e // 2 else t, e // 2, e % 2)
            if goal is not None:
                order, far, near = goal
                pairs.append((t * 4 + e, (3 - order if far else order) * 4 + 2 * far + near))
    return pairs


CROSS = chain_pairs(lambda order, far, near: (3 - order, 1 - far, near) if order >= 2 else None)
SPREAD = chain_pairs(lambda order, far, near: (order + 2, far, near) if order < 2 else None)


def move(array, pairs):
    return lax.ppermute(array, ("tensor", "example"), pairs)


def kernel_params():
    return pltpu.CompilerParams(vmem_limit_bytes=VMEM_LIMIT)


def pack_kernel(size, count, near_ref, place_ref, own_ref, other_ref, *refs):
    outs, select = refs[-1 - count : -1], refs[-1]
    rows_own = own_ref.shape[0]

    @pl.when(pl.program_id(0) == 0)
    def _():
        @pl.loop(0, count)
        def _(c):
            at = lax.broadcasted_iota(jnp.int32, (size, select.shape[1]), 0) + c * 2 * LANES
            chosen = jnp.where(at == place_ref[...], 1.0, 0.0).astype(jnp.bfloat16)
            select[pl.ds(pl.multiple_of(c * size, size), size), :] = chosen

    for c in range(count):
        rows = slice(c * size, (c + 1) * size)
        total = jnp.dot(select[rows, :rows_own], own_ref[...], preferred_element_type=jnp.float32)
        total += jnp.dot(select[rows, rows_own:], other_ref[...], preferred_element_type=jnp.float32)
        outs[c][...] = total.astype(jnp.bfloat16).T


def pack(count, size, columns, near_offset, place, own, other, after=()):
    rows = own.shape[0]
    total = count * size
    return pl.pallas_call(
        functools.partial(pack_kernel, size, count),
        grid_spec=pltpu.PrefetchScalarGridSpec(
            num_scalar_prefetch=1,
            grid=(columns // TILE,),
            in_specs=[
                pl.BlockSpec((1, 2 * rows), lambda i, near: (0, 0)),
                pl.BlockSpec((rows, TILE), lambda i, near: (0, near[0] + i)),
                pl.BlockSpec((rows, TILE), lambda i, near: (0, near[0] + i)),
            ]
            + [pl.BlockSpec(memory_space=pl.ANY)] * len(after),
            out_specs=[pl.BlockSpec((TILE, size), lambda i, near: (i, 0))] * count,
            scratch_shapes=[pltpu.VMEM((total, 2 * rows), jnp.bfloat16)],
        ),
        out_shape=[jax.ShapeDtypeStruct((columns, size), jnp.bfloat16)] * count,
        compiler_params=kernel_params(),
        cost_estimate=pl.CostEstimate(
            flops=4 * total * rows * columns,
            bytes_accessed=(4 * rows + 2 * total) * columns,
            transcendentals=0,
        ),
        name="pack_rows",
    )(near_offset, place, own, other, *after)


def cut_kernel(at_ref, source, *refs):
    refs[-1][...] = source[...]


def cut(at, gathered, after):
    columns, rows = gathered.shape
    block = columns // 8
    return pl.pallas_call(
        cut_kernel,
        grid_spec=pltpu.PrefetchScalarGridSpec(
            num_scalar_prefetch=1,
            grid=(4,),
            in_specs=[pl.BlockSpec((block, rows), lambda i, at: (4 * at[0] + i, 0))]
            + [pl.BlockSpec(memory_space=pl.ANY)] * len(after),
            out_specs=pl.BlockSpec((block, rows), lambda i, at: (i, 0)),
        ),
        out_shape=jax.ShapeDtypeStruct((columns // 2, rows), gathered.dtype),
        compiler_params=kernel_params(),
        cost_estimate=pl.CostEstimate(flops=0, bytes_accessed=2 * columns * rows, transcendentals=0),
        name="cut_columns",
    )(at, gathered, *after)


def gate_kernel(value, *refs):
    refs[-1][...] = value[...]


def ordered(value, after):
    return pl.pallas_call(
        gate_kernel,
        in_specs=[pl.BlockSpec(memory_space=pltpu.VMEM)]
        + [pl.BlockSpec(memory_space=pl.ANY)] * len(after),
        out_specs=pl.BlockSpec(memory_space=pltpu.VMEM),
        out_shape=jax.ShapeDtypeStruct(value.shape, value.dtype),
        compiler_params=kernel_params(),
        name="ordered_copy",
    )(value, *after)


def sum_kernel(a, b, c, d, *refs):
    refs[-1][...] = (a[...] + b[...]) + (c[...] + d[...])


def sum_parts(parts, after):
    return pl.pallas_call(
        sum_kernel,
        in_specs=[pl.BlockSpec(memory_space=pltpu.VMEM)] * 4
        + [pl.BlockSpec(memory_space=pl.ANY)] * len(after),
        out_specs=pl.BlockSpec(memory_space=pltpu.VMEM),
        out_shape=jax.ShapeDtypeStruct(parts[0].shape, parts[0].dtype),
        compiler_params=kernel_params(),
        name="sum_parts",
    )(*parts, *after)


def join_kernel(at_ref, a, b, c, d, *refs):
    out = refs[-1]
    size = a.shape[1]
    for bits, part in enumerate((a, b, c, d)):
        begin = pl.multiple_of((at_ref[0] ^ bits) * size, size)
        out[:, pl.ds(begin, size)] = part[...]


def join_parts(at, parts, after):
    rows, size = parts[0].shape
    return pl.pallas_call(
        join_kernel,
        in_specs=[pl.BlockSpec(memory_space=pltpu.SMEM)]
        + [pl.BlockSpec(memory_space=pltpu.VMEM)] * 4
        + [pl.BlockSpec(memory_space=pl.ANY)] * len(after),
        out_specs=pl.BlockSpec(memory_space=pltpu.VMEM),
        out_shape=jax.ShapeDtypeStruct((rows, 4 * size), parts[0].dtype),
        compiler_params=kernel_params(),
        name="join_parts",
    )(at, *parts, *after)


def halves_kernel(a, b, *refs):
    keep, send = refs[-2:]
    half = a.shape[0] // 2
    keep[:half, :], keep[half:, :] = a[:half, :], b[:half, :]
    send[:half, :], send[half:, :] = a[half:, :], b[half:, :]


def pair_halves(a, b, after):
    shape = jax.ShapeDtypeStruct(a.shape, a.dtype)
    return pl.pallas_call(
        halves_kernel,
        in_specs=[pl.BlockSpec(memory_space=pltpu.VMEM)] * 2
        + [pl.BlockSpec(memory_space=pl.ANY)] * len(after),
        out_specs=[pl.BlockSpec(memory_space=pltpu.VMEM)] * 2,
        out_shape=[shape, shape],
        compiler_params=kernel_params(),
        name="pair_halves",
    )(a, b, *after)


def stage_kernel(far, own, offset_ref, near_ref, *refs):
    refs = list(refs)
    weights = [refs.pop(0) for _ in range(4)]
    far_ins = [refs.pop(0) for _ in range(8 * far)]
    own_ins = [refs.pop(0) for _ in range(8 * own)]
    extra = [refs.pop(0) for _ in range(5 * own)]
    own_right = refs.pop() if own else None
    far_right = refs.pop() if far else None
    out = refs.pop() if own else None
    far_out = refs.pop() if far else None
    depth = weights[0].shape[1]

    def join(ins, right):
        for block in range(4):
            for k in range(2):
                right[block * depth : (block + 1) * depth, k * LANES : (k + 1) * LANES] = ins[2 * block + k][...]

    def half_sum(rows, right):
        total = 0.0
        for k in range(4):
            block = right[k * depth : (k + 1) * depth, :]
            total += jnp.dot(weights[k][rows, :], block, preferred_element_type=jnp.float32)
        return total

    @pl.when(pl.program_id(0) == 0)
    def _():
        if far:
            join(far_ins, far_right)
        if own:
            join(own_ins, own_right)
            out[...] = jnp.zeros_like(out)

    @pl.loop(0, TILE // STEP)
    def _(r):
        rows = pl.ds(pl.multiple_of(r * STEP, STEP), STEP)
        if far:
            far_out[rows, :] = half_sum(rows, far_right).astype(jnp.bfloat16)
        if own:
            came, gate_ref, up_ref, proj_gate, proj_up = extra
            rank_size = proj_gate.shape[0]
            total = half_sum(rows, own_right)
            hidden_grad = (total + came[rows, :].astype(jnp.float32)).astype(jnp.bfloat16)
            hidden_grad = hidden_grad.astype(jnp.float32)
            gate = gate_ref[rows, :].astype(jnp.float32)
            up = up_ref[rows, :].astype(jnp.float32)
            sigma = jax.nn.sigmoid(gate)
            grad_up = (hidden_grad * (gate * sigma)).astype(jnp.bfloat16)
            grad_gate = (hidden_grad * up * sigma * (1.0 + gate * (1.0 - sigma))).astype(jnp.bfloat16)
            out[:rank_size, :] += jnp.dot(proj_gate[:, rows], grad_gate, preferred_element_type=jnp.float32)
            out[rank_size:, :] += jnp.dot(proj_up[:, rows], grad_up, preferred_element_type=jnp.float32)


def side_of(near, side):
    return near[0] + side * (1 - 2 * near[0])


def in_half(side, part, near):
    return 2 * side_of(near, side) + part


def in_whole(side, part, near):
    return 4 * near[1] + 2 * side_of(near, side) + part


def in_spread(rows, side, part, near):
    half = near[1] + part * (1 - 2 * near[1])
    return 4 * half + 2 * side_of(near, side) + rows


def stage(near_offset, near, tiles, far, own, weight, weight_near, after):
    begin, count = tiles
    width = weight_near.shape[1]
    depth = width // 2
    both = 2 * LANES
    arrays, specs, outs, shapes, rights = [], [], [], [], []

    def add(array, block, index):
        arrays.append(array)
        specs.append(pl.BlockSpec(block, index))

    for k in range(2):
        add(weight, (TILE, depth), lambda i, offset, near, k=k: (offset[0] + begin + i, k))
    for k in range(2):
        add(weight_near, (TILE, depth), lambda i, offset, near, k=k: (offset[0] + begin + i, k))
    for rows in (far, own):
        if rows is not None:
            rights.append(pltpu.VMEM((2 * width, both), jnp.bfloat16))
            for block in range(4):
                for k in range(2):
                    index = functools.partial(rows[2], *divmod(block, 2))
                    add(rows[k], (depth, LANES), lambda i, offset, near, index=index: (index(near), 0))
    if far is not None:
        outs.append(pl.BlockSpec((TILE, both), lambda i, offset, near: (i, 0)))
        shapes.append(jax.ShapeDtypeStruct((count * TILE, both), jnp.bfloat16))
    if own is not None:
        (came, first), gate, up, proj_gate, proj_up = own[3:]
        rank_size = proj_gate.shape[0]
        add(came, (TILE, both), lambda i, offset, near: (begin - first + i, 0))
        for array in (gate, up):
            add(array, (TILE, both), lambda i, offset, near: (begin + i, 0))
        for array in (proj_gate, proj_up):
            add(array, (rank_size, TILE), lambda i, offset, near: (0, offset[0] + begin + i))
        outs.append(pl.BlockSpec((2 * rank_size, both), lambda i, offset, near: (0, 0)))
        shapes.append(jax.ShapeDtypeStruct((2 * rank_size, both), jnp.float32))
    parts = len(rights)
    return pl.pallas_call(
        functools.partial(stage_kernel, far is not None, own is not None),
        grid_spec=pltpu.PrefetchScalarGridSpec(
            num_scalar_prefetch=2,
            grid=(count,),
            in_specs=specs + [pl.BlockSpec(memory_space=pl.ANY)] * len(after),
            out_specs=outs,
            scratch_shapes=rights,
        ),
        out_shape=shapes,
        compiler_params=kernel_params(),
        cost_estimate=pl.CostEstimate(
            flops=4 * parts * both * width * count * TILE,
            bytes_accessed=4 * width * count * TILE + 4 * parts * both * count * TILE,
            transcendentals=0,
        ),
        name="stage",
    )(near_offset, near, *arrays, *after)


def sum_over(array, axis):
    parts = [swap(array, axis, bits) for bits in (1, 2, 3)]
    return (array + parts[0]) + (parts[1] + parts[2])


def scatter_over(array, axis, dim):
    at = lax.axis_index(axis)
    size = array.shape[dim] // 4
    parts = [swap(take(array, (at ^ bits) * size, size, dim), axis, bits) for bits in (1, 2, 3)]
    return (take(array, at * size, size, dim) + parts[0]) + (parts[1] + parts[2])


def packed_scores(capacity, args):
    (
        layer_input,
        gate_pre,
        up_pre,
        grad_rows,
        blocks,
        place,
        down_weight,
        proj_input,
        proj_hidden,
        proj_output,
        proj_gate,
        proj_up,
        rev_slot,
        own_lengths,
    ) = args
    ex_count, slot_len, width_local = layer_input.shape
    hidden_local = gate_pre.shape[2]
    row_total = ex_count * slot_len
    rank_size = proj_input.shape[0]
    rev_pairs = rev_slot.shape[0] // 2
    example_at = lax.axis_index("example")
    tensor_at = lax.axis_index("tensor")
    near, far = example_at % 2, example_at // 2
    half_hidden = hidden_local // 2
    chunks = capacity // (2 * LANES)
    offset = (near * (half_hidden // TILE)).astype(jnp.int32).reshape(1)
    near_at, far_at = near.astype(jnp.int32).reshape(1), far.astype(jnp.int32).reshape(1)
    near_far = jnp.concatenate([near_at, far_at])
    gathered = [lax.all_gather(blocks[k], "tensor", axis=0, tiled=True) for k in range(2)]

    tile_count = half_hidden // TILE
    split = tile_count - tile_count // 2
    tile_parts = [(0, split), (split, tile_count - split)]

    def near_pair(rows, index):
        return rows, swap(rows, "example", 1), index

    def run(h, far, own, after):
        return stage(offset, near_far, tile_parts[h], far, own, down_weight, weight_near, after)

    weight_near = swap(down_weight, "example", 1)
    gate_rows = gate_pre.reshape(row_total, hidden_local)
    up_rows = up_pre.reshape(row_total, hidden_local)
    gate_near, up_near = swap(gate_rows, "example", 1), swap(up_rows, "example", 1)
    crossed = [move(blocks[k], CROSS) for k in range(2, chunks)]
    away = cut(1 - far_at, gathered[0], crossed)
    inputs_rows = layer_input.reshape(row_total, width_local)
    gate_values = gate_rows.astype(jnp.float32)
    up_values = up_rows.astype(jnp.float32)
    hidden = (gate_values * jax.nn.sigmoid(gate_values) * up_values).astype(jnp.bfloat16)
    early = jnp.concatenate(
        [
            contract(proj_input, inputs_rows),
            contract(proj_hidden, hidden),
            contract(proj_output, grad_rows),
        ]
    )
    def quarter(bits):
        return take(early, (tensor_at ^ bits) * slot_len, slot_len, 1)

    sums = [quarter(0)] + [swap(quarter(bits), "tensor", bits) for bits in (1, 2, 3)]
    far_pair = near_pair(swap(away, "example", 2), in_half)

    order = jnp.where(far == 1, 3 - tensor_at, tensor_at)
    shards = []
    for k in range(2, chunks):
        keep, send = pair_halves(blocks[k], crossed[k - 2], (away,))
        shards.append(jnp.where(order < 2, keep, move(send, SPREAD)))
    gathered += [lax.all_gather(shard, "tensor", axis=0, tiled=True) for shard in shards]

    came, right, after = [], [], ()
    for h, tiles in enumerate(tile_parts):
        if h == 1:
            after += tuple(shards)
        results = run(h, far_pair, None, after)
        came.append((swap(results[0], "example", 2), tiles[0]))
        after = (results[0],)
    before = near_pair(gathered[0], in_whole)
    for k in range(1, chunks):
        if k == 1:
            away = cut(1 - far_at, gathered[1], after)
            far_next = swap(away, "example", 2)
            after = (away, came[0][0])
            gate_packed = pack(chunks, 2 * LANES, half_hidden, offset, place, gate_rows, gate_near, after)
            up_packed = pack(chunks, 2 * LANES, half_hidden, offset, place, up_rows, up_near, after)
            after = (gate_packed[0], up_packed[0])
            far_pair = near_pair(ordered(far_next, after), in_half)
            own_pair = near_pair(gathered[1], in_whole)
        else:
            both = near_pair(gathered[k], None)[:2]
            far_pair = (*both, functools.partial(in_spread, 1))
            own_pair = (*both, functools.partial(in_spread, 0))
        arrived, came = came, []
        for h, tiles in enumerate(tile_parts):
            own = (*before, arrived[h], gate_packed[k - 1], up_packed[k - 1])
            results = run(h, far_pair, (*own, proj_gate, proj_up), after)
            after = (results[0],)
            came.append((swap(results[0], "example", 2), tiles[0]))
            right.append(results[1])
            if (k, h) == (1, 0):
                sums = sum_parts(sums, after)
                after += (sums,)
                in_gate, in_down, out_down = (sums[j * rank_size : (j + 1) * rank_size] for j in range(3))
                in_gate = [in_gate] + [swap(in_gate, "tensor", bits) for bits in (1, 2, 3)]
            if (k, h) == (1, 1):
                in_gate = join_parts(tensor_at.astype(jnp.int32).reshape(1), in_gate, (*after, came[0][0]))
                after += (in_gate,)
                in_gate_near = swap(in_gate, "example", 1)
        before = own_pair
    for h, tiles in enumerate(tile_parts):
        own = (*before, came[h], gate_packed[-1], up_packed[-1], proj_gate, proj_up)
        right += run(h, None, own, after)
        after = (right[-1],)
    right = jnp.concatenate([right[k] + right[k + 1] for k in range(0, 2 * chunks, 2)], axis=1)

    slots_here = jnp.concatenate(
        [
            take(rev_slot, example_at * ex_count, ex_count, 0),
            take(rev_slot, (example_at ^ 1) * ex_count, ex_count, 0),
        ]
    )
    table = pairing_table(slots_here, rev_pairs)
    positions = jnp.arange(slot_len, dtype=jnp.int32)
    mask = (positions < take(own_lengths, tensor_at, 1, 0)).astype(jnp.float32)
    sketch_down = contract_exact(in_down * mask[None, :], out_down)
    sketch_down = take(table, tensor_at, 1, 1)[:, :, None] * sketch_down[None, :, :]
    select = jnp.arange(capacity, dtype=jnp.int32)[:, None] == place
    in_gate = jnp.concatenate([in_gate, in_gate_near], axis=1)
    in_gate = contract_exact(in_gate, select.astype(jnp.float32))
    table_rows = contract(
        jnp.repeat(table, slot_len, axis=1).astype(jnp.bfloat16), select.astype(jnp.bfloat16)
    )
    left = (table_rows[:, None, :] * in_gate[None, :, :]).reshape(rev_pairs * rank_size, capacity)
    sketch_late = contract_exact(left, right).reshape(rev_pairs, rank_size, 2 * rank_size)
    return jnp.concatenate([sketch_late, sketch_down], axis=2)


def local_four(
    layer_input,
    gate_pre,
    up_pre,
    output_grad,
    down_weight,
    proj_input,
    proj_hidden,
    proj_output,
    proj_gate,
    proj_up,
    query_sketches,
    rev_lengths,
    rev_slot,
    query_slot,
):
    ex_count, slot_len, width_local = layer_input.shape
    row_total = ex_count * slot_len
    grad_rows = output_grad.reshape(row_total, width_local)
    grad_near = swap(grad_rows, "example", 1)
    others = [swap(rev_lengths, "example", bits) for bits in (1, 2, 3)]

    near = lax.axis_index("example") % 2
    both_lengths = jnp.concatenate([rev_lengths, others[0]])
    own_begin = near * jnp.sum(others[0])
    near_begin = (1 - near) * jnp.sum(rev_lengths)
    offsets = jnp.concatenate(
        [
            own_begin + jnp.cumsum(rev_lengths) - rev_lengths,
            near_begin + jnp.cumsum(others[0]) - others[0],
        ]
    )
    positions = jnp.arange(slot_len, dtype=jnp.int32)
    place = (offsets[:, None] + positions[None, :]) ^ (near * LANES)
    place = jnp.where(positions[None, :] < both_lengths[:, None], place, -1).reshape(1, 2 * row_total)
    no_offset = jnp.zeros((1,), jnp.int32)
    full = 2 * row_total
    blocks = pack(full // (2 * LANES), LANES, width_local, no_offset, place, grad_rows, grad_near)
    sums = jnp.stack([jnp.sum(rev_lengths) + jnp.sum(others[0]), jnp.sum(others[1]) + jnp.sum(others[2])])
    most = jnp.max(sums).reshape(1)
    count = lax.axis_size("group")
    for step in range(1, count):
        shifted = lax.ppermute(most, "group", [(i, (i + step) % count) for i in range(count)])
        most = jnp.maximum(most, shifted)
    levels = [level for level in LEVELS if level < full] + [full]
    branch = jnp.sum((most[0] > jnp.array(levels[:-1], jnp.int32)).astype(jnp.int32))
    sketch = lax.switch(
        branch,
        [functools.partial(packed_scores, level) for level in levels],
        (
            layer_input,
            gate_pre,
            up_pre,
            grad_rows,
            blocks,
            place,
            down_weight,
            proj_input,
            proj_hidden,
            proj_output,
            proj_gate,
            proj_up,
            rev_slot,
            rev_lengths,
        ),
    )
    rank_size = proj_input.shape[0]
    rev_pairs = rev_slot.shape[0] // 2
    revision_pairs = sum_over(scatter_over(sketch, "tensor", 1), "example")
    example_scores = contract_exact(
        revision_pairs.reshape(rev_pairs, -1), query_sketches.astype(jnp.float32)
    )
    query_pairs = query_slot.shape[0] * 4 // 2
    pair_terms = contract_exact(example_scores, pairing_table(query_slot, query_pairs))
    total = sum_over(scatter_over(pair_terms, "example", 1), "tensor")
    return total / jnp.float32(rank_size * rank_size)


def local_any(
    layer_input,
    gate_pre,
    up_pre,
    output_grad,
    down_weight,
    proj_input,
    proj_hidden,
    proj_output,
    proj_gate,
    proj_up,
    query_sketches,
    rev_lengths,
    rev_slot,
    query_slot,
):
    ex_count, slot_len, width_local = layer_input.shape
    hidden_local = gate_pre.shape[2]
    row_total = ex_count * slot_len
    rank_size = proj_input.shape[0]
    per_rank = rank_size // lax.axis_size("tensor")
    inputs_rows = layer_input.reshape(row_total, width_local)
    grad_rows = output_grad.reshape(row_total, width_local)
    gate_values = gate_pre.reshape(row_total, hidden_local).astype(jnp.float32)
    up_values = up_pre.reshape(row_total, hidden_local).astype(jnp.float32)
    grad_full = lax.all_gather(grad_rows, "tensor", axis=1, tiled=True)
    hidden_grad = contract(grad_full, lax.all_gather(down_weight, "example", axis=1, tiled=True))
    hidden_grad = lax.optimization_barrier(hidden_grad.astype(jnp.bfloat16)).astype(jnp.float32)
    sigma = jax.nn.sigmoid(gate_values)
    active = gate_values * sigma
    hidden = (active * up_values).astype(jnp.bfloat16)
    grad_up = (hidden_grad * active).astype(jnp.bfloat16)
    grad_gate = (hidden_grad * up_values * sigma * (1.0 + gate_values * (1.0 - sigma))).astype(
        jnp.bfloat16
    )
    partials = jnp.stack(
        [
            contract(inputs_rows, proj_input),
            contract(hidden, proj_hidden),
            contract(grad_gate, proj_gate),
            contract(grad_up, proj_up),
            contract(grad_rows, proj_output),
        ]
    )
    summed = lax.psum(partials, "tensor")
    begin = lax.axis_index("tensor") * per_rank
    left = lax.dynamic_slice_in_dim(summed[:2], begin, per_rank, 2)
    right = summed[2:]
    positions = jnp.arange(slot_len, dtype=jnp.int32)
    mask = (positions[None, :] < rev_lengths[:, None]).astype(jnp.float32).reshape(row_total)
    left = left * mask[None, :, None]
    left = jnp.stack([left[0], left[0], left[1]]).reshape(3, ex_count, slot_len, per_rank)
    right = right.reshape(3, ex_count, slot_len, rank_size)
    sketches = jnp.einsum("meti,metj->eimj", left, right, precision=lax.Precision.HIGHEST).reshape(
        ex_count, per_rank * 3 * rank_size
    )
    every_sketch = lax.all_gather(sketches, "example", axis=0, tiled=True)
    rev_pairs = rev_slot.shape[0] // 2
    revision_pairs = jnp.dot(
        pairing_table(rev_slot, rev_pairs), every_sketch, precision=lax.Precision.HIGHEST
    )
    example_scores = contract_exact(revision_pairs, query_sketches.astype(jnp.float32))
    query_pairs = query_slot.shape[0] * lax.axis_size("example") // 2
    pair_terms = contract_exact(example_scores, pairing_table(query_slot, query_pairs))
    owned = lax.psum_scatter(pair_terms, "example", scatter_dimension=1, tiled=True)
    total = lax.psum(owned, "tensor")
    return total / jnp.float32(rank_size * rank_size)


def solution(mesh):
    four = mesh.shape["tensor"] == 4 and mesh.shape["example"] == 4
    return jax.shard_map(
        local_four if four else local_any,
        mesh=mesh,
        in_specs=(
            P(("group", "example"), None, "tensor"),
            P(("group", "example"), None, "tensor"),
            P(("group", "example"), None, "tensor"),
            P(("group", "example"), None, "tensor"),
            P("tensor", "example"),
            P(None, "tensor"),
            P(None, "tensor"),
            P(None, "tensor"),
            P(None, "tensor"),
            P(None, "tensor"),
            P(("group", "example"), "tensor"),
            P(("group", "example")),
            P("group"),
            P(("group", "example")),
        ),
        out_specs=P("group", "example"),
        check_vma=False,
    )
```

```python
import functools

import jax
import jax.numpy as jnp
from jax import lax
from jax.experimental import pallas as pl
from jax.experimental.pallas import tpu as pltpu
from jax.sharding import PartitionSpec as P

LEVELS = (768,)
TILE = 512
STEP = 256
LANES = 128
VMEM_LIMIT = 58 * 1024 * 1024


def contract(left_side, right_side):
    return lax.dot_general(
        left_side, right_side, (((1,), (1,)), ((), ())), preferred_element_type=jnp.float32
    )


def contract_exact(left_side, right_side):
    return lax.dot_general(
        left_side,
        right_side,
        (((1,), (1,)), ((), ())),
        precision=lax.Precision.HIGHEST,
        preferred_element_type=jnp.float32,
    )


def pairing_table(slots, pairs):
    pair_index = slots // 2
    signs = (1 - 2 * (slots % 2)).astype(jnp.float32)
    targets = jnp.arange(pairs, dtype=jnp.int32)
    return jnp.where(targets[:, None] == pair_index[None, :], signs[None, :], jnp.float32(0.0))


def take(array, start, size, axis):
    return lax.dynamic_slice_in_dim(array, start, size, axis)


def swap(array, axis, bits):
    count = lax.axis_size(axis)
    return lax.ppermute(array, axis, [(i, i ^ bits) for i in range(count)])


def chain_pairs(rule):
    pairs = []
    for t in range(4):
        for e in range(4):
            goal = rule(3 - t if e // 2 else t, e // 2, e % 2)
            if goal is not None:
                order, far, near = goal
                pairs.append((t * 4 + e, (3 - order if far else order) * 4 + 2 * far + near))
    return pairs


CROSS = chain_pairs(lambda order, far, near: (3 - order, 1 - far, near) if order >= 2 else None)
SPREAD = chain_pairs(lambda order, far, near: (order + 2, far, near) if order < 2 else None)


def move(array, pairs):
    return lax.ppermute(array, ("tensor", "example"), pairs)


def kernel_params():
    return pltpu.CompilerParams(vmem_limit_bytes=VMEM_LIMIT)


def pack_kernel(size, count, near_ref, place_ref, own_ref, other_ref, *refs):
    outs, select = refs[-1 - count : -1], refs[-1]
    rows_own = own_ref.shape[0]

    @pl.when(pl.program_id(0) == 0)
    def _():
        @pl.loop(0, count)
        def _(c):
            at = lax.broadcasted_iota(jnp.int32, (size, select.shape[1]), 0) + c * 2 * LANES
            chosen = jnp.where(at == place_ref[...], 1.0, 0.0).astype(jnp.bfloat16)
            select[pl.ds(pl.multiple_of(c * size, size), size), :] = chosen

    for c in range(count):
        rows = slice(c * size, (c + 1) * size)
        total = jnp.dot(select[rows, :rows_own], own_ref[...], preferred_element_type=jnp.float32)
        total += jnp.dot(select[rows, rows_own:], other_ref[...], preferred_element_type=jnp.float32)
        outs[c][...] = total.astype(jnp.bfloat16).T


def pack(count, size, columns, near_offset, place, own, other, after=()):
    rows = own.shape[0]
    total = count * size
    return pl.pallas_call(
        functools.partial(pack_kernel, size, count),
        grid_spec=pltpu.PrefetchScalarGridSpec(
            num_scalar_prefetch=1,
            grid=(columns // TILE,),
            in_specs=[
                pl.BlockSpec((1, 2 * rows), lambda i, near: (0, 0)),
                pl.BlockSpec((rows, TILE), lambda i, near: (0, near[0] + i)),
                pl.BlockSpec((rows, TILE), lambda i, near: (0, near[0] + i)),
            ]
            + [pl.BlockSpec(memory_space=pl.ANY)] * len(after),
            out_specs=[pl.BlockSpec((TILE, size), lambda i, near: (i, 0))] * count,
            scratch_shapes=[pltpu.VMEM((total, 2 * rows), jnp.bfloat16)],
        ),
        out_shape=[jax.ShapeDtypeStruct((columns, size), jnp.bfloat16)] * count,
        compiler_params=kernel_params(),
        cost_estimate=pl.CostEstimate(
            flops=4 * total * rows * columns,
            bytes_accessed=(4 * rows + 2 * total) * columns,
            transcendentals=0,
        ),
        name="pack_rows",
    )(near_offset, place, own, other, *after)


def cut_kernel(at_ref, source, *refs):
    refs[-1][...] = source[...]


def cut(at, gathered, after):
    columns, rows = gathered.shape
    block = columns // 8
    return pl.pallas_call(
        cut_kernel,
        grid_spec=pltpu.PrefetchScalarGridSpec(
            num_scalar_prefetch=1,
            grid=(4,),
            in_specs=[pl.BlockSpec((block, rows), lambda i, at: (4 * at[0] + i, 0))]
            + [pl.BlockSpec(memory_space=pl.ANY)] * len(after),
            out_specs=pl.BlockSpec((block, rows), lambda i, at: (i, 0)),
        ),
        out_shape=jax.ShapeDtypeStruct((columns // 2, rows), gathered.dtype),
        compiler_params=kernel_params(),
        cost_estimate=pl.CostEstimate(flops=0, bytes_accessed=2 * columns * rows, transcendentals=0),
        name="cut_columns",
    )(at, gathered, *after)


def gate_kernel(value, *refs):
    refs[-1][...] = value[...]


def ordered(value, after):
    return pl.pallas_call(
        gate_kernel,
        in_specs=[pl.BlockSpec(memory_space=pltpu.VMEM)]
        + [pl.BlockSpec(memory_space=pl.ANY)] * len(after),
        out_specs=pl.BlockSpec(memory_space=pltpu.VMEM),
        out_shape=jax.ShapeDtypeStruct(value.shape, value.dtype),
        compiler_params=kernel_params(),
        name="ordered_copy",
    )(value, *after)


def sum_kernel(a, b, c, d, *refs):
    refs[-1][...] = (a[...] + b[...]) + (c[...] + d[...])


def sum_parts(parts, after):
    return pl.pallas_call(
        sum_kernel,
        in_specs=[pl.BlockSpec(memory_space=pltpu.VMEM)] * 4
        + [pl.BlockSpec(memory_space=pl.ANY)] * len(after),
        out_specs=pl.BlockSpec(memory_space=pltpu.VMEM),
        out_shape=jax.ShapeDtypeStruct(parts[0].shape, parts[0].dtype),
        compiler_params=kernel_params(),
        name="sum_parts",
    )(*parts, *after)


def join_kernel(at_ref, a, b, c, d, *refs):
    out = refs[-1]
    size = a.shape[1]
    for bits, part in enumerate((a, b, c, d)):
        begin = pl.multiple_of((at_ref[0] ^ bits) * size, size)
        out[:, pl.ds(begin, size)] = part[...]


def join_parts(at, parts, after):
    rows, size = parts[0].shape
    return pl.pallas_call(
        join_kernel,
        in_specs=[pl.BlockSpec(memory_space=pltpu.SMEM)]
        + [pl.BlockSpec(memory_space=pltpu.VMEM)] * 4
        + [pl.BlockSpec(memory_space=pl.ANY)] * len(after),
        out_specs=pl.BlockSpec(memory_space=pltpu.VMEM),
        out_shape=jax.ShapeDtypeStruct((rows, 4 * size), parts[0].dtype),
        compiler_params=kernel_params(),
        name="join_parts",
    )(at, *parts, *after)


def halves_kernel(a, b, *refs):
    keep, send = refs[-2:]
    half = a.shape[0] // 2
    keep[:half, :], keep[half:, :] = a[:half, :], b[:half, :]
    send[:half, :], send[half:, :] = a[half:, :], b[half:, :]


def pair_halves(a, b, after):
    shape = jax.ShapeDtypeStruct(a.shape, a.dtype)
    return pl.pallas_call(
        halves_kernel,
        in_specs=[pl.BlockSpec(memory_space=pltpu.VMEM)] * 2
        + [pl.BlockSpec(memory_space=pl.ANY)] * len(after),
        out_specs=[pl.BlockSpec(memory_space=pltpu.VMEM)] * 2,
        out_shape=[shape, shape],
        compiler_params=kernel_params(),
        name="pair_halves",
    )(a, b, *after)


def stage_kernel(far, own, offset_ref, near_ref, *refs):
    refs = list(refs)
    weights = [refs.pop(0) for _ in range(4)]
    far_ins = [refs.pop(0) for _ in range(8 * far)]
    own_ins = [refs.pop(0) for _ in range(8 * own)]
    extra = [refs.pop(0) for _ in range(5 * own)]
    own_right = refs.pop() if own else None
    far_right = refs.pop() if far else None
    out = refs.pop() if own else None
    far_out = refs.pop() if far else None
    depth = weights[0].shape[1]

    def join(ins, right):
        for block in range(4):
            for k in range(2):
                right[block * depth : (block + 1) * depth, k * LANES : (k + 1) * LANES] = ins[2 * block + k][...]

    def half_sum(rows, right):
        total = 0.0
        for k in range(4):
            block = right[k * depth : (k + 1) * depth, :]
            total += jnp.dot(weights[k][rows, :], block, preferred_element_type=jnp.float32)
        return total

    @pl.when(pl.program_id(0) == 0)
    def _():
        if far:
            join(far_ins, far_right)
        if own:
            join(own_ins, own_right)
            out[...] = jnp.zeros_like(out)

    @pl.loop(0, TILE // STEP)
    def _(r):
        rows = pl.ds(pl.multiple_of(r * STEP, STEP), STEP)
        if far:
            far_out[rows, :] = half_sum(rows, far_right).astype(jnp.bfloat16)
        if own:
            came, gate_ref, up_ref, proj_gate, proj_up = extra
            rank_size = proj_gate.shape[0]
            total = half_sum(rows, own_right)
            hidden_grad = (total + came[rows, :].astype(jnp.float32)).astype(jnp.bfloat16)
            hidden_grad = hidden_grad.astype(jnp.float32)
            gate = gate_ref[rows, :].astype(jnp.float32)
            up = up_ref[rows, :].astype(jnp.float32)
            sigma = jax.nn.sigmoid(gate)
            grad_up = (hidden_grad * (gate * sigma)).astype(jnp.bfloat16)
            grad_gate = (hidden_grad * up * sigma * (1.0 + gate * (1.0 - sigma))).astype(jnp.bfloat16)
            out[:rank_size, :] += jnp.dot(proj_gate[:, rows], grad_gate, preferred_element_type=jnp.float32)
            out[rank_size:, :] += jnp.dot(proj_up[:, rows], grad_up, preferred_element_type=jnp.float32)


def side_of(near, side):
    return near[0] + side * (1 - 2 * near[0])


def in_half(side, part, near):
    return 2 * side_of(near, side) + part


def in_whole(side, part, near):
    return 4 * near[1] + 2 * side_of(near, side) + part


def in_spread(rows, side, part, near):
    half = near[1] + part * (1 - 2 * near[1])
    return 4 * half + 2 * side_of(near, side) + rows


def stage(near_offset, near, tiles, far, own, weight, weight_near, after):
    begin, count = tiles
    width = weight_near.shape[1]
    depth = width // 2
    both = 2 * LANES
    arrays, specs, outs, shapes, rights = [], [], [], [], []

    def add(array, block, index):
        arrays.append(array)
        specs.append(pl.BlockSpec(block, index))

    for k in range(2):
        add(weight, (TILE, depth), lambda i, offset, near, k=k: (offset[0] + begin + i, k))
    for k in range(2):
        add(weight_near, (TILE, depth), lambda i, offset, near, k=k: (offset[0] + begin + i, k))
    for rows in (far, own):
        if rows is not None:
            rights.append(pltpu.VMEM((2 * width, both), jnp.bfloat16))
            for block in range(4):
                for k in range(2):
                    index = functools.partial(rows[2], *divmod(block, 2))
                    add(rows[k], (depth, LANES), lambda i, offset, near, index=index: (index(near), 0))
    if far is not None:
        outs.append(pl.BlockSpec((TILE, both), lambda i, offset, near: (i, 0)))
        shapes.append(jax.ShapeDtypeStruct((count * TILE, both), jnp.bfloat16))
    if own is not None:
        (came, first), gate, up, proj_gate, proj_up = own[3:]
        rank_size = proj_gate.shape[0]
        add(came, (TILE, both), lambda i, offset, near: (begin - first + i, 0))
        for array in (gate, up):
            add(array, (TILE, both), lambda i, offset, near: (begin + i, 0))
        for array in (proj_gate, proj_up):
            add(array, (rank_size, TILE), lambda i, offset, near: (0, offset[0] + begin + i))
        outs.append(pl.BlockSpec((2 * rank_size, both), lambda i, offset, near: (0, 0)))
        shapes.append(jax.ShapeDtypeStruct((2 * rank_size, both), jnp.float32))
    parts = len(rights)
    return pl.pallas_call(
        functools.partial(stage_kernel, far is not None, own is not None),
        grid_spec=pltpu.PrefetchScalarGridSpec(
            num_scalar_prefetch=2,
            grid=(count,),
            in_specs=specs + [pl.BlockSpec(memory_space=pl.ANY)] * len(after),
            out_specs=outs,
            scratch_shapes=rights,
        ),
        out_shape=shapes,
        compiler_params=kernel_params(),
        cost_estimate=pl.CostEstimate(
            flops=4 * parts * both * width * count * TILE,
            bytes_accessed=4 * width * count * TILE + 4 * parts * both * count * TILE,
            transcendentals=0,
        ),
        name="stage",
    )(near_offset, near, *arrays, *after)


def sum_over(array, axis):
    parts = [swap(array, axis, bits) for bits in (1, 2, 3)]
    return (array + parts[0]) + (parts[1] + parts[2])


def scatter_over(array, axis, dim):
    at = lax.axis_index(axis)
    size = array.shape[dim] // 4
    parts = [swap(take(array, (at ^ bits) * size, size, dim), axis, bits) for bits in (1, 2, 3)]
    return (take(array, at * size, size, dim) + parts[0]) + (parts[1] + parts[2])


def packed_scores(capacity, args):
    (
        layer_input,
        gate_pre,
        up_pre,
        grad_rows,
        blocks,
        place,
        down_weight,
        proj_input,
        proj_hidden,
        proj_output,
        proj_gate,
        proj_up,
        rev_slot,
        own_lengths,
    ) = args
    ex_count, slot_len, width_local = layer_input.shape
    hidden_local = gate_pre.shape[2]
    row_total = ex_count * slot_len
    rank_size = proj_input.shape[0]
    rev_pairs = rev_slot.shape[0] // 2
    example_at = lax.axis_index("example")
    tensor_at = lax.axis_index("tensor")
    near, far = example_at % 2, example_at // 2
    half_hidden = hidden_local // 2
    chunks = capacity // (2 * LANES)
    offset = (near * (half_hidden // TILE)).astype(jnp.int32).reshape(1)
    near_at, far_at = near.astype(jnp.int32).reshape(1), far.astype(jnp.int32).reshape(1)
    near_far = jnp.concatenate([near_at, far_at])
    gathered = [lax.all_gather(blocks[k], "tensor", axis=0, tiled=True) for k in range(2)]

    tile_count = half_hidden // TILE
    split = tile_count - tile_count // 2
    tile_parts = [(0, split), (split, tile_count - split)]

    def near_pair(rows, index):
        return rows, swap(rows, "example", 1), index

    def run(h, far, own, after):
        return stage(offset, near_far, tile_parts[h], far, own, down_weight, weight_near, after)

    weight_near = swap(down_weight, "example", 1)
    gate_rows = gate_pre.reshape(row_total, hidden_local)
    up_rows = up_pre.reshape(row_total, hidden_local)
    gate_near, up_near = swap(gate_rows, "example", 1), swap(up_rows, "example", 1)
    crossed = [move(blocks[k], CROSS) for k in range(2, chunks)]
    away = cut(1 - far_at, gathered[0], crossed)
    inputs_rows = layer_input.reshape(row_total, width_local)
    gate_values = gate_rows.astype(jnp.float32)
    up_values = up_rows.astype(jnp.float32)
    hidden = (gate_values * jax.nn.sigmoid(gate_values) * up_values).astype(jnp.bfloat16)
    early = jnp.concatenate(
        [
            contract(proj_input, inputs_rows),
            contract(proj_hidden, hidden),
            contract(proj_output, grad_rows),
        ]
    )
    def quarter(bits):
        return take(early, (tensor_at ^ bits) * slot_len, slot_len, 1)

    sums = [quarter(0)] + [swap(quarter(bits), "tensor", bits) for bits in (1, 2, 3)]
    far_pair = near_pair(swap(away, "example", 2), in_half)

    order = jnp.where(far == 1, 3 - tensor_at, tensor_at)
    shards = []
    for k in range(2, chunks):
        keep, send = pair_halves(blocks[k], crossed[k - 2], (away,))
        shards.append(jnp.where(order < 2, keep, move(send, SPREAD)))
    gathered += [lax.all_gather(shard, "tensor", axis=0, tiled=True) for shard in shards]

    came, right, after = [], [], ()
    for h, tiles in enumerate(tile_parts):
        results = run(h, far_pair, None, after)
        came.append((swap(results[0], "example", 2), tiles[0]))
        after = (results[0],)
    before = near_pair(gathered[0], in_whole)
    for k in range(1, chunks):
        if k == 1:
            away = cut(1 - far_at, gathered[1], after)
            far_next = swap(away, "example", 2)
            after = (away, came[0][0], *shards)
            gate_packed = pack(chunks, 2 * LANES, half_hidden, offset, place, gate_rows, gate_near, after)
            up_packed = pack(chunks, 2 * LANES, half_hidden, offset, place, up_rows, up_near, after)
            after = (gate_packed[0], up_packed[0])
            far_pair = near_pair(ordered(far_next, after), in_half)
            own_pair = near_pair(gathered[1], in_whole)
        else:
            both = near_pair(gathered[k], None)[:2]
            far_pair = (*both, functools.partial(in_spread, 1))
            own_pair = (*both, functools.partial(in_spread, 0))
        arrived, came = came, []
        for h, tiles in enumerate(tile_parts):
            own = (*before, arrived[h], gate_packed[k - 1], up_packed[k - 1])
            results = run(h, far_pair, (*own, proj_gate, proj_up), after)
            after = (results[0],)
            came.append((swap(results[0], "example", 2), tiles[0]))
            right.append(results[1])
            if (k, h) == (1, 0):
                sums = sum_parts(sums, after)
                after += (sums,)
                in_gate, in_down, out_down = (sums[j * rank_size : (j + 1) * rank_size] for j in range(3))
                in_gate = [in_gate] + [swap(in_gate, "tensor", bits) for bits in (1, 2, 3)]
            if (k, h) == (1, 1):
                in_gate = join_parts(tensor_at.astype(jnp.int32).reshape(1), in_gate, (*after, came[0][0]))
                after += (in_gate,)
                in_gate_near = swap(in_gate, "example", 1)
        before = own_pair
    for h, tiles in enumerate(tile_parts):
        own = (*before, came[h], gate_packed[-1], up_packed[-1], proj_gate, proj_up)
        right += run(h, None, own, after)
        after = (right[-1],)
    right = jnp.concatenate([right[k] + right[k + 1] for k in range(0, 2 * chunks, 2)], axis=1)

    slots_here = jnp.concatenate(
        [
            take(rev_slot, example_at * ex_count, ex_count, 0),
            take(rev_slot, (example_at ^ 1) * ex_count, ex_count, 0),
        ]
    )
    table = pairing_table(slots_here, rev_pairs)
    positions = jnp.arange(slot_len, dtype=jnp.int32)
    mask = (positions < take(own_lengths, tensor_at, 1, 0)).astype(jnp.float32)
    sketch_down = contract_exact(in_down * mask[None, :], out_down)
    sketch_down = take(table, tensor_at, 1, 1)[:, :, None] * sketch_down[None, :, :]
    select = jnp.arange(capacity, dtype=jnp.int32)[:, None] == place
    in_gate = jnp.concatenate([in_gate, in_gate_near], axis=1)
    in_gate = contract_exact(in_gate, select.astype(jnp.float32))
    table_rows = contract(
        jnp.repeat(table, slot_len, axis=1).astype(jnp.bfloat16), select.astype(jnp.bfloat16)
    )
    left = (table_rows[:, None, :] * in_gate[None, :, :]).reshape(rev_pairs * rank_size, capacity)
    sketch_late = contract_exact(left, right).reshape(rev_pairs, rank_size, 2 * rank_size)
    return jnp.concatenate([sketch_late, sketch_down], axis=2)


def local_four(
    layer_input,
    gate_pre,
    up_pre,
    output_grad,
    down_weight,
    proj_input,
    proj_hidden,
    proj_output,
    proj_gate,
    proj_up,
    query_sketches,
    rev_lengths,
    rev_slot,
    query_slot,
):
    ex_count, slot_len, width_local = layer_input.shape
    row_total = ex_count * slot_len
    grad_rows = output_grad.reshape(row_total, width_local)
    grad_near = swap(grad_rows, "example", 1)
    others = [swap(rev_lengths, "example", bits) for bits in (1, 2, 3)]

    near = lax.axis_index("example") % 2
    both_lengths = jnp.concatenate([rev_lengths, others[0]])
    own_begin = near * jnp.sum(others[0])
    near_begin = (1 - near) * jnp.sum(rev_lengths)
    offsets = jnp.concatenate(
        [
            own_begin + jnp.cumsum(rev_lengths) - rev_lengths,
            near_begin + jnp.cumsum(others[0]) - others[0],
        ]
    )
    positions = jnp.arange(slot_len, dtype=jnp.int32)
    place = (offsets[:, None] + positions[None, :]) ^ (near * LANES)
    place = jnp.where(positions[None, :] < both_lengths[:, None], place, -1).reshape(1, 2 * row_total)
    no_offset = jnp.zeros((1,), jnp.int32)
    full = 2 * row_total
    blocks = pack(full // (2 * LANES), LANES, width_local, no_offset, place, grad_rows, grad_near)
    sums = jnp.stack([jnp.sum(rev_lengths) + jnp.sum(others[0]), jnp.sum(others[1]) + jnp.sum(others[2])])
    most = jnp.max(sums).reshape(1)
    count = lax.axis_size("group")
    for step in range(1, count):
        shifted = lax.ppermute(most, "group", [(i, (i + step) % count) for i in range(count)])
        most = jnp.maximum(most, shifted)
    levels = [level for level in LEVELS if level < full] + [full]
    branch = jnp.sum((most[0] > jnp.array(levels[:-1], jnp.int32)).astype(jnp.int32))
    sketch = lax.switch(
        branch,
        [functools.partial(packed_scores, level) for level in levels],
        (
            layer_input,
            gate_pre,
            up_pre,
            grad_rows,
            blocks,
            place,
            down_weight,
            proj_input,
            proj_hidden,
            proj_output,
            proj_gate,
            proj_up,
            rev_slot,
            rev_lengths,
        ),
    )
    rank_size = proj_input.shape[0]
    rev_pairs = rev_slot.shape[0] // 2
    revision_pairs = sum_over(scatter_over(sketch, "tensor", 1), "example")
    example_scores = contract_exact(
        revision_pairs.reshape(rev_pairs, -1), query_sketches.astype(jnp.float32)
    )
    query_pairs = query_slot.shape[0] * 4 // 2
    pair_terms = contract_exact(example_scores, pairing_table(query_slot, query_pairs))
    total = sum_over(scatter_over(pair_terms, "example", 1), "tensor")
    return total / jnp.float32(rank_size * rank_size)


def local_any(
    layer_input,
    gate_pre,
    up_pre,
    output_grad,
    down_weight,
    proj_input,
    proj_hidden,
    proj_output,
    proj_gate,
    proj_up,
    query_sketches,
    rev_lengths,
    rev_slot,
    query_slot,
):
    ex_count, slot_len, width_local = layer_input.shape
    hidden_local = gate_pre.shape[2]
    row_total = ex_count * slot_len
    rank_size = proj_input.shape[0]
    per_rank = rank_size // lax.axis_size("tensor")
    inputs_rows = layer_input.reshape(row_total, width_local)
    grad_rows = output_grad.reshape(row_total, width_local)
    gate_values = gate_pre.reshape(row_total, hidden_local).astype(jnp.float32)
    up_values = up_pre.reshape(row_total, hidden_local).astype(jnp.float32)
    grad_full = lax.all_gather(grad_rows, "tensor", axis=1, tiled=True)
    hidden_grad = contract(grad_full, lax.all_gather(down_weight, "example", axis=1, tiled=True))
    hidden_grad = lax.optimization_barrier(hidden_grad.astype(jnp.bfloat16)).astype(jnp.float32)
    sigma = jax.nn.sigmoid(gate_values)
    active = gate_values * sigma
    hidden = (active * up_values).astype(jnp.bfloat16)
    grad_up = (hidden_grad * active).astype(jnp.bfloat16)
    grad_gate = (hidden_grad * up_values * sigma * (1.0 + gate_values * (1.0 - sigma))).astype(
        jnp.bfloat16
    )
    partials = jnp.stack(
        [
            contract(inputs_rows, proj_input),
            contract(hidden, proj_hidden),
            contract(grad_gate, proj_gate),
            contract(grad_up, proj_up),
            contract(grad_rows, proj_output),
        ]
    )
    summed = lax.psum(partials, "tensor")
    begin = lax.axis_index("tensor") * per_rank
    left = lax.dynamic_slice_in_dim(summed[:2], begin, per_rank, 2)
    right = summed[2:]
    positions = jnp.arange(slot_len, dtype=jnp.int32)
    mask = (positions[None, :] < rev_lengths[:, None]).astype(jnp.float32).reshape(row_total)
    left = left * mask[None, :, None]
    left = jnp.stack([left[0], left[0], left[1]]).reshape(3, ex_count, slot_len, per_rank)
    right = right.reshape(3, ex_count, slot_len, rank_size)
    sketches = jnp.einsum("meti,metj->eimj", left, right, precision=lax.Precision.HIGHEST).reshape(
        ex_count, per_rank * 3 * rank_size
    )
    every_sketch = lax.all_gather(sketches, "example", axis=0, tiled=True)
    rev_pairs = rev_slot.shape[0] // 2
    revision_pairs = jnp.dot(
        pairing_table(rev_slot, rev_pairs), every_sketch, precision=lax.Precision.HIGHEST
    )
    example_scores = contract_exact(revision_pairs, query_sketches.astype(jnp.float32))
    query_pairs = query_slot.shape[0] * lax.axis_size("example") // 2
    pair_terms = contract_exact(example_scores, pairing_table(query_slot, query_pairs))
    owned = lax.psum_scatter(pair_terms, "example", scatter_dimension=1, tiled=True)
    total = lax.psum(owned, "tensor")
    return total / jnp.float32(rank_size * rank_size)


def solution(mesh):
    four = mesh.shape["tensor"] == 4 and mesh.shape["example"] == 4
    return jax.shard_map(
        local_four if four else local_any,
        mesh=mesh,
        in_specs=(
            P(("group", "example"), None, "tensor"),
            P(("group", "example"), None, "tensor"),
            P(("group", "example"), None, "tensor"),
            P(("group", "example"), None, "tensor"),
            P("tensor", "example"),
            P(None, "tensor"),
            P(None, "tensor"),
            P(None, "tensor"),
            P(None, "tensor"),
            P(None, "tensor"),
            P(("group", "example"), "tensor"),
            P(("group", "example")),
            P("group"),
            P(("group", "example")),
        ),
        out_specs=P("group", "example"),
        check_vma=False,
    )
```

```python
import functools

import jax
import jax.numpy as jnp
from jax import lax
from jax.experimental import pallas as pl
from jax.experimental.pallas import tpu as pltpu
from jax.sharding import PartitionSpec as P

LEVELS = (768,)
TILE = 512
STEP = 256
LANES = 128
VMEM_LIMIT = 58 * 1024 * 1024


def contract(left_side, right_side):
    return lax.dot_general(
        left_side, right_side, (((1,), (1,)), ((), ())), preferred_element_type=jnp.float32
    )


def contract_exact(left_side, right_side):
    return lax.dot_general(
        left_side,
        right_side,
        (((1,), (1,)), ((), ())),
        precision=lax.Precision.HIGHEST,
        preferred_element_type=jnp.float32,
    )


def pairing_table(slots, pairs):
    pair_index = slots // 2
    signs = (1 - 2 * (slots % 2)).astype(jnp.float32)
    targets = jnp.arange(pairs, dtype=jnp.int32)
    return jnp.where(targets[:, None] == pair_index[None, :], signs[None, :], jnp.float32(0.0))


def take(array, start, size, axis):
    return lax.dynamic_slice_in_dim(array, start, size, axis)


def swap(array, axis, bits):
    count = lax.axis_size(axis)
    return lax.ppermute(array, axis, [(i, i ^ bits) for i in range(count)])


def kernel_params():
    return pltpu.CompilerParams(vmem_limit_bytes=VMEM_LIMIT)


def pack_kernel(size, count, near_ref, place_ref, own_ref, other_ref, *refs):
    outs, select = refs[-1 - count : -1], refs[-1]
    rows_own = own_ref.shape[0]

    @pl.when(pl.program_id(0) == 0)
    def _():
        @pl.loop(0, count)
        def _(c):
            at = lax.broadcasted_iota(jnp.int32, (size, select.shape[1]), 0) + c * 2 * LANES
            chosen = jnp.where(at == place_ref[...], 1.0, 0.0).astype(jnp.bfloat16)
            select[pl.ds(pl.multiple_of(c * size, size), size), :] = chosen

    for c in range(count):
        rows = slice(c * size, (c + 1) * size)
        total = jnp.dot(select[rows, :rows_own], own_ref[...], preferred_element_type=jnp.float32)
        total += jnp.dot(select[rows, rows_own:], other_ref[...], preferred_element_type=jnp.float32)
        outs[c][...] = total.astype(jnp.bfloat16).T


def pack(count, size, columns, near_offset, place, own, other, after=()):
    rows = own.shape[0]
    total = count * size
    return pl.pallas_call(
        functools.partial(pack_kernel, size, count),
        grid_spec=pltpu.PrefetchScalarGridSpec(
            num_scalar_prefetch=1,
            grid=(columns // TILE,),
            in_specs=[
                pl.BlockSpec((1, 2 * rows), lambda i, near: (0, 0)),
                pl.BlockSpec((rows, TILE), lambda i, near: (0, near[0] + i)),
                pl.BlockSpec((rows, TILE), lambda i, near: (0, near[0] + i)),
            ]
            + [pl.BlockSpec(memory_space=pl.ANY)] * len(after),
            out_specs=[pl.BlockSpec((TILE, size), lambda i, near: (i, 0))] * count,
            scratch_shapes=[pltpu.VMEM((total, 2 * rows), jnp.bfloat16)],
        ),
        out_shape=[jax.ShapeDtypeStruct((columns, size), jnp.bfloat16)] * count,
        compiler_params=kernel_params(),
        cost_estimate=pl.CostEstimate(
            flops=4 * total * rows * columns,
            bytes_accessed=(4 * rows + 2 * total) * columns,
            transcendentals=0,
        ),
        name="pack_rows",
    )(near_offset, place, own, other, *after)


def cut_kernel(at_ref, source, *refs):
    refs[-1][...] = source[...]


def cut(at, gathered, after):
    columns, rows = gathered.shape
    block = columns // 8
    return pl.pallas_call(
        cut_kernel,
        grid_spec=pltpu.PrefetchScalarGridSpec(
            num_scalar_prefetch=1,
            grid=(4,),
            in_specs=[pl.BlockSpec((block, rows), lambda i, at: (4 * at[0] + i, 0))]
            + [pl.BlockSpec(memory_space=pl.ANY)] * len(after),
            out_specs=pl.BlockSpec((block, rows), lambda i, at: (i, 0)),
        ),
        out_shape=jax.ShapeDtypeStruct((columns // 2, rows), gathered.dtype),
        compiler_params=kernel_params(),
        cost_estimate=pl.CostEstimate(flops=0, bytes_accessed=2 * columns * rows, transcendentals=0),
        name="cut_columns",
    )(at, gathered, *after)


def gate_kernel(value, *refs):
    refs[-1][...] = value[...]


def ordered(value, after):
    return pl.pallas_call(
        gate_kernel,
        in_specs=[pl.BlockSpec(memory_space=pltpu.VMEM)]
        + [pl.BlockSpec(memory_space=pl.ANY)] * len(after),
        out_specs=pl.BlockSpec(memory_space=pltpu.VMEM),
        out_shape=jax.ShapeDtypeStruct(value.shape, value.dtype),
        compiler_params=kernel_params(),
        name="ordered_copy",
    )(value, *after)


def sum_kernel(a, b, c, d, *refs):
    refs[-1][...] = (a[...] + b[...]) + (c[...] + d[...])


def sum_parts(parts, after):
    return pl.pallas_call(
        sum_kernel,
        in_specs=[pl.BlockSpec(memory_space=pltpu.VMEM)] * 4
        + [pl.BlockSpec(memory_space=pl.ANY)] * len(after),
        out_specs=pl.BlockSpec(memory_space=pltpu.VMEM),
        out_shape=jax.ShapeDtypeStruct(parts[0].shape, parts[0].dtype),
        compiler_params=kernel_params(),
        name="sum_parts",
    )(*parts, *after)


def join_kernel(at_ref, a, b, c, d, *refs):
    out = refs[-1]
    size = a.shape[1]
    for bits, part in enumerate((a, b, c, d)):
        begin = pl.multiple_of((at_ref[0] ^ bits) * size, size)
        out[:, pl.ds(begin, size)] = part[...]


def join_parts(at, parts, after):
    rows, size = parts[0].shape
    return pl.pallas_call(
        join_kernel,
        in_specs=[pl.BlockSpec(memory_space=pltpu.SMEM)]
        + [pl.BlockSpec(memory_space=pltpu.VMEM)] * 4
        + [pl.BlockSpec(memory_space=pl.ANY)] * len(after),
        out_specs=pl.BlockSpec(memory_space=pltpu.VMEM),
        out_shape=jax.ShapeDtypeStruct((rows, 4 * size), parts[0].dtype),
        compiler_params=kernel_params(),
        name="join_parts",
    )(at, *parts, *after)


def stage_kernel(far, own, offset_ref, near_ref, *refs):
    refs = list(refs)
    weights = [refs.pop(0) for _ in range(4)]
    far_ins = [refs.pop(0) for _ in range(4 * far)]
    own_ins = [refs.pop(0) for _ in range(4 * own)]
    extra = [refs.pop(0) for _ in range(5 * own)]
    own_right = refs.pop() if own else None
    far_right = refs.pop() if far else None
    out = refs.pop() if own else None
    far_out = refs.pop() if far else None
    depth = weights[0].shape[1]
    width = 2 * depth

    def join(ins, right):
        for side in range(2):
            for k in range(2):
                right[side * width : (side + 1) * width, k * LANES : (k + 1) * LANES] = ins[2 * side + k][...]

    def half_sum(rows, right):
        total = 0.0
        for k in range(4):
            block = right[k * depth : (k + 1) * depth, :]
            total += jnp.dot(weights[k][rows, :], block, preferred_element_type=jnp.float32)
        return total

    @pl.when(pl.program_id(0) == 0)
    def _():
        if far:
            join(far_ins, far_right)
        if own:
            join(own_ins, own_right)
            out[...] = jnp.zeros_like(out)

    @pl.loop(0, TILE // STEP)
    def _(r):
        rows = pl.ds(pl.multiple_of(r * STEP, STEP), STEP)
        if far:
            far_out[rows, :] = half_sum(rows, far_right).astype(jnp.bfloat16)
        if own:
            came, gate_ref, up_ref, proj_gate, proj_up = extra
            rank_size = proj_gate.shape[0]
            total = half_sum(rows, own_right)
            hidden_grad = (total + came[rows, :].astype(jnp.float32)).astype(jnp.bfloat16)
            hidden_grad = hidden_grad.astype(jnp.float32)
            gate = gate_ref[rows, :].astype(jnp.float32)
            up = up_ref[rows, :].astype(jnp.float32)
            sigma = jax.nn.sigmoid(gate)
            grad_up = (hidden_grad * (gate * sigma)).astype(jnp.bfloat16)
            grad_gate = (hidden_grad * up * sigma * (1.0 + gate * (1.0 - sigma))).astype(jnp.bfloat16)
            out[:rank_size, :] += jnp.dot(proj_gate[:, rows], grad_gate, preferred_element_type=jnp.float32)
            out[rank_size:, :] += jnp.dot(proj_up[:, rows], grad_up, preferred_element_type=jnp.float32)


def stage(near_offset, near, tiles, far, own, weight, weight_near, after):
    begin, count = tiles
    width = weight_near.shape[1]
    depth = width // 2
    both = 2 * LANES
    arrays, specs, outs, shapes, rights = [], [], [], [], []

    def add(array, block, index):
        arrays.append(array)
        specs.append(pl.BlockSpec(block, index))

    for k in range(2):
        add(weight, (TILE, depth), lambda i, offset, near, k=k: (offset[0] + begin + i, k))
    for k in range(2):
        add(weight_near, (TILE, depth), lambda i, offset, near, k=k: (offset[0] + begin + i, k))
    for rows, base in ((far, 0), (own, 2)):
        if rows is not None:
            rights.append(pltpu.VMEM((2 * width, both), jnp.bfloat16))
            for k in range(4):
                side = k // 2
                add(
                    rows[k % 2],
                    (width, LANES),
                    lambda i, offset, near, side=side, base=base: (
                        base * near[1] + near[0] + side * (1 - 2 * near[0]),
                        0,
                    ),
                )
    if far is not None:
        outs.append(pl.BlockSpec((TILE, both), lambda i, offset, near: (i, 0)))
        shapes.append(jax.ShapeDtypeStruct((count * TILE, both), jnp.bfloat16))
    if own is not None:
        (came, first), gate, up, proj_gate, proj_up = own[2:]
        rank_size = proj_gate.shape[0]
        add(came, (TILE, both), lambda i, offset, near: (begin - first + i, 0))
        for array in (gate, up):
            add(array, (TILE, both), lambda i, offset, near: (begin + i, 0))
        for array in (proj_gate, proj_up):
            add(array, (rank_size, TILE), lambda i, offset, near: (0, offset[0] + begin + i))
        outs.append(pl.BlockSpec((2 * rank_size, both), lambda i, offset, near: (0, 0)))
        shapes.append(jax.ShapeDtypeStruct((2 * rank_size, both), jnp.float32))
    parts = len(rights)
    return pl.pallas_call(
        functools.partial(stage_kernel, far is not None, own is not None),
        grid_spec=pltpu.PrefetchScalarGridSpec(
            num_scalar_prefetch=2,
            grid=(count,),
            in_specs=specs + [pl.BlockSpec(memory_space=pl.ANY)] * len(after),
            out_specs=outs,
            scratch_shapes=rights,
        ),
        out_shape=shapes,
        compiler_params=kernel_params(),
        cost_estimate=pl.CostEstimate(
            flops=4 * parts * both * width * count * TILE,
            bytes_accessed=4 * width * count * TILE + 4 * parts * both * count * TILE,
            transcendentals=0,
        ),
        name="stage",
    )(near_offset, near, *arrays, *after)


def sum_over(array, axis):
    parts = [swap(array, axis, bits) for bits in (1, 2, 3)]
    return (array + parts[0]) + (parts[1] + parts[2])


def scatter_over(array, axis, dim):
    at = lax.axis_index(axis)
    size = array.shape[dim] // 4
    parts = [swap(take(array, (at ^ bits) * size, size, dim), axis, bits) for bits in (1, 2, 3)]
    return (take(array, at * size, size, dim) + parts[0]) + (parts[1] + parts[2])


def packed_scores(capacity, args):
    (
        layer_input,
        gate_pre,
        up_pre,
        grad_rows,
        blocks,
        place,
        down_weight,
        proj_input,
        proj_hidden,
        proj_output,
        proj_gate,
        proj_up,
        rev_slot,
        own_lengths,
    ) = args
    ex_count, slot_len, width_local = layer_input.shape
    hidden_local = gate_pre.shape[2]
    row_total = ex_count * slot_len
    rank_size = proj_input.shape[0]
    rev_pairs = rev_slot.shape[0] // 2
    example_at = lax.axis_index("example")
    tensor_at = lax.axis_index("tensor")
    near, far = example_at % 2, example_at // 2
    half_hidden = hidden_local // 2
    chunks = capacity // (2 * LANES)
    offset = (near * (half_hidden // TILE)).astype(jnp.int32).reshape(1)
    near_at, far_at = near.astype(jnp.int32).reshape(1), far.astype(jnp.int32).reshape(1)
    near_far = jnp.concatenate([near_at, far_at])
    gathered = [lax.all_gather(blocks[k], "tensor", axis=0, tiled=True) for k in range(chunks)]

    tile_count = half_hidden // TILE
    split = tile_count - tile_count // 2
    tile_parts = [(0, split), (split, tile_count - split)]

    def near_pair(rows):
        return rows, swap(rows, "example", 1)

    def run(h, far, own, after):
        return stage(offset, near_far, tile_parts[h], far, own, down_weight, weight_near, after)

    weight_near = swap(down_weight, "example", 1)
    gate_rows = gate_pre.reshape(row_total, hidden_local)
    up_rows = up_pre.reshape(row_total, hidden_local)
    gate_near, up_near = swap(gate_rows, "example", 1), swap(up_rows, "example", 1)
    away = cut(1 - far_at, gathered[0], ())
    inputs_rows = layer_input.reshape(row_total, width_local)
    gate_values = gate_rows.astype(jnp.float32)
    up_values = up_rows.astype(jnp.float32)
    hidden = (gate_values * jax.nn.sigmoid(gate_values) * up_values).astype(jnp.bfloat16)
    early = jnp.concatenate(
        [
            contract(proj_input, inputs_rows),
            contract(proj_hidden, hidden),
            contract(proj_output, grad_rows),
        ]
    )
    def quarter(bits):
        return take(early, (tensor_at ^ bits) * slot_len, slot_len, 1)

    sums = [quarter(0)] + [swap(quarter(bits), "tensor", bits) for bits in (1, 2, 3)]
    far_pair = near_pair(ordered(swap(away, "example", 2), (early,)))
    came, right, after = [], [], ()
    for h, tiles in enumerate(tile_parts):
        results = run(h, far_pair, None, after)
        came.append((swap(results[0], "example", 2), tiles[0]))
        after = (results[0],)
    for k in range(1, chunks):
        before = near_pair(gathered[k - 1])
        if k == 1:
            away = cut(1 - far_at, gathered[1], after)
            far_next = swap(away, "example", 2)
            after = (away, came[0][0])
            gate_packed = pack(chunks, 2 * LANES, half_hidden, offset, place, gate_rows, gate_near, after)
            up_packed = pack(chunks, 2 * LANES, half_hidden, offset, place, up_rows, up_near, after)
            after = (gate_packed[0], up_packed[0])
        far_pair = near_pair(ordered(far_next, after))
        if k + 1 < chunks:
            next_away = cut(1 - far_at, gathered[k + 1], after)
            far_next = swap(next_away, "example", 2)
            after += (next_away,)
        arrived, came = came, []
        for h, tiles in enumerate(tile_parts):
            own = (*before, arrived[h], gate_packed[k - 1], up_packed[k - 1])
            results = run(h, far_pair, (*own, proj_gate, proj_up), after)
            after = (results[0],)
            came.append((swap(results[0], "example", 2), tiles[0]))
            right.append(results[1])
            if (k, h) == (1, 1):
                sums = sum_parts(sums, after)
                after += (sums,)
                in_gate, in_down, out_down = (sums[j * rank_size : (j + 1) * rank_size] for j in range(3))
                in_gate = [in_gate] + [swap(in_gate, "tensor", bits) for bits in (1, 2, 3)]
            if (k, h) == (2, 1):
                in_gate = join_parts(tensor_at.astype(jnp.int32).reshape(1), in_gate, after)
                after += (in_gate,)
                in_gate_near = swap(in_gate, "example", 1)
    before = near_pair(gathered[-1])
    for h, tiles in enumerate(tile_parts):
        own = (*before, came[h], gate_packed[-1], up_packed[-1], proj_gate, proj_up)
        right += run(h, None, own, after)
        after = (right[-1],)
    right = jnp.concatenate([right[k] + right[k + 1] for k in range(0, 2 * chunks, 2)], axis=1)

    slots_here = jnp.concatenate(
        [
            take(rev_slot, example_at * ex_count, ex_count, 0),
            take(rev_slot, (example_at ^ 1) * ex_count, ex_count, 0),
        ]
    )
    table = pairing_table(slots_here, rev_pairs)
    positions = jnp.arange(slot_len, dtype=jnp.int32)
    mask = (positions < take(own_lengths, tensor_at, 1, 0)).astype(jnp.float32)
    sketch_down = contract_exact(in_down * mask[None, :], out_down)
    sketch_down = take(table, tensor_at, 1, 1)[:, :, None] * sketch_down[None, :, :]
    select = jnp.arange(capacity, dtype=jnp.int32)[:, None] == place
    in_gate = jnp.concatenate([in_gate, in_gate_near], axis=1)
    in_gate = contract_exact(in_gate, select.astype(jnp.float32))
    table_rows = contract(
        jnp.repeat(table, slot_len, axis=1).astype(jnp.bfloat16), select.astype(jnp.bfloat16)
    )
    left = (table_rows[:, None, :] * in_gate[None, :, :]).reshape(rev_pairs * rank_size, capacity)
    sketch_late = contract_exact(left, right).reshape(rev_pairs, rank_size, 2 * rank_size)
    return jnp.concatenate([sketch_late, sketch_down], axis=2)


def local_four(
    layer_input,
    gate_pre,
    up_pre,
    output_grad,
    down_weight,
    proj_input,
    proj_hidden,
    proj_output,
    proj_gate,
    proj_up,
    query_sketches,
    rev_lengths,
    rev_slot,
    query_slot,
):
    ex_count, slot_len, width_local = layer_input.shape
    row_total = ex_count * slot_len
    grad_rows = output_grad.reshape(row_total, width_local)
    grad_near = swap(grad_rows, "example", 1)
    others = [swap(rev_lengths, "example", bits) for bits in (1, 2, 3)]

    near = lax.axis_index("example") % 2
    both_lengths = jnp.concatenate([rev_lengths, others[0]])
    own_begin = near * jnp.sum(others[0])
    near_begin = (1 - near) * jnp.sum(rev_lengths)
    offsets = jnp.concatenate(
        [
            own_begin + jnp.cumsum(rev_lengths) - rev_lengths,
            near_begin + jnp.cumsum(others[0]) - others[0],
        ]
    )
    positions = jnp.arange(slot_len, dtype=jnp.int32)
    place = (offsets[:, None] + positions[None, :]) ^ (near * LANES)
    place = jnp.where(positions[None, :] < both_lengths[:, None], place, -1).reshape(1, 2 * row_total)
    no_offset = jnp.zeros((1,), jnp.int32)
    full = 2 * row_total
    blocks = pack(full // (2 * LANES), LANES, width_local, no_offset, place, grad_rows, grad_near)
    sums = jnp.stack([jnp.sum(rev_lengths) + jnp.sum(others[0]), jnp.sum(others[1]) + jnp.sum(others[2])])
    most = jnp.max(sums).reshape(1)
    count = lax.axis_size("group")
    for step in range(1, count):
        shifted = lax.ppermute(most, "group", [(i, (i + step) % count) for i in range(count)])
        most = jnp.maximum(most, shifted)
    levels = [level for level in LEVELS if level < full] + [full]
    branch = jnp.sum((most[0] > jnp.array(levels[:-1], jnp.int32)).astype(jnp.int32))
    sketch = lax.switch(
        branch,
        [functools.partial(packed_scores, level) for level in levels],
        (
            layer_input,
            gate_pre,
            up_pre,
            grad_rows,
            blocks,
            place,
            down_weight,
            proj_input,
            proj_hidden,
            proj_output,
            proj_gate,
            proj_up,
            rev_slot,
            rev_lengths,
        ),
    )
    rank_size = proj_input.shape[0]
    rev_pairs = rev_slot.shape[0] // 2
    revision_pairs = sum_over(scatter_over(sketch, "tensor", 1), "example")
    example_scores = contract_exact(
        revision_pairs.reshape(rev_pairs, -1), query_sketches.astype(jnp.float32)
    )
    query_pairs = query_slot.shape[0] * 4 // 2
    pair_terms = contract_exact(example_scores, pairing_table(query_slot, query_pairs))
    total = sum_over(scatter_over(pair_terms, "example", 1), "tensor")
    return total / jnp.float32(rank_size * rank_size)


def local_any(
    layer_input,
    gate_pre,
    up_pre,
    output_grad,
    down_weight,
    proj_input,
    proj_hidden,
    proj_output,
    proj_gate,
    proj_up,
    query_sketches,
    rev_lengths,
    rev_slot,
    query_slot,
):
    ex_count, slot_len, width_local = layer_input.shape
    hidden_local = gate_pre.shape[2]
    row_total = ex_count * slot_len
    rank_size = proj_input.shape[0]
    per_rank = rank_size // lax.axis_size("tensor")
    inputs_rows = layer_input.reshape(row_total, width_local)
    grad_rows = output_grad.reshape(row_total, width_local)
    gate_values = gate_pre.reshape(row_total, hidden_local).astype(jnp.float32)
    up_values = up_pre.reshape(row_total, hidden_local).astype(jnp.float32)
    grad_full = lax.all_gather(grad_rows, "tensor", axis=1, tiled=True)
    hidden_grad = contract(grad_full, lax.all_gather(down_weight, "example", axis=1, tiled=True))
    hidden_grad = lax.optimization_barrier(hidden_grad.astype(jnp.bfloat16)).astype(jnp.float32)
    sigma = jax.nn.sigmoid(gate_values)
    active = gate_values * sigma
    hidden = (active * up_values).astype(jnp.bfloat16)
    grad_up = (hidden_grad * active).astype(jnp.bfloat16)
    grad_gate = (hidden_grad * up_values * sigma * (1.0 + gate_values * (1.0 - sigma))).astype(
        jnp.bfloat16
    )
    partials = jnp.stack(
        [
            contract(inputs_rows, proj_input),
            contract(hidden, proj_hidden),
            contract(grad_gate, proj_gate),
            contract(grad_up, proj_up),
            contract(grad_rows, proj_output),
        ]
    )
    summed = lax.psum(partials, "tensor")
    begin = lax.axis_index("tensor") * per_rank
    left = lax.dynamic_slice_in_dim(summed[:2], begin, per_rank, 2)
    right = summed[2:]
    positions = jnp.arange(slot_len, dtype=jnp.int32)
    mask = (positions[None, :] < rev_lengths[:, None]).astype(jnp.float32).reshape(row_total)
    left = left * mask[None, :, None]
    left = jnp.stack([left[0], left[0], left[1]]).reshape(3, ex_count, slot_len, per_rank)
    right = right.reshape(3, ex_count, slot_len, rank_size)
    sketches = jnp.einsum("meti,metj->eimj", left, right, precision=lax.Precision.HIGHEST).reshape(
        ex_count, per_rank * 3 * rank_size
    )
    every_sketch = lax.all_gather(sketches, "example", axis=0, tiled=True)
    rev_pairs = rev_slot.shape[0] // 2
    revision_pairs = jnp.dot(
        pairing_table(rev_slot, rev_pairs), every_sketch, precision=lax.Precision.HIGHEST
    )
    example_scores = contract_exact(revision_pairs, query_sketches.astype(jnp.float32))
    query_pairs = query_slot.shape[0] * lax.axis_size("example") // 2
    pair_terms = contract_exact(example_scores, pairing_table(query_slot, query_pairs))
    owned = lax.psum_scatter(pair_terms, "example", scatter_dimension=1, tiled=True)
    total = lax.psum(owned, "tensor")
    return total / jnp.float32(rank_size * rank_size)


def solution(mesh):
    four = mesh.shape["tensor"] == 4 and mesh.shape["example"] == 4
    return jax.shard_map(
        local_four if four else local_any,
        mesh=mesh,
        in_specs=(
            P(("group", "example"), None, "tensor"),
            P(("group", "example"), None, "tensor"),
            P(("group", "example"), None, "tensor"),
            P(("group", "example"), None, "tensor"),
            P("tensor", "example"),
            P(None, "tensor"),
            P(None, "tensor"),
            P(None, "tensor"),
            P(None, "tensor"),
            P(None, "tensor"),
            P(("group", "example"), "tensor"),
            P(("group", "example")),
            P("group"),
            P(("group", "example")),
        ),
        out_specs=P("group", "example"),
        check_vma=False,
    )
```

```python
import functools

import jax
import jax.numpy as jnp
from jax import lax
from jax.experimental import pallas as pl
from jax.experimental.pallas import tpu as pltpu
from jax.sharding import PartitionSpec as P

LEVELS = (768,)
TILE = 512
STEP = 256
LANES = 128
VMEM_LIMIT = 58 * 1024 * 1024


def contract(left_side, right_side):
    return lax.dot_general(
        left_side, right_side, (((1,), (1,)), ((), ())), preferred_element_type=jnp.float32
    )


def contract_exact(left_side, right_side):
    return lax.dot_general(
        left_side,
        right_side,
        (((1,), (1,)), ((), ())),
        precision=lax.Precision.HIGHEST,
        preferred_element_type=jnp.float32,
    )


def pairing_table(slots, pairs):
    pair_index = slots // 2
    signs = (1 - 2 * (slots % 2)).astype(jnp.float32)
    targets = jnp.arange(pairs, dtype=jnp.int32)
    return jnp.where(targets[:, None] == pair_index[None, :], signs[None, :], jnp.float32(0.0))


def take(array, start, size, axis):
    return lax.dynamic_slice_in_dim(array, start, size, axis)


def swap(array, axis, bits):
    count = lax.axis_size(axis)
    return lax.ppermute(array, axis, [(i, i ^ bits) for i in range(count)])


def kernel_params():
    return pltpu.CompilerParams(vmem_limit_bytes=VMEM_LIMIT)


def pack_kernel(size, count, near_ref, place_ref, own_ref, other_ref, *refs):
    outs, select = refs[-1 - count : -1], refs[-1]
    rows_own = own_ref.shape[0]

    @pl.when(pl.program_id(0) == 0)
    def _():
        @pl.loop(0, count)
        def _(c):
            at = lax.broadcasted_iota(jnp.int32, (size, select.shape[1]), 0) + c * 2 * LANES
            chosen = jnp.where(at == place_ref[...], 1.0, 0.0).astype(jnp.bfloat16)
            select[pl.ds(pl.multiple_of(c * size, size), size), :] = chosen

    for c in range(count):
        rows = slice(c * size, (c + 1) * size)
        total = jnp.dot(select[rows, :rows_own], own_ref[...], preferred_element_type=jnp.float32)
        total += jnp.dot(select[rows, rows_own:], other_ref[...], preferred_element_type=jnp.float32)
        outs[c][...] = total.astype(jnp.bfloat16).T


def pack(count, size, columns, near_offset, place, own, other, after=()):
    rows = own.shape[0]
    total = count * size
    return pl.pallas_call(
        functools.partial(pack_kernel, size, count),
        grid_spec=pltpu.PrefetchScalarGridSpec(
            num_scalar_prefetch=1,
            grid=(columns // TILE,),
            in_specs=[
                pl.BlockSpec((1, 2 * rows), lambda i, near: (0, 0)),
                pl.BlockSpec((rows, TILE), lambda i, near: (0, near[0] + i)),
                pl.BlockSpec((rows, TILE), lambda i, near: (0, near[0] + i)),
            ]
            + [pl.BlockSpec(memory_space=pl.ANY)] * len(after),
            out_specs=[pl.BlockSpec((TILE, size), lambda i, near: (i, 0))] * count,
            scratch_shapes=[pltpu.VMEM((total, 2 * rows), jnp.bfloat16)],
        ),
        out_shape=[jax.ShapeDtypeStruct((columns, size), jnp.bfloat16)] * count,
        compiler_params=kernel_params(),
        cost_estimate=pl.CostEstimate(
            flops=4 * total * rows * columns,
            bytes_accessed=(4 * rows + 2 * total) * columns,
            transcendentals=0,
        ),
        name="pack_rows",
    )(near_offset, place, own, other, *after)


def cut_kernel(at_ref, source, *refs):
    refs[-1][...] = source[...]


def cut(at, gathered, after):
    columns, rows = gathered.shape
    block = columns // 8
    return pl.pallas_call(
        cut_kernel,
        grid_spec=pltpu.PrefetchScalarGridSpec(
            num_scalar_prefetch=1,
            grid=(4,),
            in_specs=[pl.BlockSpec((block, rows), lambda i, at: (4 * at[0] + i, 0))]
            + [pl.BlockSpec(memory_space=pl.ANY)] * len(after),
            out_specs=pl.BlockSpec((block, rows), lambda i, at: (i, 0)),
        ),
        out_shape=jax.ShapeDtypeStruct((columns // 2, rows), gathered.dtype),
        compiler_params=kernel_params(),
        cost_estimate=pl.CostEstimate(flops=0, bytes_accessed=2 * columns * rows, transcendentals=0),
        name="cut_columns",
    )(at, gathered, *after)


def gate_kernel(value, *refs):
    refs[-1][...] = value[...]


def ordered(value, after):
    return pl.pallas_call(
        gate_kernel,
        in_specs=[pl.BlockSpec(memory_space=pltpu.VMEM)]
        + [pl.BlockSpec(memory_space=pl.ANY)] * len(after),
        out_specs=pl.BlockSpec(memory_space=pltpu.VMEM),
        out_shape=jax.ShapeDtypeStruct(value.shape, value.dtype),
        compiler_params=kernel_params(),
        name="ordered_copy",
    )(value, *after)


def sum_kernel(a, b, c, d, *refs):
    refs[-1][...] = (a[...] + b[...]) + (c[...] + d[...])


def sum_parts(parts, after):
    return pl.pallas_call(
        sum_kernel,
        in_specs=[pl.BlockSpec(memory_space=pltpu.VMEM)] * 4
        + [pl.BlockSpec(memory_space=pl.ANY)] * len(after),
        out_specs=pl.BlockSpec(memory_space=pltpu.VMEM),
        out_shape=jax.ShapeDtypeStruct(parts[0].shape, parts[0].dtype),
        compiler_params=kernel_params(),
        name="sum_parts",
    )(*parts, *after)


def join_kernel(at_ref, a, b, c, d, *refs):
    out = refs[-1]
    size = a.shape[1]
    for bits, part in enumerate((a, b, c, d)):
        begin = pl.multiple_of((at_ref[0] ^ bits) * size, size)
        out[:, pl.ds(begin, size)] = part[...]


def join_parts(at, parts, after):
    rows, size = parts[0].shape
    return pl.pallas_call(
        join_kernel,
        in_specs=[pl.BlockSpec(memory_space=pltpu.SMEM)]
        + [pl.BlockSpec(memory_space=pltpu.VMEM)] * 4
        + [pl.BlockSpec(memory_space=pl.ANY)] * len(after),
        out_specs=pl.BlockSpec(memory_space=pltpu.VMEM),
        out_shape=jax.ShapeDtypeStruct((rows, 4 * size), parts[0].dtype),
        compiler_params=kernel_params(),
        name="join_parts",
    )(at, *parts, *after)


def stage_kernel(far, own, offset_ref, near_ref, *refs):
    refs = list(refs)
    weights = [refs.pop(0) for _ in range(4)]
    far_ins = [refs.pop(0) for _ in range(4 * far)]
    own_ins = [refs.pop(0) for _ in range(4 * own)]
    extra = [refs.pop(0) for _ in range(5 * own)]
    own_right = refs.pop() if own else None
    far_right = refs.pop() if far else None
    out = refs.pop() if own else None
    far_out = refs.pop() if far else None
    depth = weights[0].shape[1]
    width = 2 * depth

    def join(ins, right):
        for side in range(2):
            for k in range(2):
                right[side * width : (side + 1) * width, k * LANES : (k + 1) * LANES] = ins[2 * side + k][...]

    def half_sum(rows, right):
        total = 0.0
        for k in range(4):
            block = right[k * depth : (k + 1) * depth, :]
            total += jnp.dot(weights[k][rows, :], block, preferred_element_type=jnp.float32)
        return total

    @pl.when(pl.program_id(0) == 0)
    def _():
        if far:
            join(far_ins, far_right)
        if own:
            join(own_ins, own_right)
            out[...] = jnp.zeros_like(out)

    @pl.loop(0, TILE // STEP)
    def _(r):
        rows = pl.ds(pl.multiple_of(r * STEP, STEP), STEP)
        if far:
            far_out[rows, :] = half_sum(rows, far_right).astype(jnp.bfloat16)
        if own:
            came, gate_ref, up_ref, proj_gate, proj_up = extra
            rank_size = proj_gate.shape[0]
            total = half_sum(rows, own_right)
            hidden_grad = (total + came[rows, :].astype(jnp.float32)).astype(jnp.bfloat16)
            hidden_grad = hidden_grad.astype(jnp.float32)
            gate = gate_ref[rows, :].astype(jnp.float32)
            up = up_ref[rows, :].astype(jnp.float32)
            sigma = jax.nn.sigmoid(gate)
            grad_up = (hidden_grad * (gate * sigma)).astype(jnp.bfloat16)
            grad_gate = (hidden_grad * up * sigma * (1.0 + gate * (1.0 - sigma))).astype(jnp.bfloat16)
            out[:rank_size, :] += jnp.dot(proj_gate[:, rows], grad_gate, preferred_element_type=jnp.float32)
            out[rank_size:, :] += jnp.dot(proj_up[:, rows], grad_up, preferred_element_type=jnp.float32)


def stage(near_offset, near, tiles, far, own, weight, weight_near, after):
    begin, count = tiles
    width = weight_near.shape[1]
    depth = width // 2
    both = 2 * LANES
    arrays, specs, outs, shapes, rights = [], [], [], [], []

    def add(array, block, index):
        arrays.append(array)
        specs.append(pl.BlockSpec(block, index))

    for k in range(2):
        add(weight, (TILE, depth), lambda i, offset, near, k=k: (offset[0] + begin + i, k))
    for k in range(2):
        add(weight_near, (TILE, depth), lambda i, offset, near, k=k: (offset[0] + begin + i, k))
    for rows, base in ((far, 0), (own, 2)):
        if rows is not None:
            rights.append(pltpu.VMEM((2 * width, both), jnp.bfloat16))
            for k in range(4):
                side = k // 2
                add(
                    rows[k % 2],
                    (width, LANES),
                    lambda i, offset, near, side=side, base=base: (
                        base * near[1] + near[0] + side * (1 - 2 * near[0]),
                        0,
                    ),
                )
    if far is not None:
        outs.append(pl.BlockSpec((TILE, both), lambda i, offset, near: (i, 0)))
        shapes.append(jax.ShapeDtypeStruct((count * TILE, both), jnp.bfloat16))
    if own is not None:
        (came, first), gate, up, proj_gate, proj_up = own[2:]
        rank_size = proj_gate.shape[0]
        add(came, (TILE, both), lambda i, offset, near: (begin - first + i, 0))
        for array in (gate, up):
            add(array, (TILE, both), lambda i, offset, near: (begin + i, 0))
        for array in (proj_gate, proj_up):
            add(array, (rank_size, TILE), lambda i, offset, near: (0, offset[0] + begin + i))
        outs.append(pl.BlockSpec((2 * rank_size, both), lambda i, offset, near: (0, 0)))
        shapes.append(jax.ShapeDtypeStruct((2 * rank_size, both), jnp.float32))
    parts = len(rights)
    return pl.pallas_call(
        functools.partial(stage_kernel, far is not None, own is not None),
        grid_spec=pltpu.PrefetchScalarGridSpec(
            num_scalar_prefetch=2,
            grid=(count,),
            in_specs=specs + [pl.BlockSpec(memory_space=pl.ANY)] * len(after),
            out_specs=outs,
            scratch_shapes=rights,
        ),
        out_shape=shapes,
        compiler_params=kernel_params(),
        cost_estimate=pl.CostEstimate(
            flops=4 * parts * both * width * count * TILE,
            bytes_accessed=4 * width * count * TILE + 4 * parts * both * count * TILE,
            transcendentals=0,
        ),
        name="stage",
    )(near_offset, near, *arrays, *after)


def sum_over(array, axis):
    parts = [swap(array, axis, bits) for bits in (1, 2, 3)]
    return (array + parts[0]) + (parts[1] + parts[2])


def scatter_over(array, axis, dim):
    at = lax.axis_index(axis)
    size = array.shape[dim] // 4
    parts = [swap(take(array, (at ^ bits) * size, size, dim), axis, bits) for bits in (1, 2, 3)]
    return (take(array, at * size, size, dim) + parts[0]) + (parts[1] + parts[2])


def packed_scores(capacity, args):
    (
        layer_input,
        gate_pre,
        up_pre,
        grad_rows,
        blocks,
        place,
        down_weight,
        proj_input,
        proj_hidden,
        proj_output,
        proj_gate,
        proj_up,
        rev_slot,
        own_lengths,
    ) = args
    ex_count, slot_len, width_local = layer_input.shape
    hidden_local = gate_pre.shape[2]
    row_total = ex_count * slot_len
    rank_size = proj_input.shape[0]
    rev_pairs = rev_slot.shape[0] // 2
    example_at = lax.axis_index("example")
    tensor_at = lax.axis_index("tensor")
    near, far = example_at % 2, example_at // 2
    half_hidden = hidden_local // 2
    chunks = capacity // (2 * LANES)
    offset = (near * (half_hidden // TILE)).astype(jnp.int32).reshape(1)
    near_at, far_at = near.astype(jnp.int32).reshape(1), far.astype(jnp.int32).reshape(1)
    near_far = jnp.concatenate([near_at, far_at])
    gathered = [lax.all_gather(blocks[k], "tensor", axis=0, tiled=True) for k in range(chunks)]

    tile_count = half_hidden // TILE
    split = tile_count - tile_count // 2
    tile_parts = [(0, split), (split, tile_count - split)]

    def near_pair(rows):
        return rows, swap(rows, "example", 1)

    def run(h, far, own, after):
        return stage(offset, near_far, tile_parts[h], far, own, down_weight, weight_near, after)

    weight_near = swap(down_weight, "example", 1)
    gate_rows = gate_pre.reshape(row_total, hidden_local)
    up_rows = up_pre.reshape(row_total, hidden_local)
    gate_near, up_near = swap(gate_rows, "example", 1), swap(up_rows, "example", 1)
    away = cut(1 - far_at, gathered[0], ())
    inputs_rows = layer_input.reshape(row_total, width_local)
    gate_values = gate_rows.astype(jnp.float32)
    up_values = up_rows.astype(jnp.float32)
    hidden = (gate_values * jax.nn.sigmoid(gate_values) * up_values).astype(jnp.bfloat16)
    early = jnp.concatenate(
        [
            contract(proj_input, inputs_rows),
            contract(proj_hidden, hidden),
            contract(proj_output, grad_rows),
        ]
    )
    def quarter(bits):
        return take(early, (tensor_at ^ bits) * slot_len, slot_len, 1)

    sums = [quarter(0)] + [swap(quarter(bits), "tensor", bits) for bits in (1, 2, 3)]
    far_pair = near_pair(ordered(swap(away, "example", 2), (early,)))
    came, right, after = [], [], ()
    for h, tiles in enumerate(tile_parts):
        results = run(h, far_pair, None, after)
        came.append((swap(results[0], "example", 2), tiles[0]))
        after = (results[0],)
    for k in range(1, chunks):
        before = near_pair(gathered[k - 1])
        if k == 1:
            away = cut(1 - far_at, gathered[1], after)
            far_next = swap(away, "example", 2)
            gate_packed = pack(chunks, 2 * LANES, half_hidden, offset, place, gate_rows, gate_near, (away,))
            after = (gate_packed[0], came[0][0])
            up_packed = pack(chunks, 2 * LANES, half_hidden, offset, place, up_rows, up_near, after)
            after = (gate_packed[0], up_packed[0])
        far_pair = near_pair(ordered(far_next, after))
        if k + 1 < chunks:
            next_away = cut(1 - far_at, gathered[k + 1], after)
            far_next = swap(next_away, "example", 2)
            after += (next_away,)
        arrived, came = came, []
        for h, tiles in enumerate(tile_parts):
            own = (*before, arrived[h], gate_packed[k - 1], up_packed[k - 1])
            results = run(h, far_pair, (*own, proj_gate, proj_up), after)
            after = (results[0],)
            came.append((swap(results[0], "example", 2), tiles[0]))
            right.append(results[1])
            if (k, h) == (1, 1):
                sums = sum_parts(sums, after)
                after += (sums,)
                in_gate, in_down, out_down = (sums[j * rank_size : (j + 1) * rank_size] for j in range(3))
                in_gate = [in_gate] + [swap(in_gate, "tensor", bits) for bits in (1, 2, 3)]
            if (k, h) == (2, 1):
                in_gate = join_parts(tensor_at.astype(jnp.int32).reshape(1), in_gate, after)
                after += (in_gate,)
                in_gate_near = swap(in_gate, "example", 1)
    before = near_pair(gathered[-1])
    for h, tiles in enumerate(tile_parts):
        own = (*before, came[h], gate_packed[-1], up_packed[-1], proj_gate, proj_up)
        right += run(h, None, own, after)
        after = (right[-1],)
    right = jnp.concatenate([right[k] + right[k + 1] for k in range(0, 2 * chunks, 2)], axis=1)

    slots_here = jnp.concatenate(
        [
            take(rev_slot, example_at * ex_count, ex_count, 0),
            take(rev_slot, (example_at ^ 1) * ex_count, ex_count, 0),
        ]
    )
    table = pairing_table(slots_here, rev_pairs)
    positions = jnp.arange(slot_len, dtype=jnp.int32)
    mask = (positions < take(own_lengths, tensor_at, 1, 0)).astype(jnp.float32)
    sketch_down = contract_exact(in_down * mask[None, :], out_down)
    sketch_down = take(table, tensor_at, 1, 1)[:, :, None] * sketch_down[None, :, :]
    select = jnp.arange(capacity, dtype=jnp.int32)[:, None] == place
    in_gate = jnp.concatenate([in_gate, in_gate_near], axis=1)
    in_gate = contract_exact(in_gate, select.astype(jnp.float32))
    table_rows = contract(
        jnp.repeat(table, slot_len, axis=1).astype(jnp.bfloat16), select.astype(jnp.bfloat16)
    )
    left = (table_rows[:, None, :] * in_gate[None, :, :]).reshape(rev_pairs * rank_size, capacity)
    sketch_late = contract_exact(left, right).reshape(rev_pairs, rank_size, 2 * rank_size)
    return jnp.concatenate([sketch_late, sketch_down], axis=2)


def local_four(
    layer_input,
    gate_pre,
    up_pre,
    output_grad,
    down_weight,
    proj_input,
    proj_hidden,
    proj_output,
    proj_gate,
    proj_up,
    query_sketches,
    rev_lengths,
    rev_slot,
    query_slot,
):
    ex_count, slot_len, width_local = layer_input.shape
    row_total = ex_count * slot_len
    grad_rows = output_grad.reshape(row_total, width_local)
    grad_near = swap(grad_rows, "example", 1)
    others = [swap(rev_lengths, "example", bits) for bits in (1, 2, 3)]

    near = lax.axis_index("example") % 2
    both_lengths = jnp.concatenate([rev_lengths, others[0]])
    own_begin = near * jnp.sum(others[0])
    near_begin = (1 - near) * jnp.sum(rev_lengths)
    offsets = jnp.concatenate(
        [
            own_begin + jnp.cumsum(rev_lengths) - rev_lengths,
            near_begin + jnp.cumsum(others[0]) - others[0],
        ]
    )
    positions = jnp.arange(slot_len, dtype=jnp.int32)
    place = (offsets[:, None] + positions[None, :]) ^ (near * LANES)
    place = jnp.where(positions[None, :] < both_lengths[:, None], place, -1).reshape(1, 2 * row_total)
    no_offset = jnp.zeros((1,), jnp.int32)
    full = 2 * row_total
    blocks = pack(full // (2 * LANES), LANES, width_local, no_offset, place, grad_rows, grad_near)
    sums = jnp.stack([jnp.sum(rev_lengths) + jnp.sum(others[0]), jnp.sum(others[1]) + jnp.sum(others[2])])
    most = jnp.max(sums).reshape(1)
    count = lax.axis_size("group")
    for step in range(1, count):
        shifted = lax.ppermute(most, "group", [(i, (i + step) % count) for i in range(count)])
        most = jnp.maximum(most, shifted)
    levels = [level for level in LEVELS if level < full] + [full]
    branch = jnp.sum((most[0] > jnp.array(levels[:-1], jnp.int32)).astype(jnp.int32))
    sketch = lax.switch(
        branch,
        [functools.partial(packed_scores, level) for level in levels],
        (
            layer_input,
            gate_pre,
            up_pre,
            grad_rows,
            blocks,
            place,
            down_weight,
            proj_input,
            proj_hidden,
            proj_output,
            proj_gate,
            proj_up,
            rev_slot,
            rev_lengths,
        ),
    )
    rank_size = proj_input.shape[0]
    rev_pairs = rev_slot.shape[0] // 2
    revision_pairs = sum_over(scatter_over(sketch, "tensor", 1), "example")
    example_scores = contract_exact(
        revision_pairs.reshape(rev_pairs, -1), query_sketches.astype(jnp.float32)
    )
    query_pairs = query_slot.shape[0] * 4 // 2
    pair_terms = contract_exact(example_scores, pairing_table(query_slot, query_pairs))
    total = sum_over(scatter_over(pair_terms, "example", 1), "tensor")
    return total / jnp.float32(rank_size * rank_size)


def local_any(
    layer_input,
    gate_pre,
    up_pre,
    output_grad,
    down_weight,
    proj_input,
    proj_hidden,
    proj_output,
    proj_gate,
    proj_up,
    query_sketches,
    rev_lengths,
    rev_slot,
    query_slot,
):
    ex_count, slot_len, width_local = layer_input.shape
    hidden_local = gate_pre.shape[2]
    row_total = ex_count * slot_len
    rank_size = proj_input.shape[0]
    per_rank = rank_size // lax.axis_size("tensor")
    inputs_rows = layer_input.reshape(row_total, width_local)
    grad_rows = output_grad.reshape(row_total, width_local)
    gate_values = gate_pre.reshape(row_total, hidden_local).astype(jnp.float32)
    up_values = up_pre.reshape(row_total, hidden_local).astype(jnp.float32)
    grad_full = lax.all_gather(grad_rows, "tensor", axis=1, tiled=True)
    hidden_grad = contract(grad_full, lax.all_gather(down_weight, "example", axis=1, tiled=True))
    hidden_grad = lax.optimization_barrier(hidden_grad.astype(jnp.bfloat16)).astype(jnp.float32)
    sigma = jax.nn.sigmoid(gate_values)
    active = gate_values * sigma
    hidden = (active * up_values).astype(jnp.bfloat16)
    grad_up = (hidden_grad * active).astype(jnp.bfloat16)
    grad_gate = (hidden_grad * up_values * sigma * (1.0 + gate_values * (1.0 - sigma))).astype(
        jnp.bfloat16
    )
    partials = jnp.stack(
        [
            contract(inputs_rows, proj_input),
            contract(hidden, proj_hidden),
            contract(grad_gate, proj_gate),
            contract(grad_up, proj_up),
            contract(grad_rows, proj_output),
        ]
    )
    summed = lax.psum(partials, "tensor")
    begin = lax.axis_index("tensor") * per_rank
    left = lax.dynamic_slice_in_dim(summed[:2], begin, per_rank, 2)
    right = summed[2:]
    positions = jnp.arange(slot_len, dtype=jnp.int32)
    mask = (positions[None, :] < rev_lengths[:, None]).astype(jnp.float32).reshape(row_total)
    left = left * mask[None, :, None]
    left = jnp.stack([left[0], left[0], left[1]]).reshape(3, ex_count, slot_len, per_rank)
    right = right.reshape(3, ex_count, slot_len, rank_size)
    sketches = jnp.einsum("meti,metj->eimj", left, right, precision=lax.Precision.HIGHEST).reshape(
        ex_count, per_rank * 3 * rank_size
    )
    every_sketch = lax.all_gather(sketches, "example", axis=0, tiled=True)
    rev_pairs = rev_slot.shape[0] // 2
    revision_pairs = jnp.dot(
        pairing_table(rev_slot, rev_pairs), every_sketch, precision=lax.Precision.HIGHEST
    )
    example_scores = contract_exact(revision_pairs, query_sketches.astype(jnp.float32))
    query_pairs = query_slot.shape[0] * lax.axis_size("example") // 2
    pair_terms = contract_exact(example_scores, pairing_table(query_slot, query_pairs))
    owned = lax.psum_scatter(pair_terms, "example", scatter_dimension=1, tiled=True)
    total = lax.psum(owned, "tensor")
    return total / jnp.float32(rank_size * rank_size)


def solution(mesh):
    four = mesh.shape["tensor"] == 4 and mesh.shape["example"] == 4
    return jax.shard_map(
        local_four if four else local_any,
        mesh=mesh,
        in_specs=(
            P(("group", "example"), None, "tensor"),
            P(("group", "example"), None, "tensor"),
            P(("group", "example"), None, "tensor"),
            P(("group", "example"), None, "tensor"),
            P("tensor", "example"),
            P(None, "tensor"),
            P(None, "tensor"),
            P(None, "tensor"),
            P(None, "tensor"),
            P(None, "tensor"),
            P(("group", "example"), "tensor"),
            P(("group", "example")),
            P("group"),
            P(("group", "example")),
        ),
        out_specs=P("group", "example"),
        check_vma=False,
    )
```

```python
import functools

import jax
import jax.numpy as jnp
from jax import lax
from jax.experimental import pallas as pl
from jax.experimental.pallas import tpu as pltpu
from jax.sharding import PartitionSpec as P

LEVELS = (768,)
TILE = 512
STEP = 256
LANES = 128
VMEM_LIMIT = 58 * 1024 * 1024


def contract(left_side, right_side):
    return lax.dot_general(
        left_side, right_side, (((1,), (1,)), ((), ())), preferred_element_type=jnp.float32
    )


def contract_exact(left_side, right_side):
    return lax.dot_general(
        left_side,
        right_side,
        (((1,), (1,)), ((), ())),
        precision=lax.Precision.HIGHEST,
        preferred_element_type=jnp.float32,
    )


def pairing_table(slots, pairs):
    pair_index = slots // 2
    signs = (1 - 2 * (slots % 2)).astype(jnp.float32)
    targets = jnp.arange(pairs, dtype=jnp.int32)
    return jnp.where(targets[:, None] == pair_index[None, :], signs[None, :], jnp.float32(0.0))


def take(array, start, size, axis):
    return lax.dynamic_slice_in_dim(array, start, size, axis)


def swap(array, axis, bits):
    count = lax.axis_size(axis)
    return lax.ppermute(array, axis, [(i, i ^ bits) for i in range(count)])


def kernel_params():
    return pltpu.CompilerParams(vmem_limit_bytes=VMEM_LIMIT)


def pack_kernel(size, count, near_ref, place_ref, own_ref, other_ref, *refs):
    outs, select = refs[-1 - count : -1], refs[-1]
    rows_own = own_ref.shape[0]

    @pl.when(pl.program_id(0) == 0)
    def _():
        @pl.loop(0, count)
        def _(c):
            at = lax.broadcasted_iota(jnp.int32, (size, select.shape[1]), 0) + c * 2 * LANES
            chosen = jnp.where(at == place_ref[...], 1.0, 0.0).astype(jnp.bfloat16)
            select[pl.ds(pl.multiple_of(c * size, size), size), :] = chosen

    for c in range(count):
        rows = slice(c * size, (c + 1) * size)
        total = jnp.dot(select[rows, :rows_own], own_ref[...], preferred_element_type=jnp.float32)
        total += jnp.dot(select[rows, rows_own:], other_ref[...], preferred_element_type=jnp.float32)
        outs[c][...] = total.astype(jnp.bfloat16).T


def pack(count, size, columns, near_offset, place, own, other, after=()):
    rows = own.shape[0]
    total = count * size
    return pl.pallas_call(
        functools.partial(pack_kernel, size, count),
        grid_spec=pltpu.PrefetchScalarGridSpec(
            num_scalar_prefetch=1,
            grid=(columns // TILE,),
            in_specs=[
                pl.BlockSpec((1, 2 * rows), lambda i, near: (0, 0)),
                pl.BlockSpec((rows, TILE), lambda i, near: (0, near[0] + i)),
                pl.BlockSpec((rows, TILE), lambda i, near: (0, near[0] + i)),
            ]
            + [pl.BlockSpec(memory_space=pl.ANY)] * len(after),
            out_specs=[pl.BlockSpec((TILE, size), lambda i, near: (i, 0))] * count,
            scratch_shapes=[pltpu.VMEM((total, 2 * rows), jnp.bfloat16)],
        ),
        out_shape=[jax.ShapeDtypeStruct((columns, size), jnp.bfloat16)] * count,
        compiler_params=kernel_params(),
        cost_estimate=pl.CostEstimate(
            flops=4 * total * rows * columns,
            bytes_accessed=(4 * rows + 2 * total) * columns,
            transcendentals=0,
        ),
        name="pack_rows",
    )(near_offset, place, own, other, *after)


def cut_kernel(at_ref, source, *refs):
    refs[-1][...] = source[...]


def cut(at, gathered, after):
    columns, rows = gathered.shape
    block = columns // 8
    return pl.pallas_call(
        cut_kernel,
        grid_spec=pltpu.PrefetchScalarGridSpec(
            num_scalar_prefetch=1,
            grid=(4,),
            in_specs=[pl.BlockSpec((block, rows), lambda i, at: (4 * at[0] + i, 0))]
            + [pl.BlockSpec(memory_space=pl.ANY)] * len(after),
            out_specs=pl.BlockSpec((block, rows), lambda i, at: (i, 0)),
        ),
        out_shape=jax.ShapeDtypeStruct((columns // 2, rows), gathered.dtype),
        compiler_params=kernel_params(),
        cost_estimate=pl.CostEstimate(flops=0, bytes_accessed=2 * columns * rows, transcendentals=0),
        name="cut_columns",
    )(at, gathered, *after)


def gate_kernel(value, *refs):
    refs[-1][...] = value[...]


def ordered(value, after):
    return pl.pallas_call(
        gate_kernel,
        in_specs=[pl.BlockSpec(memory_space=pltpu.VMEM)]
        + [pl.BlockSpec(memory_space=pl.ANY)] * len(after),
        out_specs=pl.BlockSpec(memory_space=pltpu.VMEM),
        out_shape=jax.ShapeDtypeStruct(value.shape, value.dtype),
        compiler_params=kernel_params(),
        name="ordered_copy",
    )(value, *after)


def sum_kernel(a, b, c, d, *refs):
    refs[-1][...] = (a[...] + b[...]) + (c[...] + d[...])


def sum_parts(parts, after):
    return pl.pallas_call(
        sum_kernel,
        in_specs=[pl.BlockSpec(memory_space=pltpu.VMEM)] * 4
        + [pl.BlockSpec(memory_space=pl.ANY)] * len(after),
        out_specs=pl.BlockSpec(memory_space=pltpu.VMEM),
        out_shape=jax.ShapeDtypeStruct(parts[0].shape, parts[0].dtype),
        compiler_params=kernel_params(),
        name="sum_parts",
    )(*parts, *after)


def join_kernel(at_ref, a, b, c, d, *refs):
    out = refs[-1]
    size = a.shape[1]
    for bits, part in enumerate((a, b, c, d)):
        begin = pl.multiple_of((at_ref[0] ^ bits) * size, size)
        out[:, pl.ds(begin, size)] = part[...]


def join_parts(at, parts, after):
    rows, size = parts[0].shape
    return pl.pallas_call(
        join_kernel,
        in_specs=[pl.BlockSpec(memory_space=pltpu.SMEM)]
        + [pl.BlockSpec(memory_space=pltpu.VMEM)] * 4
        + [pl.BlockSpec(memory_space=pl.ANY)] * len(after),
        out_specs=pl.BlockSpec(memory_space=pltpu.VMEM),
        out_shape=jax.ShapeDtypeStruct((rows, 4 * size), parts[0].dtype),
        compiler_params=kernel_params(),
        name="join_parts",
    )(at, *parts, *after)


def stage_kernel(far, own, offset_ref, near_ref, *refs):
    refs = list(refs)
    weights = [refs.pop(0) for _ in range(4)]
    far_ins = [refs.pop(0) for _ in range(4 * far)]
    own_ins = [refs.pop(0) for _ in range(4 * own)]
    extra = [refs.pop(0) for _ in range(5 * own)]
    own_right = refs.pop() if own else None
    far_right = refs.pop() if far else None
    out = refs.pop() if own else None
    far_out = refs.pop() if far else None
    depth = weights[0].shape[1]
    width = 2 * depth

    def join(ins, right):
        for side in range(2):
            for k in range(2):
                right[side * width : (side + 1) * width, k * LANES : (k + 1) * LANES] = ins[2 * side + k][...]

    def half_sum(rows, right):
        total = 0.0
        for k in range(4):
            block = right[k * depth : (k + 1) * depth, :]
            total += jnp.dot(weights[k][rows, :], block, preferred_element_type=jnp.float32)
        return total

    @pl.when(pl.program_id(0) == 0)
    def _():
        if far:
            join(far_ins, far_right)
        if own:
            join(own_ins, own_right)
            out[...] = jnp.zeros_like(out)

    @pl.loop(0, TILE // STEP)
    def _(r):
        rows = pl.ds(pl.multiple_of(r * STEP, STEP), STEP)
        if far:
            far_out[rows, :] = half_sum(rows, far_right).astype(jnp.bfloat16)
        if own:
            came, gate_ref, up_ref, proj_gate, proj_up = extra
            rank_size = proj_gate.shape[0]
            total = half_sum(rows, own_right)
            hidden_grad = (total + came[rows, :].astype(jnp.float32)).astype(jnp.bfloat16)
            hidden_grad = hidden_grad.astype(jnp.float32)
            gate = gate_ref[rows, :].astype(jnp.float32)
            up = up_ref[rows, :].astype(jnp.float32)
            sigma = jax.nn.sigmoid(gate)
            grad_up = (hidden_grad * (gate * sigma)).astype(jnp.bfloat16)
            grad_gate = (hidden_grad * up * sigma * (1.0 + gate * (1.0 - sigma))).astype(jnp.bfloat16)
            out[:rank_size, :] += jnp.dot(proj_gate[:, rows], grad_gate, preferred_element_type=jnp.float32)
            out[rank_size:, :] += jnp.dot(proj_up[:, rows], grad_up, preferred_element_type=jnp.float32)


def stage(near_offset, near, tiles, far, own, weight, weight_near, after):
    begin, count = tiles
    width = weight_near.shape[1]
    depth = width // 2
    both = 2 * LANES
    arrays, specs, outs, shapes, rights = [], [], [], [], []

    def add(array, block, index):
        arrays.append(array)
        specs.append(pl.BlockSpec(block, index))

    for k in range(2):
        add(weight, (TILE, depth), lambda i, offset, near, k=k: (offset[0] + begin + i, k))
    for k in range(2):
        add(weight_near, (TILE, depth), lambda i, offset, near, k=k: (offset[0] + begin + i, k))
    for rows, base in ((far, 0), (own, 2)):
        if rows is not None:
            rights.append(pltpu.VMEM((2 * width, both), jnp.bfloat16))
            for k in range(4):
                side = k // 2
                add(
                    rows[k % 2],
                    (width, LANES),
                    lambda i, offset, near, side=side, base=base: (
                        base * near[1] + near[0] + side * (1 - 2 * near[0]),
                        0,
                    ),
                )
    if far is not None:
        outs.append(pl.BlockSpec((TILE, both), lambda i, offset, near: (i, 0)))
        shapes.append(jax.ShapeDtypeStruct((count * TILE, both), jnp.bfloat16))
    if own is not None:
        (came, first), gate, up, proj_gate, proj_up = own[2:]
        rank_size = proj_gate.shape[0]
        add(came, (TILE, both), lambda i, offset, near: (begin - first + i, 0))
        for array in (gate, up):
            add(array, (TILE, both), lambda i, offset, near: (begin + i, 0))
        for array in (proj_gate, proj_up):
            add(array, (rank_size, TILE), lambda i, offset, near: (0, offset[0] + begin + i))
        outs.append(pl.BlockSpec((2 * rank_size, both), lambda i, offset, near: (0, 0)))
        shapes.append(jax.ShapeDtypeStruct((2 * rank_size, both), jnp.float32))
    parts = len(rights)
    return pl.pallas_call(
        functools.partial(stage_kernel, far is not None, own is not None),
        grid_spec=pltpu.PrefetchScalarGridSpec(
            num_scalar_prefetch=2,
            grid=(count,),
            in_specs=specs + [pl.BlockSpec(memory_space=pl.ANY)] * len(after),
            out_specs=outs,
            scratch_shapes=rights,
        ),
        out_shape=shapes,
        compiler_params=kernel_params(),
        cost_estimate=pl.CostEstimate(
            flops=4 * parts * both * width * count * TILE,
            bytes_accessed=4 * width * count * TILE + 4 * parts * both * count * TILE,
            transcendentals=0,
        ),
        name="stage",
    )(near_offset, near, *arrays, *after)


def sum_over(array, axis):
    parts = [swap(array, axis, bits) for bits in (1, 2, 3)]
    return (array + parts[0]) + (parts[1] + parts[2])


def scatter_over(array, axis, dim):
    at = lax.axis_index(axis)
    size = array.shape[dim] // 4
    parts = [swap(take(array, (at ^ bits) * size, size, dim), axis, bits) for bits in (1, 2, 3)]
    return (take(array, at * size, size, dim) + parts[0]) + (parts[1] + parts[2])


def packed_scores(capacity, args):
    (
        layer_input,
        gate_pre,
        up_pre,
        grad_rows,
        blocks,
        place,
        down_weight,
        proj_input,
        proj_hidden,
        proj_output,
        proj_gate,
        proj_up,
        rev_slot,
        own_lengths,
    ) = args
    ex_count, slot_len, width_local = layer_input.shape
    hidden_local = gate_pre.shape[2]
    row_total = ex_count * slot_len
    rank_size = proj_input.shape[0]
    rev_pairs = rev_slot.shape[0] // 2
    example_at = lax.axis_index("example")
    tensor_at = lax.axis_index("tensor")
    near, far = example_at % 2, example_at // 2
    half_hidden = hidden_local // 2
    chunks = capacity // (2 * LANES)
    offset = (near * (half_hidden // TILE)).astype(jnp.int32).reshape(1)
    near_at, far_at = near.astype(jnp.int32).reshape(1), far.astype(jnp.int32).reshape(1)
    near_far = jnp.concatenate([near_at, far_at])
    gathered = [lax.all_gather(blocks[k], "tensor", axis=0, tiled=True) for k in range(chunks)]

    tile_count = half_hidden // TILE
    split = tile_count - tile_count // 2
    tile_parts = [(0, split), (split, tile_count - split)]

    def near_pair(rows):
        return rows, swap(rows, "example", 1)

    def run(h, far, own, after):
        return stage(offset, near_far, tile_parts[h], far, own, down_weight, weight_near, after)

    weight_near = swap(down_weight, "example", 1)
    gate_rows = gate_pre.reshape(row_total, hidden_local)
    up_rows = up_pre.reshape(row_total, hidden_local)
    gate_near, up_near = swap(gate_rows, "example", 1), swap(up_rows, "example", 1)
    away = cut(1 - far_at, gathered[0], ())
    inputs_rows = layer_input.reshape(row_total, width_local)
    gate_values = gate_rows.astype(jnp.float32)
    up_values = up_rows.astype(jnp.float32)
    hidden = (gate_values * jax.nn.sigmoid(gate_values) * up_values).astype(jnp.bfloat16)
    early = jnp.concatenate(
        [
            contract(proj_input, inputs_rows),
            contract(proj_hidden, hidden),
            contract(proj_output, grad_rows),
        ]
    )
    def quarter(bits):
        return take(early, (tensor_at ^ bits) * slot_len, slot_len, 1)

    sums = [quarter(0)] + [swap(quarter(bits), "tensor", bits) for bits in (1, 2, 3)]
    far_pair = near_pair(ordered(swap(away, "example", 2), (early,)))
    came, right, after = [], [], ()
    for h, tiles in enumerate(tile_parts):
        results = run(h, far_pair, None, after)
        came.append((swap(results[0], "example", 2), tiles[0]))
        after = (results[0],)
    for k in range(1, chunks):
        before = near_pair(gathered[k - 1])
        if k == 1:
            away = cut(1 - far_at, gathered[1], after)
            far_next = swap(away, "example", 2)
            gate_packed = pack(chunks, 2 * LANES, half_hidden, offset, place, gate_rows, gate_near, (away,))
            after = (gate_packed[0], came[0][0])
            up_packed = pack(chunks, 2 * LANES, half_hidden, offset, place, up_rows, up_near, after)
            after = (gate_packed[0], up_packed[0])
        came_far = far_next
        if k + 1 < chunks:
            next_away = cut(1 - far_at, gathered[k + 1], after)
            far_next = swap(next_away, "example", 2)
            after += (next_away,)
        far_pair = near_pair(ordered(came_far, after))
        arrived, came = came, []
        for h, tiles in enumerate(tile_parts):
            own = (*before, arrived[h], gate_packed[k - 1], up_packed[k - 1])
            results = run(h, far_pair, (*own, proj_gate, proj_up), after)
            after = (results[0],)
            came.append((swap(results[0], "example", 2), tiles[0]))
            right.append(results[1])
            if (k, h) == (1, 0):
                sums = sum_parts(sums, after)
                after += (sums,)
                in_gate, in_down, out_down = (sums[j * rank_size : (j + 1) * rank_size] for j in range(3))
                in_gate = [in_gate] + [swap(in_gate, "tensor", bits) for bits in (1, 2, 3)]
            if (k, h) == (1, 1):
                in_gate = join_parts(tensor_at.astype(jnp.int32).reshape(1), in_gate, after)
                after += (in_gate,)
                in_gate_near = swap(in_gate, "example", 1)
    before = near_pair(gathered[-1])
    for h, tiles in enumerate(tile_parts):
        own = (*before, came[h], gate_packed[-1], up_packed[-1], proj_gate, proj_up)
        right += run(h, None, own, after)
        after = (right[-1],)
    right = jnp.concatenate([right[k] + right[k + 1] for k in range(0, 2 * chunks, 2)], axis=1)

    slots_here = jnp.concatenate(
        [
            take(rev_slot, example_at * ex_count, ex_count, 0),
            take(rev_slot, (example_at ^ 1) * ex_count, ex_count, 0),
        ]
    )
    table = pairing_table(slots_here, rev_pairs)
    positions = jnp.arange(slot_len, dtype=jnp.int32)
    mask = (positions < take(own_lengths, tensor_at, 1, 0)).astype(jnp.float32)
    sketch_down = contract_exact(in_down * mask[None, :], out_down)
    sketch_down = take(table, tensor_at, 1, 1)[:, :, None] * sketch_down[None, :, :]
    select = jnp.arange(capacity, dtype=jnp.int32)[:, None] == place
    in_gate = jnp.concatenate([in_gate, in_gate_near], axis=1)
    in_gate = contract_exact(in_gate, select.astype(jnp.float32))
    table_rows = contract(
        jnp.repeat(table, slot_len, axis=1).astype(jnp.bfloat16), select.astype(jnp.bfloat16)
    )
    left = (table_rows[:, None, :] * in_gate[None, :, :]).reshape(rev_pairs * rank_size, capacity)
    sketch_late = contract_exact(left, right).reshape(rev_pairs, rank_size, 2 * rank_size)
    return jnp.concatenate([sketch_late, sketch_down], axis=2)


def local_four(
    layer_input,
    gate_pre,
    up_pre,
    output_grad,
    down_weight,
    proj_input,
    proj_hidden,
    proj_output,
    proj_gate,
    proj_up,
    query_sketches,
    rev_lengths,
    rev_slot,
    query_slot,
):
    ex_count, slot_len, width_local = layer_input.shape
    row_total = ex_count * slot_len
    grad_rows = output_grad.reshape(row_total, width_local)
    grad_near = swap(grad_rows, "example", 1)
    others = [swap(rev_lengths, "example", bits) for bits in (1, 2, 3)]

    near = lax.axis_index("example") % 2
    both_lengths = jnp.concatenate([rev_lengths, others[0]])
    own_begin = near * jnp.sum(others[0])
    near_begin = (1 - near) * jnp.sum(rev_lengths)
    offsets = jnp.concatenate(
        [
            own_begin + jnp.cumsum(rev_lengths) - rev_lengths,
            near_begin + jnp.cumsum(others[0]) - others[0],
        ]
    )
    positions = jnp.arange(slot_len, dtype=jnp.int32)
    place = (offsets[:, None] + positions[None, :]) ^ (near * LANES)
    place = jnp.where(positions[None, :] < both_lengths[:, None], place, -1).reshape(1, 2 * row_total)
    no_offset = jnp.zeros((1,), jnp.int32)
    full = 2 * row_total
    blocks = pack(full // (2 * LANES), LANES, width_local, no_offset, place, grad_rows, grad_near)
    sums = jnp.stack([jnp.sum(rev_lengths) + jnp.sum(others[0]), jnp.sum(others[1]) + jnp.sum(others[2])])
    most = jnp.max(sums).reshape(1)
    count = lax.axis_size("group")
    for step in range(1, count):
        shifted = lax.ppermute(most, "group", [(i, (i + step) % count) for i in range(count)])
        most = jnp.maximum(most, shifted)
    levels = [level for level in LEVELS if level < full] + [full]
    branch = jnp.sum((most[0] > jnp.array(levels[:-1], jnp.int32)).astype(jnp.int32))
    sketch = lax.switch(
        branch,
        [functools.partial(packed_scores, level) for level in levels],
        (
            layer_input,
            gate_pre,
            up_pre,
            grad_rows,
            blocks,
            place,
            down_weight,
            proj_input,
            proj_hidden,
            proj_output,
            proj_gate,
            proj_up,
            rev_slot,
            rev_lengths,
        ),
    )
    rank_size = proj_input.shape[0]
    rev_pairs = rev_slot.shape[0] // 2
    revision_pairs = sum_over(scatter_over(sketch, "tensor", 1), "example")
    example_scores = contract_exact(
        revision_pairs.reshape(rev_pairs, -1), query_sketches.astype(jnp.float32)
    )
    query_pairs = query_slot.shape[0] * 4 // 2
    pair_terms = contract_exact(example_scores, pairing_table(query_slot, query_pairs))
    total = sum_over(scatter_over(pair_terms, "example", 1), "tensor")
    return total / jnp.float32(rank_size * rank_size)


def local_any(
    layer_input,
    gate_pre,
    up_pre,
    output_grad,
    down_weight,
    proj_input,
    proj_hidden,
    proj_output,
    proj_gate,
    proj_up,
    query_sketches,
    rev_lengths,
    rev_slot,
    query_slot,
):
    ex_count, slot_len, width_local = layer_input.shape
    hidden_local = gate_pre.shape[2]
    row_total = ex_count * slot_len
    rank_size = proj_input.shape[0]
    per_rank = rank_size // lax.axis_size("tensor")
    inputs_rows = layer_input.reshape(row_total, width_local)
    grad_rows = output_grad.reshape(row_total, width_local)
    gate_values = gate_pre.reshape(row_total, hidden_local).astype(jnp.float32)
    up_values = up_pre.reshape(row_total, hidden_local).astype(jnp.float32)
    grad_full = lax.all_gather(grad_rows, "tensor", axis=1, tiled=True)
    hidden_grad = contract(grad_full, lax.all_gather(down_weight, "example", axis=1, tiled=True))
    hidden_grad = lax.optimization_barrier(hidden_grad.astype(jnp.bfloat16)).astype(jnp.float32)
    sigma = jax.nn.sigmoid(gate_values)
    active = gate_values * sigma
    hidden = (active * up_values).astype(jnp.bfloat16)
    grad_up = (hidden_grad * active).astype(jnp.bfloat16)
    grad_gate = (hidden_grad * up_values * sigma * (1.0 + gate_values * (1.0 - sigma))).astype(
        jnp.bfloat16
    )
    partials = jnp.stack(
        [
            contract(inputs_rows, proj_input),
            contract(hidden, proj_hidden),
            contract(grad_gate, proj_gate),
            contract(grad_up, proj_up),
            contract(grad_rows, proj_output),
        ]
    )
    summed = lax.psum(partials, "tensor")
    begin = lax.axis_index("tensor") * per_rank
    left = lax.dynamic_slice_in_dim(summed[:2], begin, per_rank, 2)
    right = summed[2:]
    positions = jnp.arange(slot_len, dtype=jnp.int32)
    mask = (positions[None, :] < rev_lengths[:, None]).astype(jnp.float32).reshape(row_total)
    left = left * mask[None, :, None]
    left = jnp.stack([left[0], left[0], left[1]]).reshape(3, ex_count, slot_len, per_rank)
    right = right.reshape(3, ex_count, slot_len, rank_size)
    sketches = jnp.einsum("meti,metj->eimj", left, right, precision=lax.Precision.HIGHEST).reshape(
        ex_count, per_rank * 3 * rank_size
    )
    every_sketch = lax.all_gather(sketches, "example", axis=0, tiled=True)
    rev_pairs = rev_slot.shape[0] // 2
    revision_pairs = jnp.dot(
        pairing_table(rev_slot, rev_pairs), every_sketch, precision=lax.Precision.HIGHEST
    )
    example_scores = contract_exact(revision_pairs, query_sketches.astype(jnp.float32))
    query_pairs = query_slot.shape[0] * lax.axis_size("example") // 2
    pair_terms = contract_exact(example_scores, pairing_table(query_slot, query_pairs))
    owned = lax.psum_scatter(pair_terms, "example", scatter_dimension=1, tiled=True)
    total = lax.psum(owned, "tensor")
    return total / jnp.float32(rank_size * rank_size)


def solution(mesh):
    four = mesh.shape["tensor"] == 4 and mesh.shape["example"] == 4
    return jax.shard_map(
        local_four if four else local_any,
        mesh=mesh,
        in_specs=(
            P(("group", "example"), None, "tensor"),
            P(("group", "example"), None, "tensor"),
            P(("group", "example"), None, "tensor"),
            P(("group", "example"), None, "tensor"),
            P("tensor", "example"),
            P(None, "tensor"),
            P(None, "tensor"),
            P(None, "tensor"),
            P(None, "tensor"),
            P(None, "tensor"),
            P(("group", "example"), "tensor"),
            P(("group", "example")),
            P("group"),
            P(("group", "example")),
        ),
        out_specs=P("group", "example"),
        check_vma=False,
    )
```
